256 devices in a mesh: dp: 16 (over z, core), seq: 16 (over y, x).
Axes of the slice: x: 4, y: 4, z: 8, core: 2. Of those that a mesh axis runs over, the one named last changes fastest.
Arguments:
- tokens: bfloat16 [16, 16, 320, 1152], P('dp', 'seq'), may hold values from -6 to 6
- cotangent: bfloat16 [16, 16, 320, 1152], P('dp', 'seq'), may hold values from -6 to 6
- modulation: float32 [16, 6, 1152], P('dp'), may hold values from -3 to 3
- lengths: int32 [16], P('dp'), may hold values from 1 to 16, as said below
- w_spatial_qkv: bfloat16 [1152, 1728], replicated, may hold values from -1 to 1
- w_spatial_out: bfloat16 [576, 1152], replicated, may hold values from -0.25 to 0.25
- w_temporal_qkv: bfloat16 [1152, 1728], replicated, may hold values from -1 to 1
- w_temporal_out: bfloat16 [576, 1152], replicated, may hold values from -0.25 to 0.25
Outputs:
- grad_tokens: bfloat16 [16, 16, 320, 1152], P('dp', 'seq')
- grad_spatial_qkv: bfloat16 [1152, 1728], P('seq')
- grad_spatial_out: bfloat16 [576, 1152], P('seq')
- grad_temporal_qkv: bfloat16 [1152, 1728], P('seq')
- grad_temporal_out: bfloat16 [576, 1152], P('seq')
The draws below stay inside these ranges and needn't reach their ends.
Inputs may be any that keep to these rules, and one draw needn't show every extreme that they name: `lengths`: frames of each clip that hold data; later frames are padding. Some clip holds all 16 frames and some other clip only its first.
All inputs are finite; a program needn't handle non-finite values.
Results may differ from the reference program's by a relative error of at most 0.04.
Values may be sent and summed in bfloat16 or wider, within the bound.
A program may use at most 192 MiB of HBM per device.

```python
import math
import jax
import jax.numpy as jnp
from jax import lax

D = 1152
HEADS = 8
HEAD_DIM = 72
F = 16
S = 320
INNER = 576
B = 16


def draw_tokens(key, part):
    key = jax.random.fold_in(key, 22)
    return jnp.clip(jax.random.normal(key, (B, F, S, D), jnp.float32), -6.0, 6.0).astype(jnp.bfloat16)


def draw_w_spatial_qkv(key, part):
    key = jax.random.fold_in(key, 21)
    base = jnp.clip(jax.random.normal(key, (D, 3 * HEADS * HEAD_DIM), jnp.float32), -6.0, 6.0) / math.sqrt(D)
    return base.astype(jnp.bfloat16)


def draw_w_temporal_qkv(key, part):
    key = jax.random.fold_in(key, 23)
    base = jnp.clip(jax.random.normal(key, (D, 3 * HEADS * HEAD_DIM), jnp.float32), -6.0, 6.0) / math.sqrt(D)
    return base.astype(jnp.bfloat16)


def draw_lengths(key, part):
    key = jax.random.fold_in(key, 24)
    first, second, third = jax.random.split(key, 3)
    base = jax.random.randint(first, (B,), 1, F + 1)
    full_clip = jax.random.randint(second, (), 0, B)
    short_clip = (full_clip + 1 + jax.random.randint(third, (), 0, B - 1)) % B
    index = jnp.arange(B)
    return jnp.where(index == full_clip, F, jnp.where(index == short_clip, 1, base)).astype(jnp.int32)


def block_levels(key, shape, cuts, smallest, top_value):
    loudness, own = 1.0, jax.random.fold_in(key, 6)
    for position, shards_of in cuts:
        heights = jnp.exp(jax.random.uniform(jax.random.fold_in(own, position), (shards_of,), jnp.float32, smallest / len(cuts), top_value / len(cuts)))
        loudness = loudness * jnp.repeat(heights, shape[position] // shards_of).reshape([-1 if axis == position else 1 for axis in range(len(shape))])
    return loudness


def bell_draw(key, shape, scale, reach, cuts=(), kind=jnp.bfloat16):
    gain = block_levels(key, shape, cuts, -0.22, 0.18) if cuts else 1.0
    entries = jax.random.normal(key, shape, jnp.float32) * scale * gain
    return jnp.minimum(jnp.maximum(entries, -reach), reach).astype(kind)


def setup_inputs(seed: int = 0) -> dict:
    keys = jax.random.split(jax.random.key(seed), 9)
    return {
        "tokens": draw_tokens(jax.random.fold_in(keys[8], 71), 0),
        "cotangent": bell_draw(keys[1], (B, F, S, D), 1.0, 6.0, ((0, 16), (1, 16))),
        "modulation": bell_draw(keys[2], (B, 6, D), 0.5, 3.0, ((0, 16),), jnp.float32),
        "lengths": draw_lengths(jax.random.fold_in(keys[8], 71), 0),
        "w_spatial_qkv": draw_w_spatial_qkv(jax.random.fold_in(keys[8], 71), 0),
        "w_spatial_out": bell_draw(keys[5], (INNER, D), INNER ** -0.5, 0.25),
        "w_temporal_qkv": draw_w_temporal_qkv(jax.random.fold_in(keys[8], 71), 0),
        "w_temporal_out": bell_draw(keys[7], (INNER, D), INNER ** -0.5, 0.25),
    }


NORM_EPS = 1e-06
MASKED = -1e+30
SPATIAL_FORMS = ('cfqhd', 'cfkhd', 'cfhqk')
TEMPORAL_FORMS = ('cqphd', 'ckphd', 'cphqk')

def modulated_norm(source, shift, scale):
    average = lax.optimization_barrier(jnp.mean(source, axis=-1, keepdims=True))
    centred = source - average
    variance = lax.optimization_barrier(jnp.mean(centred * centred, axis=-1, keepdims=True))
    return centred * lax.rsqrt(variance + NORM_EPS) * (1.0 + scale) + shift

def norm_back(source, shift, scale, upstream):
    pullback = jax.vjp(lambda inputs: modulated_norm(inputs, shift, scale), source)[1]
    return pullback(upstream)[0]

def split_heads(packed):
    return packed.reshape(packed.shape[:-1] + (HEADS, HEAD_DIM))

def merge_heads(spread):
    return spread.reshape(spread.shape[:-2] + (HEADS * HEAD_DIM,))

def product(form_left, form_right, form_out, left_side, right_side):
    return jnp.einsum(form_left + ',' + form_right + '->' + form_out, left_side.astype(jnp.float32), right_side.astype(jnp.float32))

def thirds(packed):
    inner_width = HEADS * HEAD_DIM
    return (split_heads(packed[..., :inner_width]), split_heads(packed[..., inner_width:2 * inner_width]), split_heads(packed[..., 2 * inner_width:]))

def attention_probs(query_rows, key_rows, keep, forms):
    scores = product(forms[0], forms[1], forms[2], query_rows, key_rows) * HEAD_DIM ** (-0.5)
    scores = jnp.where(keep, scores, MASKED)
    highest = lax.optimization_barrier(jnp.max(scores, axis=-1, keepdims=True))
    exponent = jnp.exp(scores - highest)
    return exponent / lax.optimization_barrier(jnp.sum(exponent, axis=-1, keepdims=True))

def attend_forward(packed, keep, forms):
    query_rows, key_rows, value_rows = thirds(packed)
    soft_rounded = attention_probs(query_rows, key_rows, keep, forms).astype(jnp.bfloat16)
    mixed = product(forms[2], forms[1], forms[0], soft_rounded, value_rows)
    return merge_heads(mixed).astype(jnp.bfloat16)

def attend_backward(packed, keep, upstream, forms):
    query_rows, key_rows, value_rows = thirds(packed)
    soft_weights = attention_probs(query_rows, key_rows, keep, forms)
    soft_rounded = soft_weights.astype(jnp.bfloat16)
    grad_heads = split_heads(upstream)
    grad_values = product(forms[2], forms[0], forms[1], soft_rounded, grad_heads).astype(jnp.bfloat16)
    grad_raw = product(forms[0], forms[1], forms[2], grad_heads, value_rows)
    centred = grad_raw - lax.optimization_barrier(jnp.sum(grad_raw * soft_weights, axis=-1, keepdims=True))
    grad_scores = (soft_weights * centred * HEAD_DIM ** (-0.5)).astype(jnp.bfloat16)
    grad_queries = product(forms[2], forms[1], forms[0], grad_scores, key_rows).astype(jnp.bfloat16)
    grad_keys = product(forms[2], forms[0], forms[1], grad_scores, query_rows).astype(jnp.bfloat16)
    return jnp.concatenate([merge_heads(grad_queries), merge_heads(grad_keys), merge_heads(grad_values)], axis=-1)

def project(rows, weight):
    flat = rows.reshape(-1, rows.shape[-1])
    result = jnp.dot(flat, weight, preferred_element_type=jnp.float32)
    return result.reshape(rows.shape[:-1] + (weight.shape[1],))

def project_back(grads, weight):
    flat = grads.reshape(-1, grads.shape[-1])
    result = jnp.dot(flat, weight.T, preferred_element_type=jnp.float32)
    return result.reshape(grads.shape[:-1] + (weight.shape[0],))

def weight_grad(rows, grads):
    return jnp.dot(rows.reshape(-1, rows.shape[-1]).T, grads.reshape(-1, grads.shape[-1]), preferred_element_type=jnp.float32)

def clip_pass(tokens, cotangent, modulation, lengths, w_spatial_qkv, w_spatial_out, w_temporal_qkv, w_temporal_out):
    factors = modulation[:, :, None, None, :]
    frame_index = jnp.arange(F, dtype=jnp.int32)
    live = (frame_index[None, :] < lengths[:, None]).astype(jnp.float32)
    masked = cotangent.astype(jnp.float32) * live[:, :, None, None]
    keep_time = (frame_index[None, :] < lengths[:, None])[:, None, None, None, :]
    source_wide = tokens.astype(jnp.float32)
    normed = modulated_norm(source_wide, factors[:, 0], factors[:, 1]).astype(jnp.bfloat16)
    packed = project(normed, w_spatial_qkv).astype(jnp.bfloat16)
    mixed = attend_forward(packed, True, SPATIAL_FORMS)
    residual = (source_wide + factors[:, 2] * project(mixed, w_spatial_out)).astype(jnp.bfloat16)
    residual_wide = residual.astype(jnp.float32)
    normed_time = modulated_norm(residual_wide, factors[:, 3], factors[:, 4]).astype(jnp.bfloat16)
    packed_time = project(normed_time, w_temporal_qkv).astype(jnp.bfloat16)
    attended = attend_forward(packed_time, keep_time, TEMPORAL_FORMS)
    scaled_cot = (factors[:, 5] * masked).astype(jnp.bfloat16)
    grad_temporal_out = weight_grad(attended, scaled_cot)
    grad_attended = project_back(scaled_cot, w_temporal_out).astype(jnp.bfloat16)
    grad_packed_time = attend_backward(packed_time, keep_time, grad_attended, TEMPORAL_FORMS)
    grad_temporal_qkv = weight_grad(normed_time, grad_packed_time)
    grad_residual = masked + norm_back(residual_wide, factors[:, 3], factors[:, 4], project_back(grad_packed_time, w_temporal_qkv))
    scaled_residual = (factors[:, 2] * grad_residual).astype(jnp.bfloat16)
    grad_spatial_out = weight_grad(mixed, scaled_residual)
    grad_mixed = project_back(scaled_residual, w_spatial_out).astype(jnp.bfloat16)
    grad_packed = attend_backward(packed, True, grad_mixed, SPATIAL_FORMS)
    grad_spatial_qkv = weight_grad(normed, grad_packed)
    grad_tokens = grad_residual + norm_back(source_wide, factors[:, 0], factors[:, 1], project_back(grad_packed, w_spatial_qkv))
    return (grad_tokens.astype(jnp.bfloat16), (grad_spatial_qkv, grad_spatial_out, grad_temporal_qkv, grad_temporal_out))

def reference(tokens, cotangent, modulation, lengths, w_spatial_qkv, w_spatial_out, w_temporal_qkv, w_temporal_out):

    def step(totals, slices):
        token_clip, cot_clip, factor_clip, length_clip = slices
        grad_clip, grads = clip_pass(token_clip[None], cot_clip[None], factor_clip[None], length_clip[None], w_spatial_qkv, w_spatial_out, w_temporal_qkv, w_temporal_out)
        added = jax.tree.map(lambda total_part, clip_part: total_part + clip_part, totals, grads)
        return (added, grad_clip[0])
    inner_width = HEADS * HEAD_DIM
    start = (jnp.zeros((D, 3 * inner_width), jnp.float32), jnp.zeros((inner_width, D), jnp.float32), jnp.zeros((D, 3 * inner_width), jnp.float32), jnp.zeros((inner_width, D), jnp.float32))
    totals, grad_tokens = lax.scan(step, start, (tokens, cotangent, modulation, lengths))
    return (grad_tokens, totals[0].astype(jnp.bfloat16), totals[1].astype(jnp.bfloat16), totals[2].astype(jnp.bfloat16), totals[3].astype(jnp.bfloat16))
```

```python
import functools

import jax
import jax.numpy as jnp
from jax import lax
from jax.experimental import pallas as pl
from jax.experimental.pallas import tpu as pltpu
from jax.sharding import PartitionSpec as P

HEADS = 8
HEAD_DIM = 72
F = 16
SIDE = 4
NZ = 8
WIDE = 2304
HALF = 1152
PIECE = 384
VMEM_LIMIT = 60 * 1024 * 1024


def remote(src, dst, send, recv, device):
    return pltpu.make_async_remote_copy(
        src_ref=src,
        dst_ref=dst,
        send_sem=send,
        recv_sem=recv,
        device_id=device,
        device_id_type=pl.DeviceIdType.MESH,
    )


def greet(devices):
    barrier = pltpu.get_barrier_semaphore()
    for device in devices:
        pl.semaphore_signal(barrier, inc=1, device_id=device, device_id_type=pl.DeviceIdType.MESH)
    pl.semaphore_wait(barrier, len(devices))


def exchange_kernel(in_ref, out_ref, own_sem, send_sems, recv_sems):
    dp, me = lax.axis_index("dp"), lax.axis_index("seq")
    n = SIDE * SIDE
    own = pltpu.make_async_copy(in_ref.at[me], out_ref.at[me], own_sem)
    own.start()
    greet([(dp, lax.rem(me + d, n)) for d in range(1, n)])

    def out_copy(d):
        to = lax.rem(me + d, n)
        return remote(in_ref.at[to], out_ref.at[me], send_sems.at[d], recv_sems.at[d], (dp, to))

    for d in range(1, n):
        out_copy(d).start()
    for d in range(1, n):
        source = lax.rem(me + n - d, n)
        remote(
            in_ref.at[source], out_ref.at[source], send_sems.at[d], recv_sems.at[d], (dp, source)
        ).wait_recv()
    for d in range(1, n):
        out_copy(d).wait_send()
    own.wait()


def exchange(blocks, collective_id):
    n = SIDE * SIDE
    return pl.pallas_call(
        exchange_kernel,
        out_shape=jax.ShapeDtypeStruct(blocks.shape, blocks.dtype),
        in_specs=[pl.BlockSpec(memory_space=pltpu.VMEM)],
        out_specs=pl.BlockSpec(memory_space=pltpu.VMEM),
        scratch_shapes=[
            pltpu.SemaphoreType.DMA,
            pltpu.SemaphoreType.DMA((n,)),
            pltpu.SemaphoreType.DMA((n,)),
        ],
        compiler_params=pltpu.CompilerParams(
            collective_id=collective_id, has_side_effects=True, vmem_limit_bytes=VMEM_LIMIT
        ),
    )(blocks)


def plus(*refs):
    total = refs[0].astype(jnp.float32)
    for ref in refs[1:]:
        total = total + ref.astype(jnp.float32)
    return total.astype(jnp.bfloat16)


def reduce_kernel(
    grads,
    out,
    acc,
    core_in,
    near,
    far,
    near_last,
    far_last,
    final,
    z_in,
    z_sum,
    z_out,
    z_pair,
    core_send,
    core_recv,
    near_send,
    near_recv,
    far_send,
    far_recv,
    near_last_send,
    near_last_recv,
    far_last_send,
    far_last_recv,
    z_send,
    z_recv,
    zo_send,
    zo_recv,
    zp_send,
    zp_recv,
):
    dp, seq = lax.axis_index("dp"), lax.axis_index("seq")
    z, c = lax.div(dp, 2), lax.rem(dp, 2)
    y, x = lax.div(seq, SIDE), lax.rem(seq, SIDE)
    twin = (z * 2 + 1 - c, seq)
    place = (x, y)

    def lanes(part):
        return pl.ds(part * HALF, HALF)

    def block(part, j, d):
        if part == 0:
            return j * SIDE + lax.rem(x + d, SIDE)
        return lax.rem(y + d, SIDE) * SIDE + j

    def neighbour(axis, dirn):
        step = 1 if dirn == 0 else SIDE - 1
        if axis == 0:
            return (dp, y * SIDE + lax.rem(x + step, SIDE))
        return (dp, lax.rem(y + step, SIDE) * SIDE + x)

    def z_device(d):
        return (lax.rem(z + d, NZ) * 2 + c, seq)

    greet(
        [twin]
        + [neighbour(axis, dirn) for axis in range(2) for dirn in range(2)]
        + [z_device(d) for d in range(1, NZ)]
    )

    def core_copy(part, b):
        return remote(
            grads.at[1 - c, b, :, lanes(part)],
            core_in.at[b, :, lanes(part)],
            core_send.at[part, b],
            core_recv.at[part, b],
            twin,
        )

    for d in (2, 1, 3, 0):

        @pl.loop(0, SIDE)
        def _(j):
            for part in range(2):
                core_copy(part, block(part, j, d)).start()

    def near_copy(part, dirn, k, b):
        return remote(
            acc.at[b, :, lanes(part)],
            near.at[part, dirn, k],
            near_send.at[part, dirn, k],
            near_recv.at[part, dirn, k],
            neighbour(part, dirn),
        )

    def far_copy(part, dirn, j, b):
        return remote(
            acc.at[b, :, lanes(part)],
            far.at[part, dirn, j],
            far_send.at[part, dirn, j],
            far_recv.at[part, dirn, j],
            neighbour(part, dirn),
        )

    def gather(part, b, *more):
        core_copy(part, b).wait_recv()
        acc[b, :, lanes(part)] = plus(grads[c, b, :, lanes(part)], core_in[b, :, lanes(part)], *more)

    for dirn in range(2):

        @pl.loop(0, 2)
        def _(k):
            for part in range(2):
                b = block(part, 2 * dirn + k, 2)
                gather(part, b)
                near_copy(part, dirn, k, b).start()

    for dirn in range(2):

        @pl.loop(0, 2)
        def _(k):
            for part in range(2):
                j = 2 * (1 - dirn) + k
                b = block(part, j, 1 + 2 * dirn)
                gather(part, b)
                far_copy(part, dirn, j, b).start()

    for dirn in range(2):

        @pl.loop(0, 2)
        def _(k):
            for part in range(2):
                j = 2 * dirn + k
                b = block(part, j, 1 + 2 * dirn)
                near_copy(part, dirn, k, b).wait_recv()
                gather(part, b, near[part, dirn, k])
                far_copy(part, dirn, j, b).start()

    cuts = ((0, 640), (640, 512))

    def last_lanes(part, dirn):
        return pl.ds(part * HALF + cuts[dirn][0], cuts[dirn][1])

    def near_last_copy(part, dirn, b):
        width = cuts[dirn][1]
        return remote(
            acc.at[b, :, last_lanes(part, dirn)],
            near_last.at[part, dirn, :, pl.ds(0, width)],
            near_last_send.at[part, dirn],
            near_last_recv.at[part, dirn],
            neighbour(1 - part, dirn),
        )

    def far_last_copy(part, dirn, b):
        return remote(
            acc.at[b, :, lanes(part)],
            far_last.at[part, dirn],
            far_last_send.at[part, dirn],
            far_last_recv.at[part, dirn],
            neighbour(1 - part, dirn),
        )

    def last_block(part, d):
        return block(1 - part, (x, y)[part], d)

    def finish(part, d):
        b = last_block(part, d)
        j = lax.rem(place[1 - part] + d, SIDE)
        for dirn in range(2):
            far_copy(part, dirn, j, b).wait_recv()
        gather(part, b, far[part, 0, j], far[part, 1, j])
        return b

    for part in range(2):
        b = finish(part, 2)
        for dirn in range(2):
            near_last_copy(part, dirn, b).start()
    for dirn in range(2):
        for part in range(2):
            b = finish(part, 1 + 2 * dirn)
            near_last_copy(part, dirn, b).wait_recv()
            width = cuts[dirn][1]
            acc[b, :, last_lanes(part, dirn)] = plus(
                acc[b, :, last_lanes(part, dirn)], near_last[part, dirn, :, pl.ds(0, width)]
            )
            far_last_copy(part, dirn, b).start()
    for part in range(2):
        b = finish(part, 0)
        for dirn in range(2):
            far_last_copy(part, dirn, b).wait_recv()
        final[:, lanes(part)] = plus(
            acc[b, :, lanes(part)], far_last[part, 0], far_last[part, 1]
        )

    def piece(p):
        return pl.ds(pl.multiple_of(256 * p + 128 * lax.div(p, NZ - 1), 128), PIECE)

    def z_copy(d):
        return remote(
            final.at[:, piece(lax.rem(z + d, NZ))],
            z_in.at[d],
            z_send.at[d],
            z_recv.at[d],
            z_device(d),
        )

    for d in range(1, NZ):
        z_copy(d).start()
    total = final[:, piece(z)].astype(jnp.float32)
    for d in range(1, NZ):
        z_copy(d).wait_recv()
        total = total + z_in[d].astype(jnp.float32)
    z_sum[...] = total.astype(jnp.bfloat16)

    def zo_copy(d):
        return remote(z_sum, z_out.at[d], zo_send.at[d], zo_recv.at[d], z_device(d))

    def zp_copy(d):
        source = z_sum if d == 0 else z_out.at[d]
        return remote(source, z_pair.at[d], zp_send.at[d], zp_recv.at[d], twin)

    for d in range(1, NZ):
        zo_copy(d).start()
    zp_copy(0).start()
    out[c, :, piece(z)] = z_sum[...]
    for d in range(1, NZ):
        zo_copy(d).wait_recv()
        zp_copy(d).start()
        out[c, :, piece(lax.rem(z + NZ - d, NZ))] = z_out[d]
    for d in range(NZ):
        zp_copy(d).wait_recv()
        out[1 - c, :, piece(lax.rem(z + NZ - d, NZ))] = z_pair[d]

    for d in range(NZ):
        if d:
            z_copy(d).wait_send()
            zo_copy(d).wait_send()
        zp_copy(d).wait_send()
    for part in range(2):

        @pl.loop(0, SIDE * SIDE)
        def _(b):
            core_copy(part, b).wait_send()

        for dirn in range(2):

            @pl.loop(0, 2)
            def _(k):
                near_copy(part, dirn, k, 0).wait_send()

            @pl.loop(0, SIDE)
            def _(j):
                far_copy(part, dirn, j, 0).wait_send()

            near_last_copy(part, dirn, 0).wait_send()
            far_last_copy(part, dirn, 0).wait_send()


def reduce_weights(grads, collective_id):
    n = SIDE * SIDE
    rows = grads.shape[2]
    dma = pltpu.SemaphoreType.DMA
    half = jnp.bfloat16
    return pl.pallas_call(
        reduce_kernel,
        out_shape=jax.ShapeDtypeStruct((2, rows, WIDE), half),
        in_specs=[pl.BlockSpec(memory_space=pltpu.VMEM)],
        out_specs=pl.BlockSpec(memory_space=pltpu.VMEM),
        scratch_shapes=[
            pltpu.VMEM((n, rows, WIDE), half),
            pltpu.VMEM((n, rows, WIDE), half),
            pltpu.VMEM((2, 2, 2, rows, HALF), half),
            pltpu.VMEM((2, 2, SIDE, rows, HALF), half),
            pltpu.VMEM((2, 2, rows, 640), half),
            pltpu.VMEM((2, 2, rows, HALF), half),
            pltpu.VMEM((rows, WIDE), half),
            pltpu.VMEM((NZ, rows, PIECE), half),
            pltpu.VMEM((rows, PIECE), half),
            pltpu.VMEM((NZ, rows, PIECE), half),
            pltpu.VMEM((NZ, rows, PIECE), half),
            dma((2, n)),
            dma((2, n)),
            dma((2, 2, 2)),
            dma((2, 2, 2)),
            dma((2, 2, SIDE)),
            dma((2, 2, SIDE)),
            dma((2, 2)),
            dma((2, 2)),
            dma((2, 2)),
            dma((2, 2)),
            dma((NZ,)),
            dma((NZ,)),
            dma((NZ,)),
            dma((NZ,)),
            dma((NZ,)),
            dma((NZ,)),
        ],
        compiler_params=pltpu.CompilerParams(
            collective_id=collective_id, has_side_effects=True, vmem_limit_bytes=VMEM_LIMIT
        ),
    )(grads)


NORM_EPS = 1e-06
MASKED = -1e30
SPATIAL_FORMS = ("cfqhd", "cfkhd", "cfhqk")
TEMPORAL_FORMS = ("cqphd", "ckphd", "cphqk")


def modulated_norm(source, shift, scale):
    average = jnp.mean(source, axis=-1, keepdims=True)
    centred = source - average
    variance = jnp.mean(centred * centred, axis=-1, keepdims=True)
    return centred * lax.rsqrt(variance + NORM_EPS) * (1.0 + scale) + shift


def norm_back(source, shift, scale, upstream):
    pullback = jax.vjp(lambda inputs: modulated_norm(inputs, shift, scale), source)[1]
    return pullback(upstream)[0]


def split_heads(packed):
    return packed.reshape(packed.shape[:-1] + (HEADS, HEAD_DIM))


def merge_heads(spread):
    return spread.reshape(spread.shape[:-2] + (HEADS * HEAD_DIM,))


def product(form_left, form_right, form_out, left_side, right_side):
    return jnp.einsum(
        form_left + "," + form_right + "->" + form_out,
        left_side,
        right_side,
        preferred_element_type=jnp.float32,
    )


def thirds(packed):
    inner_width = HEADS * HEAD_DIM
    return (
        split_heads(packed[..., :inner_width]),
        split_heads(packed[..., inner_width : 2 * inner_width]),
        split_heads(packed[..., 2 * inner_width :]),
    )


def attention_probs(query_rows, key_rows, keep, forms):
    scores = product(forms[0], forms[1], forms[2], query_rows, key_rows) * HEAD_DIM ** (-0.5)
    scores = jnp.where(keep, scores, MASKED)
    highest = jnp.max(scores, axis=-1, keepdims=True)
    exponent = jnp.exp(scores - highest)
    return exponent / jnp.sum(exponent, axis=-1, keepdims=True)


def attend_forward(packed, keep, forms):
    query_rows, key_rows, value_rows = thirds(packed)
    soft_rounded = attention_probs(query_rows, key_rows, keep, forms).astype(jnp.bfloat16)
    mixed = product(forms[2], forms[1], forms[0], soft_rounded, value_rows)
    return merge_heads(mixed).astype(jnp.bfloat16)


def attend_backward(packed, keep, upstream, forms):
    query_rows, key_rows, value_rows = thirds(packed)
    soft_weights = attention_probs(query_rows, key_rows, keep, forms)
    soft_rounded = soft_weights.astype(jnp.bfloat16)
    grad_heads = split_heads(upstream)
    grad_values = product(forms[2], forms[0], forms[1], soft_rounded, grad_heads).astype(
        jnp.bfloat16
    )
    grad_raw = product(forms[0], forms[1], forms[2], grad_heads, value_rows)
    centred = grad_raw - jnp.sum(grad_raw * soft_weights, axis=-1, keepdims=True)
    grad_scores = (soft_weights * centred * HEAD_DIM ** (-0.5)).astype(jnp.bfloat16)
    grad_queries = product(forms[2], forms[1], forms[0], grad_scores, key_rows).astype(jnp.bfloat16)
    grad_keys = product(forms[2], forms[0], forms[1], grad_scores, query_rows).astype(jnp.bfloat16)
    return jnp.concatenate(
        [merge_heads(grad_queries), merge_heads(grad_keys), merge_heads(grad_values)], axis=-1
    )


def project(rows, weight):
    flat = rows.reshape(-1, rows.shape[-1])
    result = jnp.dot(flat, weight, preferred_element_type=jnp.float32)
    return result.reshape(rows.shape[:-1] + (weight.shape[1],))


def project_back(grads, weight):
    flat = grads.reshape(-1, grads.shape[-1])
    result = lax.dot_general(
        flat, weight, (((1,), (1,)), ((), ())), preferred_element_type=jnp.float32
    )
    return result.reshape(grads.shape[:-1] + (weight.shape[0],))


def weight_grad(rows, grads):
    return lax.dot_general(
        rows.reshape(-1, rows.shape[-1]),
        grads.reshape(-1, grads.shape[-1]),
        (((0,), (0,)), ((), ())),
        preferred_element_type=jnp.float32,
    )


def pack_grads(qkv, out):
    n = SIDE * SIDE
    rows = out.astype(jnp.bfloat16).reshape(n, 36, 2, 576)
    tall = jnp.concatenate([rows[:, :, 0], rows[:, :, 1]], axis=1)
    return jnp.concatenate([qkv.astype(jnp.bfloat16).reshape(n, 72, 1728), tall], axis=-1)


def unpack_grads(block):
    tall = block[:, 1728:]
    return block[:, :1728], jnp.concatenate([tall[:36], tall[36:]], axis=-1)


def local(
    tokens,
    cotangent,
    modulation,
    lengths,
    w_spatial_qkv,
    w_spatial_out,
    w_temporal_qkv,
    w_temporal_out,
):
    n = SIDE * SIDE
    factors = modulation[:, :, None, None, :]
    live = (jnp.arange(F, dtype=jnp.int32)[None, :] < lengths[:, None]).astype(jnp.float32)
    keep_time = (jnp.arange(F, dtype=jnp.int32)[None, :] < lengths[:, None])[:, None, None, None, :]

    cot_place = exchange(cotangent.reshape(n, 20, 1152), 0)[None]
    masked = cot_place.astype(jnp.float32) * live[:, :, None, None]

    source_wide = tokens.astype(jnp.float32)
    normed = modulated_norm(source_wide, factors[:, 0], factors[:, 1]).astype(jnp.bfloat16)
    packed = project(normed, w_spatial_qkv).astype(jnp.bfloat16)
    mixed = attend_forward(packed, True, SPATIAL_FORMS)
    residual = (source_wide + factors[:, 2] * project(mixed, w_spatial_out)).astype(jnp.bfloat16)

    residual_place = exchange(residual.reshape(n, 20, 1152), 1)[None]
    residual_wide = residual_place.astype(jnp.float32)
    normed_time = modulated_norm(residual_wide, factors[:, 3], factors[:, 4]).astype(jnp.bfloat16)
    packed_time = project(normed_time, w_temporal_qkv).astype(jnp.bfloat16)
    attended = attend_forward(packed_time, keep_time, TEMPORAL_FORMS)
    scaled_cot = (factors[:, 5] * masked).astype(jnp.bfloat16)
    temporal_out_part = weight_grad(attended, scaled_cot)
    grad_attended = project_back(scaled_cot, w_temporal_out).astype(jnp.bfloat16)
    grad_packed_time = attend_backward(packed_time, keep_time, grad_attended, TEMPORAL_FORMS)
    temporal_qkv_part = weight_grad(normed_time, grad_packed_time)
    grad_residual = masked + norm_back(
        residual_wide, factors[:, 3], factors[:, 4], project_back(grad_packed_time, w_temporal_qkv)
    )

    grad_residual = exchange(grad_residual.astype(jnp.bfloat16)[0], 2)
    grad_residual = grad_residual.reshape(1, 1, 320, 1152).astype(jnp.float32)
    scaled_residual = (factors[:, 2] * grad_residual).astype(jnp.bfloat16)
    spatial_out_part = weight_grad(mixed, scaled_residual)
    grad_mixed = project_back(scaled_residual, w_spatial_out).astype(jnp.bfloat16)
    grad_packed = attend_backward(packed, True, grad_mixed, SPATIAL_FORMS)
    spatial_qkv_part = weight_grad(normed, grad_packed)
    grad_source = grad_residual + norm_back(
        source_wide, factors[:, 0], factors[:, 1], project_back(grad_packed, w_spatial_qkv)
    )

    summed = reduce_weights(
        jnp.stack(
            [
                pack_grads(temporal_qkv_part, temporal_out_part),
                pack_grads(spatial_qkv_part, spatial_out_part),
            ]
        ),
        3,
    )
    temporal_qkv, temporal_out = unpack_grads(summed[0])
    spatial_qkv, spatial_out = unpack_grads(summed[1])
    return (grad_source.astype(jnp.bfloat16), spatial_qkv, spatial_out, temporal_qkv, temporal_out)


def solution(mesh):
    placed = (
        P("dp", "seq", None, None),
        P("dp", "seq", None, None),
        P("dp", None, None),
        P("dp"),
        P(),
        P(),
        P(),
        P(),
    )
    return jax.shard_map(
        local,
        mesh=mesh,
        in_specs=placed,
        out_specs=(
            P("dp", "seq", None, None),
            P("seq", None),
            P("seq", None),
            P("seq", None),
            P("seq", None),
        ),
        check_vma=False,
    )
```

```python
import functools

import jax
import jax.numpy as jnp
from jax import lax
from jax.experimental import pallas as pl
from jax.experimental.pallas import tpu as pltpu
from jax.sharding import PartitionSpec as P

HEADS = 8
HEAD_DIM = 72
F = 16
SIDE = 4
NZ = 8
BLOCKS = 16
WIDE = 2304
HALF = 1152
PIECE = 384
VMEM_LIMIT = 60 * 1024 * 1024


def remote(src, dst, send, recv, device):
    return pltpu.make_async_remote_copy(
        src_ref=src,
        dst_ref=dst,
        send_sem=send,
        recv_sem=recv,
        device_id=device,
        device_id_type=pl.DeviceIdType.MESH,
    )


def greet(devices):
    barrier = pltpu.get_barrier_semaphore()
    for device in devices:
        pl.semaphore_signal(barrier, inc=1, device_id=device, device_id_type=pl.DeviceIdType.MESH)
    pl.semaphore_wait(barrier, len(devices))


def exchange_kernel(in_ref, out_ref, own_sem, send_sems, recv_sems):
    dp, me = lax.axis_index("dp"), lax.axis_index("seq")
    n = SIDE * SIDE
    own = pltpu.make_async_copy(in_ref.at[me], out_ref.at[me], own_sem)
    own.start()
    greet([(dp, lax.rem(me + d, n)) for d in range(1, n)])

    def out_copy(d):
        to = lax.rem(me + d, n)
        return remote(in_ref.at[to], out_ref.at[me], send_sems.at[d], recv_sems.at[d], (dp, to))

    for d in range(1, n):
        out_copy(d).start()
    for d in range(1, n):
        source = lax.rem(me + n - d, n)
        remote(
            in_ref.at[source], out_ref.at[source], send_sems.at[d], recv_sems.at[d], (dp, source)
        ).wait_recv()
    for d in range(1, n):
        out_copy(d).wait_send()
    own.wait()


def exchange(blocks, collective_id):
    n = SIDE * SIDE
    return pl.pallas_call(
        exchange_kernel,
        out_shape=jax.ShapeDtypeStruct(blocks.shape, blocks.dtype),
        in_specs=[pl.BlockSpec(memory_space=pltpu.VMEM)],
        out_specs=pl.BlockSpec(memory_space=pltpu.VMEM),
        scratch_shapes=[
            pltpu.SemaphoreType.DMA,
            pltpu.SemaphoreType.DMA((n,)),
            pltpu.SemaphoreType.DMA((n,)),
        ],
        compiler_params=pltpu.CompilerParams(
            collective_id=collective_id, has_side_effects=True, vmem_limit_bytes=VMEM_LIMIT
        ),
    )(blocks)


def plus(*refs):
    total = refs[0].astype(jnp.float32)
    for ref in refs[1:]:
        total = total + ref.astype(jnp.float32)
    return total.astype(jnp.bfloat16)


CUTS = ((0, 640), (640, 512))
LAST_CUTS = (((0, 384), (384, 256)), ((0, 256), (256, 256)))
DMA_COUNTS = (
    (BLOCKS, 2),
    (2, 2, 2),
    (2, 2, SIDE),
    (2, 2),
    (2, 2),
)


class Place:
    def __init__(self):
        dp, seq = lax.axis_index("dp"), lax.axis_index("seq")
        self.dp, self.seq = dp, seq
        self.z, self.c = lax.div(dp, 2), lax.rem(dp, 2)
        self.y, self.x = lax.div(seq, SIDE), lax.rem(seq, SIDE)
        self.twin = (self.z * 2 + 1 - self.c, seq)

    def neighbour(self, axis, dirn):
        step = 1 if dirn == 0 else SIDE - 1
        if axis == 0:
            return (self.dp, self.y * SIDE + lax.rem(self.x + step, SIDE))
        return (self.dp, lax.rem(self.y + step, SIDE) * SIDE + self.x)

    def along_z(self, d):
        return (lax.rem(self.z + d, NZ) * 2 + self.c, self.seq)

    def friends(self):
        return (
            [self.twin]
            + [self.neighbour(axis, dirn) for axis in range(2) for dirn in range(2)]
            + [self.along_z(d) for d in range(1, NZ)]
        )


class Reduction:
    def __init__(self, place, grads, buffers, sems):
        self.place, self.grads = place, grads
        self.acc, self.core_in, self.near, self.far, self.near_last, self.far_last = buffers
        (
            self.core_send,
            self.core_recv,
            self.near_send,
            self.near_recv,
            self.far_send,
            self.far_recv,
            self.near_last_send,
            self.near_last_recv,
            self.far_last_send,
            self.far_last_recv,
        ) = sems

    def lanes(self, part):
        return pl.ds(CUTS[part][0], CUTS[part][1])

    def lanes_of(self, part, core):
        return pl.ds(pl.multiple_of(core * HALF + CUTS[part][0], 128), CUTS[part][1])

    def block(self, part, j, d):
        at = self.place
        if part == 0:
            return j * SIDE + lax.rem(at.x + d, SIDE)
        return lax.rem(at.y + d, SIDE) * SIDE + j

    def core_copy(self, part, b):
        at = self.place
        return remote(
            self.grads.at[b, :, self.lanes_of(part, 1 - at.c)],
            self.core_in.at[b, :, self.lanes(part)],
            self.core_send.at[b, part],
            self.core_recv.at[b, part],
            at.twin,
        )

    def near_copy(self, part, dirn, k, b):
        return remote(
            self.acc.at[b, :, self.lanes(part)],
            self.near.at[part, dirn, k, :, pl.ds(0, CUTS[part][1])],
            self.near_send.at[part, dirn, k],
            self.near_recv.at[part, dirn, k],
            self.place.neighbour(part, dirn),
        )

    def far_copy(self, part, dirn, j, b):
        return remote(
            self.acc.at[b, :, self.lanes(part)],
            self.far.at[part, dirn, j, :, pl.ds(0, CUTS[part][1])],
            self.far_send.at[part, dirn, j],
            self.far_recv.at[part, dirn, j],
            self.place.neighbour(part, dirn),
        )

    def last_lanes(self, part, dirn):
        start, width = LAST_CUTS[part][dirn]
        return pl.ds(CUTS[part][0] + start, width)

    def near_last_copy(self, part, dirn, b):
        width = LAST_CUTS[part][dirn][1]
        return remote(
            self.acc.at[b, :, self.last_lanes(part, dirn)],
            self.near_last.at[part, dirn, :, pl.ds(0, width)],
            self.near_last_send.at[part, dirn],
            self.near_last_recv.at[part, dirn],
            self.place.neighbour(1 - part, dirn),
        )

    def far_last_copy(self, part, dirn, b):
        return remote(
            self.acc.at[b, :, self.lanes(part)],
            self.far_last.at[part, dirn, :, pl.ds(0, CUTS[part][1])],
            self.far_last_send.at[part, dirn],
            self.far_last_recv.at[part, dirn],
            self.place.neighbour(1 - part, dirn),
        )

    def gather(self, part, b, *more):
        self.core_copy(part, b).wait_recv()
        lanes = self.lanes(part)
        mine = self.grads[b, :, self.lanes_of(part, self.place.c)]
        self.acc[b, :, lanes] = plus(mine, self.core_in[b, :, lanes], *more)

    def start(self):
        for d in (2, 1, 3, 0):

            @pl.loop(0, SIDE)
            def _(j):
                for part in range(2):
                    self.core_copy(part, self.block(part, j, d)).start()

    def first(self):
        for dirn in range(2):

            @pl.loop(0, 2)
            def _(k):
                for part in range(2):
                    b = self.block(part, 2 * dirn + k, 2)
                    self.gather(part, b)
                    self.near_copy(part, dirn, k, b).start()

    def second(self):
        for dirn in range(2):

            @pl.loop(0, 2)
            def _(k):
                for part in range(2):
                    j = 2 * (1 - dirn) + k
                    b = self.block(part, j, 1 + 2 * dirn)
                    self.gather(part, b)
                    self.far_copy(part, dirn, j, b).start()

    def third(self):
        for dirn in range(2):

            @pl.loop(0, 2)
            def _(k):
                for part in range(2):
                    j = 2 * dirn + k
                    b = self.block(part, j, 1 + 2 * dirn)
                    self.near_copy(part, dirn, k, b).wait_recv()
                    self.gather(part, b, self.near[part, dirn, k, :, pl.ds(0, CUTS[part][1])])
                    self.far_copy(part, dirn, j, b).start()

    def finish(self, part, d):
        at = self.place
        b = self.block(1 - part, (at.x, at.y)[part], d)
        j = lax.rem((at.y, at.x)[part] + d, SIDE)
        for dirn in range(2):
            self.far_copy(part, dirn, j, b).wait_recv()
        width = pl.ds(0, CUTS[part][1])
        self.gather(part, b, self.far[part, 0, j, :, width], self.far[part, 1, j, :, width])
        return b

    def fourth(self):
        for part in range(2):
            b = self.finish(part, 2)
            for dirn in range(2):
                self.near_last_copy(part, dirn, b).start()

    def fifth(self):
        for dirn in range(2):
            for part in range(2):
                b = self.finish(part, 1 + 2 * dirn)
                self.near_last_copy(part, dirn, b).wait_recv()
                lanes = self.last_lanes(part, dirn)
                width = LAST_CUTS[part][dirn][1]
                self.acc[b, :, lanes] = plus(
                    self.acc[b, :, lanes], self.near_last[part, dirn, :, pl.ds(0, width)]
                )
                self.far_last_copy(part, dirn, b).start()

    def sixth(self, final, offset):
        for part in range(2):
            b = self.finish(part, 0)
            for dirn in range(2):
                self.far_last_copy(part, dirn, b).wait_recv()
            start, width = CUTS[part]
            final[:, offset + start : offset + start + width] = plus(
                self.acc[b, :, self.lanes(part)],
                self.far_last[part, 0, :, pl.ds(0, width)],
                self.far_last[part, 1, :, pl.ds(0, width)],
            )

    def settle(self):
        for part in range(2):

            @pl.loop(0, BLOCKS)
            def _(b):
                self.core_copy(part, b).wait_send()

            for dirn in range(2):

                @pl.loop(0, 2)
                def _(k):
                    self.near_copy(part, dirn, k, 0).wait_send()

                @pl.loop(0, SIDE)
                def _(j):
                    self.far_copy(part, dirn, j, 0).wait_send()

                self.near_last_copy(part, dirn, 0).wait_send()
                self.far_last_copy(part, dirn, 0).wait_send()


def reduction_buffers():
    half = jnp.bfloat16
    return [
        pltpu.VMEM((BLOCKS, 72, HALF), half),
        pltpu.VMEM((BLOCKS, 72, HALF), half),
        pltpu.VMEM((2, 2, 2, 72, 640), half),
        pltpu.VMEM((2, 2, SIDE, 72, 640), half),
        pltpu.VMEM((2, 2, 72, 640), half),
        pltpu.VMEM((2, 2, 72, 640), half),
    ]


def reduction_sems():
    return [pltpu.SemaphoreType.DMA(counts) for counts in DMA_COUNTS for _ in range(2)]


def over_z(at, final, out, z_in, z_sum, z_out, z_pair, sems):
    z_send, z_recv, zo_send, zo_recv, zp_send, zp_recv = sems
    z, c = at.z, at.c

    def piece(p):
        return pl.ds(pl.multiple_of(256 * p + 128 * lax.div(p, NZ - 1), 128), PIECE)

    def z_copy(d):
        return remote(
            final.at[:, piece(lax.rem(z + d, NZ))],
            z_in.at[d],
            z_send.at[d],
            z_recv.at[d],
            at.along_z(d),
        )

    def zo_copy(d):
        return remote(z_sum, z_out.at[d], zo_send.at[d], zo_recv.at[d], at.along_z(d))

    def zp_copy(d):
        source = z_sum if d == 0 else z_out.at[d]
        return remote(source, z_pair.at[d], zp_send.at[d], zp_recv.at[d], at.twin)

    for d in range(1, NZ):
        z_copy(d).start()
    total = final[:, piece(z)].astype(jnp.float32)
    for d in range(1, NZ):
        z_copy(d).wait_recv()
        total = total + z_in[d].astype(jnp.float32)
    z_sum[...] = total.astype(jnp.bfloat16)
    for d in range(1, NZ):
        zo_copy(d).start()
    zp_copy(0).start()
    out[c, :, piece(z)] = z_sum[...]
    for d in range(1, NZ):
        zo_copy(d).wait_recv()
        zp_copy(d).start()
        out[c, :, piece(lax.rem(z + NZ - d, NZ))] = z_out[d]
    for d in range(NZ):
        zp_copy(d).wait_recv()
        out[1 - c, :, piece(lax.rem(z + NZ - d, NZ))] = z_pair[d]
    for d in range(NZ):
        if d:
            z_copy(d).wait_send()
            zo_copy(d).wait_send()
        zp_copy(d).wait_send()


def z_scratch():
    half = jnp.bfloat16
    return [
        pltpu.VMEM((72, WIDE), half),
        pltpu.VMEM((NZ, 72, PIECE), half),
        pltpu.VMEM((72, PIECE), half),
        pltpu.VMEM((NZ, 72, PIECE), half),
        pltpu.VMEM((NZ, 72, PIECE), half),
    ]


def z_sems():
    return [pltpu.SemaphoreType.DMA((NZ,))] * 6


def reduce_kernel(temporal, spatial, out, *scratch):
    at = Place()
    greet(at.friends())
    final, z_buffers, scratch = scratch[0], scratch[1:5], scratch[5:]
    z_sem, scratch = scratch[:6], scratch[6:]
    parts = []
    for grads in (temporal, spatial):
        parts.append(Reduction(at, grads, scratch[:6], scratch[6:16]))
        scratch = scratch[16:]
    one, two = parts
    one.start()
    two.start()
    one.first()
    one.second()
    two.first()
    one.third()
    two.second()
    one.fourth()
    two.third()
    one.fifth()
    two.fourth()
    one.sixth(final, 0)
    two.fifth()
    two.sixth(final, HALF)
    over_z(at, final, out, *z_buffers, z_sem)
    one.settle()
    two.settle()


def reduce_weights(temporal, spatial, collective_id):
    return pl.pallas_call(
        reduce_kernel,
        out_shape=jax.ShapeDtypeStruct((2, 72, WIDE), jnp.bfloat16),
        in_specs=[pl.BlockSpec(memory_space=pltpu.VMEM)] * 2,
        out_specs=pl.BlockSpec(memory_space=pltpu.VMEM),
        scratch_shapes=z_scratch()
        + z_sems()
        + reduction_buffers()
        + reduction_sems()
        + reduction_buffers()
        + reduction_sems(),
        compiler_params=pltpu.CompilerParams(
            collective_id=collective_id, has_side_effects=True, vmem_limit_bytes=VMEM_LIMIT
        ),
    )(temporal, spatial)


NORM_EPS = 1e-06
MASKED = -1e30
ROWS = 320
SPAN = 20
D = 1152
INNER = 576
QKV = 1728
STEP = 32
UNROLL = 2
SHARP = HEAD_DIM ** (-0.5)
NN = (((1,), (0,)), ((), ()))
NT = (((1,), (1,)), ((), ()))
TN = (((0,), (0,)), ((), ()))


def matmul(left, right, dims=NN):
    return lax.dot_general(left, right, dims, preferred_element_type=jnp.float32)


def columns(total, width=256):
    return [(start, min(width, total - start)) for start in range(0, total, width)]


def by_rows(body):
    @pl.loop(0, ROWS, step=STEP)
    def _(start):
        body(pl.ds(pl.multiple_of(start, STEP), STEP))


def normalise(source):
    average = jnp.mean(source, axis=-1, keepdims=True)
    centred = source - average
    variance = jnp.mean(centred * centred, axis=-1, keepdims=True)
    spread = lax.rsqrt(variance + NORM_EPS)
    return centred * spread, spread


def modulate(source_ref, mod_ref, first, out_ref):
    shift = mod_ref[first : first + 1, :]
    gain = 1.0 + mod_ref[first + 1 : first + 2, :]

    def body(rows):
        unit, _ = normalise(source_ref[rows, :].astype(jnp.float32))
        out_ref[rows, :] = (unit * gain + shift).astype(jnp.bfloat16)

    by_rows(body)


def norm_pullback(source, upstream, gain):
    unit, spread = normalise(source)
    grad = upstream * gain
    along = jnp.mean(grad * unit, axis=-1, keepdims=True)
    return spread * (grad - jnp.mean(grad, axis=-1, keepdims=True) - unit * along)


def project_rows(rows_ref, weight_ref, out_ref):
    for start, width in columns(weight_ref.shape[0]):
        cols = slice(start, start + width)
        out_ref[:, cols] = matmul(rows_ref[...], weight_ref[cols, :], NT).astype(out_ref.dtype)


def spread_heads(wide_ref, heads_ref, count):
    for i in range(count):
        heads_ref[i] = wide_ref[:, i * HEAD_DIM : (i + 1) * HEAD_DIM]


def join_heads(heads_ref, wide_ref, count):
    for i in range(count):
        wide_ref[:, i * HEAD_DIM : (i + 1) * HEAD_DIM] = heads_ref[i]


def from_blocks(blocks_ref, flat_ref):
    for i in range(BLOCKS):
        flat_ref[i * SPAN : (i + 1) * SPAN, :] = blocks_ref[i].astype(jnp.float32)


def to_block(flat_ref, i):
    return flat_ref[i * SPAN : (i + 1) * SPAN, :].astype(jnp.bfloat16)


def attend_spatial(heads, mixed_heads):
    def body(h, _):
        scores = matmul(heads[h], heads[HEADS + h], NT) * SHARP
        exponent = jnp.exp(scores - jnp.max(scores, axis=-1, keepdims=True))
        soft = exponent / jnp.sum(exponent, axis=-1, keepdims=True)
        mixed_heads[h] = matmul(soft.astype(jnp.bfloat16), heads[2 * HEADS + h]).astype(jnp.bfloat16)
        return 0

    lax.fori_loop(0, HEADS, body, 0, unroll=UNROLL)


def attend_back(heads, grad_heads, out_heads, keep=None, attended=None):
    def body(h, _):
        queries, keys, values = heads[h], heads[HEADS + h], heads[2 * HEADS + h]
        scores = matmul(keys, queries, NT) * SHARP
        if keep is not None:
            scores = jnp.where(keep[...] > 0.0, scores, MASKED)
        exponent = jnp.exp(scores - jnp.max(scores, axis=0, keepdims=True))
        soft = exponent / jnp.sum(exponent, axis=0, keepdims=True)
        soft_rounded = soft.astype(jnp.bfloat16)
        if attended is not None:
            rows = pl.ds(pl.multiple_of(h * HEAD_DIM, 8), HEAD_DIM)
            attended[rows, :] = matmul(values, soft_rounded, TN)
        upstream = grad_heads[h]
        raw = matmul(values, upstream, NT)
        centred = raw - jnp.sum(raw * soft, axis=0, keepdims=True)
        grad_scores = (soft * centred * SHARP).astype(jnp.bfloat16)
        out_heads[2 * HEADS + h] = matmul(soft_rounded, upstream).astype(jnp.bfloat16)
        out_heads[HEADS + h] = matmul(grad_scores, queries).astype(jnp.bfloat16)
        out_heads[h] = matmul(grad_scores, keys, TN).astype(jnp.bfloat16)
        return 0

    lax.fori_loop(0, HEADS, body, 0, unroll=UNROLL)


def weight_blocks(tall, packed_grads, inner_tall, cot, low, high, grads):
    for start, width in columns(QKV):
        cols = slice(start, start + width)
        product = matmul(tall[...], packed_grads[:, cols])
        grads[:, :, cols] = product.reshape(BLOCKS, 72, width).astype(jnp.bfloat16)
    low[...] = jnp.zeros_like(low)
    high[...] = jnp.zeros_like(high)
    for s in range(BLOCKS):
        rows = inner_tall[s * 36 : (s + 1) * 36, :]
        low[s * 72 : s * 72 + 36, :] = rows
        high[s * 72 + 36 : (s + 1) * 72, :] = rows
    low_rows, high_rows = low[...].astype(jnp.bfloat16), high[...].astype(jnp.bfloat16)
    for start, width in ((0, 192), (192, 192), (384, 192)):
        product = matmul(low_rows, cot[:, start : start + width]) + matmul(
            high_rows, cot[:, INNER + start : INNER + start + width]
        )
        grads[:, :, QKV + start : QKV + start + width] = product.reshape(BLOCKS, 72, width).astype(
            jnp.bfloat16
        )


def transposed(rows_ref, tall_ref):
    for start, width in columns(rows_ref.shape[1], 128):
        cols = slice(start, start + width)
        tall_ref[cols, :] = rows_ref[:, cols].T


def front_kernel(tokens, mod, w_qkv, w_out, packed, mixed, blocks, normed, heads, mixed_heads, flat):
    modulate(tokens, mod, 0, normed)
    project_rows(normed, w_qkv, packed)
    spread_heads(packed, heads, 3 * HEADS)
    attend_spatial(heads, mixed_heads)
    join_heads(mixed_heads, mixed, HEADS)
    gate = mod[2:3, :]
    for start, width in columns(D):
        cols = slice(start, start + width)
        product = matmul(mixed[...], w_out[:, cols])
        flat[:, cols] = tokens[:, cols].astype(jnp.float32) + gate[:, cols] * product
    for i in range(BLOCKS):
        blocks[i] = to_block(flat, i)


def middle_kernel(
    resid_blocks,
    cot_blocks,
    lengths,
    mod,
    w_qkv,
    w_out,
    grad_blocks,
    grads,
    flat,
    cot_flat,
    normed,
    packed,
    heads,
    scaled,
    grad_attended,
    grad_heads,
    out_heads,
    keep,
    attended,
    packed_grads,
    tall,
    low,
    high,
    upstream,
):
    limit = lengths[0].astype(jnp.float32)

    def frame_of(index):
        return jnp.floor((index + 0.5) * (1.0 / SPAN))

    keys = lax.broadcasted_iota(jnp.int32, (ROWS, 1), 0).astype(jnp.float32)
    queries = lax.broadcasted_iota(jnp.int32, (1, ROWS), 1).astype(jnp.float32)
    key_frame, query_frame = frame_of(keys), frame_of(queries)
    same = (keys - SPAN * key_frame) == (queries - SPAN * query_frame)
    keep[...] = jnp.where(same & (key_frame < limit), 1.0, 0.0)

    from_blocks(cot_blocks, cot_flat)
    gate = mod[5:6, :]

    def scale_cot(rows):
        start = rows.start
        index = lax.broadcasted_iota(jnp.int32, (STEP, 1), 0) + start
        live = jnp.where(frame_of(index.astype(jnp.float32)) < limit, 1.0, 0.0)
        masked = cot_flat[rows, :] * live
        cot_flat[rows, :] = masked
        scaled[rows, :] = (gate * masked).astype(jnp.bfloat16)

    by_rows(scale_cot)
    grad_attended[...] = matmul(scaled[...], w_out[...], NT).astype(jnp.bfloat16)
    spread_heads(grad_attended, grad_heads, HEADS)

    from_blocks(resid_blocks, flat)
    modulate(flat, mod, 3, normed)
    project_rows(normed, w_qkv, packed)
    spread_heads(packed, heads, 3 * HEADS)
    attend_back(heads, grad_heads, out_heads, keep, attended)
    join_heads(out_heads, packed_grads, 3 * HEADS)
    pull_back(packed_grads, w_qkv, flat, mod, 3, cot_flat, upstream)
    for i in range(BLOCKS):
        grad_blocks[i] = to_block(cot_flat, i)
    transposed(normed, tall)
    weight_blocks(tall, packed_grads, attended, scaled, low, high, grads)


def pull_back(packed_grads, w_qkv, source, mod, first, into, upstream):
    gain = 1.0 + mod[first + 1 : first + 2, :]
    for start, width in columns(D):
        cols = slice(start, start + width)
        upstream[:, cols] = matmul(packed_grads[...], w_qkv[:, cols])

    def body(rows):
        into[rows, :] = into[rows, :] + norm_pullback(
            source[rows, :].astype(jnp.float32), upstream[rows, :], gain
        )

    by_rows(body)


def back_kernel(
    tokens,
    grad_blocks,
    packed,
    mixed,
    mod,
    w_qkv,
    w_out,
    grad_tokens,
    grads,
    flat,
    normed,
    heads,
    scaled,
    grad_mixed,
    grad_heads,
    out_heads,
    mixed_tall,
    packed_grads,
    tall,
    low,
    high,
    upstream,
):
    from_blocks(grad_blocks, flat)
    gate = mod[2:3, :]

    def scale(rows):
        scaled[rows, :] = (gate * flat[rows, :]).astype(jnp.bfloat16)

    by_rows(scale)
    grad_mixed[...] = matmul(scaled[...], w_out[...], NT).astype(jnp.bfloat16)
    spread_heads(grad_mixed, grad_heads, HEADS)
    spread_heads(packed, heads, 3 * HEADS)
    attend_back(heads, grad_heads, out_heads)
    join_heads(out_heads, packed_grads, 3 * HEADS)
    modulate(tokens, mod, 0, normed)
    transposed(normed, tall)
    mixed_tall[...] = mixed[...].astype(jnp.float32).T
    weight_blocks(tall, packed_grads, mixed_tall, scaled, low, high, grads)
    pull_back(packed_grads, w_qkv, tokens, mod, 0, flat, upstream)

    def last(rows):
        grad_tokens[rows, :] = flat[rows, :].astype(jnp.bfloat16)

    by_rows(last)


HALF16 = jnp.bfloat16


def vmem(shape, dtype=HALF16):
    return pltpu.VMEM(shape, dtype)


def whole(count):
    return [pl.BlockSpec(memory_space=pltpu.VMEM)] * count


def front(tokens, mod, w_qkv, w_out):
    return pl.pallas_call(
        front_kernel,
        out_shape=(
            jax.ShapeDtypeStruct((ROWS, QKV), HALF16),
            jax.ShapeDtypeStruct((ROWS, INNER), HALF16),
            jax.ShapeDtypeStruct((BLOCKS, SPAN, D), HALF16),
        ),
        in_specs=whole(4),
        out_specs=tuple(whole(3)),
        scratch_shapes=[
            vmem((ROWS, D)),
            vmem((3 * HEADS, ROWS, HEAD_DIM)),
            vmem((HEADS, ROWS, HEAD_DIM)),
            vmem((ROWS, D), jnp.float32),
        ],
        compiler_params=pltpu.CompilerParams(vmem_limit_bytes=VMEM_LIMIT),
    )(tokens, mod, w_qkv, w_out)


def middle(resid_blocks, cot_blocks, lengths, mod, w_qkv, w_out):
    wide = jnp.float32
    return pl.pallas_call(
        middle_kernel,
        out_shape=(
            jax.ShapeDtypeStruct((BLOCKS, SPAN, D), HALF16),
            jax.ShapeDtypeStruct((BLOCKS, 72, WIDE), HALF16),
        ),
        in_specs=whole(2) + [pl.BlockSpec(memory_space=pltpu.SMEM)] + whole(3),
        out_specs=tuple(whole(2)),
        scratch_shapes=[
            vmem((ROWS, D), wide),
            vmem((ROWS, D), wide),
            vmem((ROWS, D)),
            vmem((ROWS, QKV)),
            vmem((3 * HEADS, ROWS, HEAD_DIM)),
            vmem((ROWS, D)),
            vmem((ROWS, INNER)),
            vmem((HEADS, ROWS, HEAD_DIM)),
            vmem((3 * HEADS, ROWS, HEAD_DIM)),
            vmem((ROWS, ROWS), wide),
            vmem((INNER, ROWS), wide),
            vmem((ROWS, QKV)),
            vmem((D, ROWS)),
            vmem((D, ROWS), wide),
            vmem((D, ROWS), wide),
            vmem((ROWS, D), wide),
        ],
        compiler_params=pltpu.CompilerParams(vmem_limit_bytes=VMEM_LIMIT),
    )(resid_blocks, cot_blocks, lengths, mod, w_qkv, w_out)


def back(tokens, grad_blocks, packed, mixed, mod, w_qkv, w_out):
    wide = jnp.float32
    return pl.pallas_call(
        back_kernel,
        out_shape=(
            jax.ShapeDtypeStruct((ROWS, D), HALF16),
            jax.ShapeDtypeStruct((BLOCKS, 72, WIDE), HALF16),
        ),
        in_specs=whole(7),
        out_specs=tuple(whole(2)),
        scratch_shapes=[
            vmem((ROWS, D), wide),
            vmem((ROWS, D)),
            vmem((3 * HEADS, ROWS, HEAD_DIM)),
            vmem((ROWS, D)),
            vmem((ROWS, INNER)),
            vmem((HEADS, ROWS, HEAD_DIM)),
            vmem((3 * HEADS, ROWS, HEAD_DIM)),
            vmem((INNER, ROWS), wide),
            vmem((ROWS, QKV)),
            vmem((D, ROWS)),
            vmem((D, ROWS), wide),
            vmem((D, ROWS), wide),
            vmem((ROWS, D), wide),
        ],
        compiler_params=pltpu.CompilerParams(vmem_limit_bytes=VMEM_LIMIT),
    )(tokens, grad_blocks, packed, mixed, mod, w_qkv, w_out)


def unpack_grads(summed, item):
    left, right = (half[:, item * HALF : (item + 1) * HALF] for half in (summed[0], summed[1]))
    tall = right[:, QKV - HALF :]
    return (
        jnp.concatenate([left, right[:, : QKV - HALF]], axis=-1),
        jnp.concatenate([tall[:36], tall[36:]], axis=-1),
    )


def local(
    tokens,
    cotangent,
    modulation,
    lengths,
    w_spatial_qkv,
    w_spatial_out,
    w_temporal_qkv,
    w_temporal_out,
):
    mod = modulation[0]
    source = tokens.reshape(ROWS, D)
    w_spatial_qkv, w_temporal_qkv = w_spatial_qkv.T, w_temporal_qkv.T
    cot_place = exchange(cotangent.reshape(BLOCKS, SPAN, D), 0)
    packed, mixed, residual = front(source, mod, w_spatial_qkv, w_spatial_out)
    residual_place = exchange(residual, 1)
    grad_residual, temporal = middle(
        residual_place, cot_place, lengths, mod, w_temporal_qkv, w_temporal_out
    )
    grad_home = exchange(grad_residual, 2)
    grad_tokens, spatial = back(source, grad_home, packed, mixed, mod, w_spatial_qkv, w_spatial_out)
    summed = reduce_weights(temporal, spatial, 3)
    temporal_qkv, temporal_out = unpack_grads(summed, 0)
    spatial_qkv, spatial_out = unpack_grads(summed, 1)
    return (
        grad_tokens.reshape(tokens.shape),
        spatial_qkv,
        spatial_out,
        temporal_qkv,
        temporal_out,
    )


def solution(mesh):
    placed = (
        P("dp", "seq", None, None),
        P("dp", "seq", None, None),
        P("dp", None, None),
        P("dp"),
        P(),
        P(),
        P(),
        P(),
    )
    return jax.shard_map(
        local,
        mesh=mesh,
        in_specs=placed,
        out_specs=(
            P("dp", "seq", None, None),
            P("seq", None),
            P("seq", None),
            P("seq", None),
            P("seq", None),
        ),
        check_vma=False,
    )
```

```python
import functools

import jax
import jax.numpy as jnp
from jax import lax
from jax.experimental import pallas as pl
from jax.experimental.pallas import tpu as pltpu
from jax.sharding import PartitionSpec as P

HEADS = 8
HEAD_DIM = 72
F = 16
SIDE = 4
NZ = 8
BLOCKS = 16
WIDE = 2304
HALF = 1152
PIECE = 384
VMEM_LIMIT = 60 * 1024 * 1024


def remote(src, dst, send, recv, device):
    return pltpu.make_async_remote_copy(
        src_ref=src,
        dst_ref=dst,
        send_sem=send,
        recv_sem=recv,
        device_id=device,
        device_id_type=pl.DeviceIdType.MESH,
    )


def hail(devices):
    barrier = pltpu.get_barrier_semaphore()
    for device in devices:
        pl.semaphore_signal(barrier, inc=1, device_id=device, device_id_type=pl.DeviceIdType.MESH)


def meet(devices):
    pl.semaphore_wait(pltpu.get_barrier_semaphore(), len(devices))


class Exchange:
    def __init__(self, place, source, into, own_sem, send_sems, recv_sems):
        self.place, self.source, self.into = place, source, into
        self.own_sem, self.send_sems, self.recv_sems = own_sem, send_sems, recv_sems

    def to(self, d):
        return lax.rem(self.place.seq + d, BLOCKS)

    def copy(self, d):
        at = self.place
        return remote(
            self.source.at[self.to(d)],
            self.into.at[at.seq],
            self.send_sems.at[d],
            self.recv_sems.at[d],
            (at.dp, self.to(d)),
        )

    def own(self):
        me = self.place.seq
        return pltpu.make_async_copy(self.source.at[me], self.into.at[me], self.own_sem)

    def start(self):
        self.own().start()
        for d in range(1, BLOCKS):
            self.copy(d).start()

    def arrive(self):
        at = self.place
        for d in range(1, BLOCKS):
            origin = lax.rem(at.seq + BLOCKS - d, BLOCKS)
            remote(
                self.source.at[origin],
                self.into.at[origin],
                self.send_sems.at[d],
                self.recv_sems.at[d],
                (at.dp, origin),
            ).wait_recv()
        self.own().wait()

    def settle(self):
        for d in range(1, BLOCKS):
            self.copy(d).wait_send()


def exchange_sems():
    dma = pltpu.SemaphoreType.DMA
    return [dma, dma((BLOCKS,)), dma((BLOCKS,))]


def plus(*refs):
    total = refs[0].astype(jnp.float32)
    for ref in refs[1:]:
        total = total + ref.astype(jnp.float32)
    return total.astype(jnp.bfloat16)


CUTS = ((0, 640), (640, 512))
LAST_CUTS = (((0, 384), (384, 256)), ((0, 256), (256, 256)))
DMA_COUNTS = (
    (BLOCKS, 2),
    (2, 2, 2),
    (2, 2, SIDE),
    (2, 2),
    (2, 2),
)


class Place:
    def __init__(self):
        dp, seq = lax.axis_index("dp"), lax.axis_index("seq")
        self.dp, self.seq = dp, seq
        self.z, self.c = lax.div(dp, 2), lax.rem(dp, 2)
        self.y, self.x = lax.div(seq, SIDE), lax.rem(seq, SIDE)
        self.twin = (self.z * 2 + 1 - self.c, seq)

    def neighbour(self, axis, dirn):
        step = 1 if dirn == 0 else SIDE - 1
        if axis == 0:
            return (self.dp, self.y * SIDE + lax.rem(self.x + step, SIDE))
        return (self.dp, lax.rem(self.y + step, SIDE) * SIDE + self.x)

    def along_z(self, d):
        return (lax.rem(self.z + d, NZ) * 2 + self.c, self.seq)

    def line(self):
        return [(self.dp, lax.rem(self.seq + d, BLOCKS)) for d in range(1, BLOCKS)]

    def friends(self):
        return (
            [self.twin]
            + [self.neighbour(axis, dirn) for axis in range(2) for dirn in range(2)]
            + [self.along_z(d) for d in range(1, NZ)]
        )


class Reduction:
    def __init__(self, place, grads, buffers, sems):
        self.place, self.grads = place, grads
        self.acc, self.near, self.far, self.near_last, self.far_last = buffers
        (
            self.core_send,
            self.core_recv,
            self.near_send,
            self.near_recv,
            self.far_send,
            self.far_recv,
            self.near_last_send,
            self.near_last_recv,
            self.far_last_send,
            self.far_last_recv,
        ) = sems

    def lanes(self, part):
        return pl.ds(CUTS[part][0], CUTS[part][1])

    def lanes_of(self, part, core):
        return pl.ds(pl.multiple_of(core * HALF + CUTS[part][0], 128), CUTS[part][1])

    def block(self, part, j, d):
        at = self.place
        if part == 0:
            return j * SIDE + lax.rem(at.x + d, SIDE)
        return lax.rem(at.y + d, SIDE) * SIDE + j

    def core_copy(self, part, b):
        at = self.place
        return remote(
            self.grads.at[b, :, self.lanes_of(part, 1 - at.c)],
            self.acc.at[b, :, self.lanes(part)],
            self.core_send.at[b, part],
            self.core_recv.at[b, part],
            at.twin,
        )

    def near_copy(self, part, dirn, k, b):
        return remote(
            self.acc.at[b, :, self.lanes(part)],
            self.near.at[part, dirn, k, :, pl.ds(0, CUTS[part][1])],
            self.near_send.at[part, dirn, k],
            self.near_recv.at[part, dirn, k],
            self.place.neighbour(part, dirn),
        )

    def far_copy(self, part, dirn, j, b):
        return remote(
            self.acc.at[b, :, self.lanes(part)],
            self.far.at[part, dirn, j, :, pl.ds(0, CUTS[part][1])],
            self.far_send.at[part, dirn, j],
            self.far_recv.at[part, dirn, j],
            self.place.neighbour(part, dirn),
        )

    def last_lanes(self, part, dirn):
        start, width = LAST_CUTS[part][dirn]
        return pl.ds(CUTS[part][0] + start, width)

    def near_last_copy(self, part, dirn, b):
        width = LAST_CUTS[part][dirn][1]
        return remote(
            self.acc.at[b, :, self.last_lanes(part, dirn)],
            self.near_last.at[part, dirn, :, pl.ds(0, width)],
            self.near_last_send.at[part, dirn],
            self.near_last_recv.at[part, dirn],
            self.place.neighbour(1 - part, dirn),
        )

    def far_last_copy(self, part, dirn, b):
        return remote(
            self.acc.at[b, :, self.lanes(part)],
            self.far_last.at[part, dirn, :, pl.ds(0, CUTS[part][1])],
            self.far_last_send.at[part, dirn],
            self.far_last_recv.at[part, dirn],
            self.place.neighbour(1 - part, dirn),
        )

    def gather(self, part, b, *more):
        self.core_copy(part, b).wait_recv()
        lanes = self.lanes(part)
        mine = self.grads[b, :, self.lanes_of(part, self.place.c)]
        self.acc[b, :, lanes] = plus(mine, self.acc[b, :, lanes], *more)

    def start(self):
        for d in (2, 1, 3, 0):

            @pl.loop(0, SIDE)
            def _(j):
                for part in range(2):
                    self.core_copy(part, self.block(part, j, d)).start()

    def first(self):
        for dirn in range(2):

            @pl.loop(0, 2)
            def _(k):
                for part in range(2):
                    b = self.block(part, 2 * dirn + k, 2)
                    self.gather(part, b)
                    self.near_copy(part, dirn, k, b).start()

    def second(self):
        for dirn in range(2):

            @pl.loop(0, 2)
            def _(k):
                for part in range(2):
                    j = 2 * (1 - dirn) + k
                    b = self.block(part, j, 1 + 2 * dirn)
                    self.gather(part, b)
                    self.far_copy(part, dirn, j, b).start()

    def third(self):
        for dirn in range(2):

            @pl.loop(0, 2)
            def _(k):
                for part in range(2):
                    j = 2 * dirn + k
                    b = self.block(part, j, 1 + 2 * dirn)
                    self.near_copy(part, dirn, k, b).wait_recv()
                    self.gather(part, b, self.near[part, dirn, k, :, pl.ds(0, CUTS[part][1])])
                    self.far_copy(part, dirn, j, b).start()

    def finish(self, part, d):
        at = self.place
        b = self.block(1 - part, (at.x, at.y)[part], d)
        j = lax.rem((at.y, at.x)[part] + d, SIDE)
        for dirn in range(2):
            self.far_copy(part, dirn, j, b).wait_recv()
        width = pl.ds(0, CUTS[part][1])
        self.gather(part, b, self.far[part, 0, j, :, width], self.far[part, 1, j, :, width])
        return b

    def fourth(self):
        for part in range(2):
            b = self.finish(part, 2)
            for dirn in range(2):
                self.near_last_copy(part, dirn, b).start()

    def fifth(self):
        for dirn in range(2):
            for part in range(2):
                b = self.finish(part, 1 + 2 * dirn)
                self.near_last_copy(part, dirn, b).wait_recv()
                lanes = self.last_lanes(part, dirn)
                width = LAST_CUTS[part][dirn][1]
                self.acc[b, :, lanes] = plus(
                    self.acc[b, :, lanes], self.near_last[part, dirn, :, pl.ds(0, width)]
                )
                self.far_last_copy(part, dirn, b).start()

    def sixth(self, final, offset):
        for part in range(2):
            b = self.finish(part, 0)
            for dirn in range(2):
                self.far_last_copy(part, dirn, b).wait_recv()
            start, width = CUTS[part]
            final[:, offset + start : offset + start + width] = plus(
                self.acc[b, :, self.lanes(part)],
                self.far_last[part, 0, :, pl.ds(0, width)],
                self.far_last[part, 1, :, pl.ds(0, width)],
            )

    def settle(self):
        for part in range(2):

            @pl.loop(0, BLOCKS)
            def _(b):
                self.core_copy(part, b).wait_send()

            for dirn in range(2):

                @pl.loop(0, 2)
                def _(k):
                    self.near_copy(part, dirn, k, 0).wait_send()

                @pl.loop(0, SIDE)
                def _(j):
                    self.far_copy(part, dirn, j, 0).wait_send()

                self.near_last_copy(part, dirn, 0).wait_send()
                self.far_last_copy(part, dirn, 0).wait_send()


def reduction_buffers():
    half = jnp.bfloat16
    return [
        pltpu.VMEM((BLOCKS, 72, HALF), half),
        pltpu.VMEM((2, 2, 2, 72, 640), half),
        pltpu.VMEM((2, 2, SIDE, 72, 640), half),
        pltpu.VMEM((2, 2, 72, 640), half),
        pltpu.VMEM((2, 2, 72, 640), half),
    ]


def reduction_sems():
    return [pltpu.SemaphoreType.DMA(counts) for counts in DMA_COUNTS for _ in range(2)]


def over_z(at, final, out, z_in, z_sum, z_out, z_pair, sems):
    z_send, z_recv, zo_send, zo_recv, zp_send, zp_recv = sems
    z, c = at.z, at.c

    def piece(p):
        return pl.ds(pl.multiple_of(256 * p + 128 * lax.div(p, NZ - 1), 128), PIECE)

    def z_copy(d):
        return remote(
            final.at[:, piece(lax.rem(z + d, NZ))],
            z_in.at[d],
            z_send.at[d],
            z_recv.at[d],
            at.along_z(d),
        )

    def zo_copy(d):
        return remote(z_sum, z_out.at[d], zo_send.at[d], zo_recv.at[d], at.along_z(d))

    def zp_copy(d):
        source = z_sum if d == 0 else z_out.at[d]
        return remote(source, z_pair.at[d], zp_send.at[d], zp_recv.at[d], at.twin)

    for d in range(1, NZ):
        z_copy(d).start()
    total = final[:, piece(z)].astype(jnp.float32)
    for d in range(1, NZ):
        z_copy(d).wait_recv()
        total = total + z_in[d].astype(jnp.float32)
    z_sum[...] = total.astype(jnp.bfloat16)
    for d in range(1, NZ):
        zo_copy(d).start()
    zp_copy(0).start()
    out[c, :, piece(z)] = z_sum[...]
    for d in range(1, NZ):
        zo_copy(d).wait_recv()
        zp_copy(d).start()
        out[c, :, piece(lax.rem(z + NZ - d, NZ))] = z_out[d]
    for d in range(NZ):
        zp_copy(d).wait_recv()
        out[1 - c, :, piece(lax.rem(z + NZ - d, NZ))] = z_pair[d]
    for d in range(NZ):
        if d:
            z_copy(d).wait_send()
            zo_copy(d).wait_send()
        zp_copy(d).wait_send()


def z_scratch():
    half = jnp.bfloat16
    return [
        pltpu.VMEM((72, WIDE), half),
        pltpu.VMEM((NZ, 72, PIECE), half),
        pltpu.VMEM((72, PIECE), half),
        pltpu.VMEM((NZ, 72, PIECE), half),
        pltpu.VMEM((NZ, 72, PIECE), half),
    ]


def z_sems():
    return [pltpu.SemaphoreType.DMA((NZ,))] * 6


NORM_EPS = 1e-06
MASKED = -1e30
ROWS = 320
SPAN = 20
D = 1152
INNER = 576
QKV = 1728
STEP = 32
UNROLL = 2
SHARP = HEAD_DIM ** (-0.5)
NN = (((1,), (0,)), ((), ()))
NT = (((1,), (1,)), ((), ()))
TN = (((0,), (0,)), ((), ()))


def matmul(left, right, dims=NN):
    return lax.dot_general(left, right, dims, preferred_element_type=jnp.float32)


def columns(total, width=256):
    return [(start, min(width, total - start)) for start in range(0, total, width)]


def by_rows(body):
    @pl.loop(0, ROWS, step=STEP)
    def _(start):
        body(pl.ds(pl.multiple_of(start, STEP), STEP))


def normalise(source):
    average = jnp.mean(source, axis=-1, keepdims=True)
    centred = source - average
    variance = jnp.mean(centred * centred, axis=-1, keepdims=True)
    spread = lax.rsqrt(variance + NORM_EPS)
    return centred * spread, spread


def modulate(source_ref, mod_ref, first, out_ref):
    shift = mod_ref[first : first + 1, :]
    gain = 1.0 + mod_ref[first + 1 : first + 2, :]

    def body(rows):
        unit, _ = normalise(source_ref[rows, :].astype(jnp.float32))
        out_ref[rows, :] = (unit * gain + shift).astype(jnp.bfloat16)

    by_rows(body)


def norm_pullback(source, upstream, gain):
    unit, spread = normalise(source)
    grad = upstream * gain
    along = jnp.mean(grad * unit, axis=-1, keepdims=True)
    return spread * (grad - jnp.mean(grad, axis=-1, keepdims=True) - unit * along)


def project_rows(rows_ref, weight_ref, out_ref):
    for start, width in columns(weight_ref.shape[0]):
        cols = slice(start, start + width)
        out_ref[:, cols] = matmul(rows_ref[...], weight_ref[cols, :], NT).astype(out_ref.dtype)


def spread_heads(wide_ref, heads_ref, count):
    for i in range(count):
        heads_ref[i] = wide_ref[:, i * HEAD_DIM : (i + 1) * HEAD_DIM]


def join_heads(heads_ref, wide_ref, count):
    for i in range(count):
        wide_ref[:, i * HEAD_DIM : (i + 1) * HEAD_DIM] = heads_ref[i]


def from_blocks(blocks_ref, flat_ref):
    for i in range(BLOCKS):
        flat_ref[i * SPAN : (i + 1) * SPAN, :] = blocks_ref[i].astype(jnp.float32)


def to_block(flat_ref, i):
    return flat_ref[i * SPAN : (i + 1) * SPAN, :].astype(jnp.bfloat16)


def attend_spatial(heads, mixed_heads):
    def body(h, _):
        scores = matmul(heads[h], heads[HEADS + h], NT) * SHARP
        exponent = jnp.exp(scores - jnp.max(scores, axis=-1, keepdims=True))
        soft = exponent / jnp.sum(exponent, axis=-1, keepdims=True)
        mixed_heads[h] = matmul(soft.astype(jnp.bfloat16), heads[2 * HEADS + h]).astype(jnp.bfloat16)
        return 0

    lax.fori_loop(0, HEADS, body, 0, unroll=UNROLL)


def attend_back(heads, grad_heads, out_heads, span, keep=None, attended=None):
    def body(h, _):
        queries, keys, values = heads[h], heads[HEADS + h], heads[2 * HEADS + h]
        scores = matmul(keys, queries, NT) * SHARP
        if keep is not None:
            scores = jnp.where(keep[...] > 0.0, scores, MASKED)
        exponent = jnp.exp(scores - jnp.max(scores, axis=0, keepdims=True))
        soft = exponent / jnp.sum(exponent, axis=0, keepdims=True)
        soft_rounded = soft.astype(jnp.bfloat16)
        if attended is not None:
            rows = pl.ds(pl.multiple_of(h * HEAD_DIM, 8), HEAD_DIM)
            attended[rows, :] = matmul(values, soft_rounded, TN)
        upstream = grad_heads[h]
        raw = matmul(values, upstream, NT)
        centred = raw - jnp.sum(raw * soft, axis=0, keepdims=True)
        grad_scores = (soft * centred * SHARP).astype(jnp.bfloat16)
        out_heads[2 * HEADS + h] = matmul(soft_rounded, upstream).astype(jnp.bfloat16)
        out_heads[HEADS + h] = matmul(grad_scores, queries).astype(jnp.bfloat16)
        out_heads[h] = matmul(grad_scores, keys, TN).astype(jnp.bfloat16)
        return 0

    lax.fori_loop(span[0], span[1], body, 0, unroll=UNROLL)


def weight_blocks(tall, packed_grads, inner_tall, cot, low, high, grads):
    for start, width in columns(QKV):
        cols = slice(start, start + width)
        product = matmul(tall[...], packed_grads[:, cols])
        grads[:, :, cols] = product.reshape(BLOCKS, 72, width).astype(jnp.bfloat16)
    low[...] = jnp.zeros_like(low)
    high[...] = jnp.zeros_like(high)
    for s in range(BLOCKS):
        rows = inner_tall[s * 36 : (s + 1) * 36, :]
        low[s * 72 : s * 72 + 36, :] = rows
        high[s * 72 + 36 : (s + 1) * 72, :] = rows
    low_rows, high_rows = low[...].astype(jnp.bfloat16), high[...].astype(jnp.bfloat16)
    for start, width in ((0, 192), (192, 192), (384, 192)):
        product = matmul(low_rows, cot[:, start : start + width]) + matmul(
            high_rows, cot[:, INNER + start : INNER + start + width]
        )
        grads[:, :, QKV + start : QKV + start + width] = product.reshape(BLOCKS, 72, width).astype(
            jnp.bfloat16
        )


def transposed(rows_ref, tall_ref):
    for start, width in columns(rows_ref.shape[1], 128):
        cols = slice(start, start + width)
        tall_ref[cols, :] = rows_ref[:, cols].T


def front_kernel(
    tokens,
    cotangent,
    mod,
    w_qkv,
    w_out,
    packed,
    mixed,
    resid_place,
    cot_place,
    normed,
    heads,
    mixed_heads,
    flat,
    resid_blocks,
    cot_blocks,
    *sems,
):
    at = Place()
    cot_trip = Exchange(at, cot_blocks, cot_place, *sems[:3])
    resid_trip = Exchange(at, resid_blocks, resid_place, *sems[3:])
    hail(at.line())
    flat[...] = cotangent[...].astype(jnp.float32)
    for i in range(BLOCKS):
        cot_blocks[i] = to_block(flat, i)
    meet(at.line())
    cot_trip.start()
    modulate(tokens, mod, 0, normed)
    project_rows(normed, w_qkv, packed)
    spread_heads(packed, heads, 3 * HEADS)
    attend_spatial(heads, mixed_heads)
    join_heads(mixed_heads, mixed, HEADS)
    gate = mod[2:3, :]
    for start, width in columns(D):
        cols = slice(start, start + width)
        product = matmul(mixed[...], w_out[:, cols])
        flat[:, cols] = tokens[:, cols].astype(jnp.float32) + gate[:, cols] * product
    for i in range(BLOCKS):
        resid_blocks[i] = to_block(flat, i)
    resid_trip.start()
    for trip in (cot_trip, resid_trip):
        trip.arrive()
    for trip in (cot_trip, resid_trip):
        trip.settle()


def middle_kernel(
    resid_blocks,
    cot_blocks,
    lengths,
    mod,
    w_qkv,
    w_out,
    grad_place,
    grads,
    grad_blocks,
    flat,
    cot_flat,
    normed,
    packed,
    heads,
    scaled,
    grad_attended,
    grad_heads,
    out_heads,
    keep,
    attended,
    packed_grads,
    tall,
    low,
    high,
    upstream,
    *sems,
):
    at = Place()
    grad_trip = Exchange(at, grad_blocks, grad_place, *sems)
    hail(at.line())
    limit = lengths[0].astype(jnp.float32)

    def frame_of(index):
        return jnp.floor((index + 0.5) * (1.0 / SPAN))

    keys = lax.broadcasted_iota(jnp.int32, (ROWS, 1), 0).astype(jnp.float32)
    queries = lax.broadcasted_iota(jnp.int32, (1, ROWS), 1).astype(jnp.float32)
    key_frame, query_frame = frame_of(keys), frame_of(queries)
    same = (keys - SPAN * key_frame) == (queries - SPAN * query_frame)
    keep[...] = jnp.where(same & (key_frame < limit), 1.0, 0.0)

    from_blocks(cot_blocks, cot_flat)
    gate = mod[5:6, :]

    def scale_cot(rows):
        start = rows.start
        index = lax.broadcasted_iota(jnp.int32, (STEP, 1), 0) + start
        live = jnp.where(frame_of(index.astype(jnp.float32)) < limit, 1.0, 0.0)
        masked = cot_flat[rows, :] * live
        cot_flat[rows, :] = masked
        scaled[rows, :] = (gate * masked).astype(jnp.bfloat16)

    by_rows(scale_cot)
    grad_attended[...] = matmul(scaled[...], w_out[...], NT).astype(jnp.bfloat16)
    spread_heads(grad_attended, grad_heads, HEADS)

    from_blocks(resid_blocks, flat)
    modulate(flat, mod, 3, normed)
    project_rows(normed, w_qkv, packed)
    spread_heads(packed, heads, 3 * HEADS)
    attend_back(heads, grad_heads, out_heads, (0, HEADS), keep, attended)
    join_heads(out_heads, packed_grads, 3 * HEADS)
    pull_back(packed_grads, w_qkv, flat, mod, 3, cot_flat, upstream)
    for i in range(BLOCKS):
        grad_blocks[i] = to_block(cot_flat, i)
    meet(at.line())
    grad_trip.start()
    transposed(normed, tall)
    weight_blocks(tall, packed_grads, attended, scaled, low, high, grads)
    grad_trip.arrive()
    grad_trip.settle()


def pull_back(packed_grads, w_qkv, source, mod, first, into, upstream):
    gain = 1.0 + mod[first + 1 : first + 2, :]
    for start, width in columns(D):
        cols = slice(start, start + width)
        upstream[:, cols] = matmul(packed_grads[...], w_qkv[:, cols])

    def body(rows):
        into[rows, :] = into[rows, :] + norm_pullback(
            source[rows, :].astype(jnp.float32), upstream[rows, :], gain
        )

    by_rows(body)


def back_kernel(
    tokens,
    grad_blocks,
    packed,
    mixed,
    mod,
    w_qkv,
    w_out,
    temporal,
    grad_tokens,
    out,
    grads,
    flat,
    normed,
    heads,
    scaled,
    grad_mixed,
    grad_heads,
    out_heads,
    mixed_tall,
    packed_grads,
    tall,
    low,
    high,
    upstream,
    *scratch,
):
    at = Place()
    final, z_buffers, scratch = scratch[0], scratch[1:5], scratch[5:]
    z_sem, scratch = scratch[:6], scratch[6:]
    one = Reduction(at, temporal, scratch[:5], scratch[5:15])
    two = Reduction(at, grads, scratch[15:20], scratch[20:])
    hail(at.friends())
    from_blocks(grad_blocks, flat)
    gate = mod[2:3, :]

    def scale(rows):
        scaled[rows, :] = (gate * flat[rows, :]).astype(jnp.bfloat16)

    by_rows(scale)
    meet(at.friends())
    one.start()
    grad_mixed[...] = matmul(scaled[...], w_out[...], NT).astype(jnp.bfloat16)
    spread_heads(grad_mixed, grad_heads, HEADS)
    spread_heads(packed, heads, 3 * HEADS)
    one.first()
    one.second()
    attend_back(heads, grad_heads, out_heads, (0, 4))
    one.third()
    attend_back(heads, grad_heads, out_heads, (4, HEADS))
    one.fourth()
    join_heads(out_heads, packed_grads, 3 * HEADS)
    modulate(tokens, mod, 0, normed)
    transposed(normed, tall)
    mixed_tall[...] = mixed[...].astype(jnp.float32).T
    one.fifth()
    weight_blocks(tall, packed_grads, mixed_tall, scaled, low, high, grads)
    two.start()
    one.sixth(final, 0)
    two.first()
    two.second()
    pull_back(packed_grads, w_qkv, tokens, mod, 0, flat, upstream)

    def last(rows):
        grad_tokens[rows, :] = flat[rows, :].astype(jnp.bfloat16)

    by_rows(last)
    two.third()
    two.fourth()
    two.fifth()
    two.sixth(final, HALF)
    over_z(at, final, out, *z_buffers, z_sem)
    one.settle()
    two.settle()


HALF16 = jnp.bfloat16


def vmem(shape, dtype=HALF16):
    return pltpu.VMEM(shape, dtype)


def talking(collective_id):
    return pltpu.CompilerParams(
        collective_id=collective_id, has_side_effects=True, vmem_limit_bytes=VMEM_LIMIT
    )


def whole(count):
    return [pl.BlockSpec(memory_space=pltpu.VMEM)] * count


def front(tokens, cotangent, mod, w_qkv, w_out):
    return pl.pallas_call(
        front_kernel,
        out_shape=(
            jax.ShapeDtypeStruct((ROWS, QKV), HALF16),
            jax.ShapeDtypeStruct((ROWS, INNER), HALF16),
            jax.ShapeDtypeStruct((BLOCKS, SPAN, D), HALF16),
            jax.ShapeDtypeStruct((BLOCKS, SPAN, D), HALF16),
        ),
        in_specs=whole(5),
        out_specs=tuple(whole(4)),
        scratch_shapes=[
            vmem((ROWS, D)),
            vmem((3 * HEADS, ROWS, HEAD_DIM)),
            vmem((HEADS, ROWS, HEAD_DIM)),
            vmem((ROWS, D), jnp.float32),
            vmem((BLOCKS, SPAN, D)),
            vmem((BLOCKS, SPAN, D)),
        ]
        + exchange_sems()
        + exchange_sems(),
        compiler_params=talking(0),
    )(tokens, cotangent, mod, w_qkv, w_out)


def middle(resid_blocks, cot_blocks, lengths, mod, w_qkv, w_out):
    wide = jnp.float32
    return pl.pallas_call(
        middle_kernel,
        out_shape=(
            jax.ShapeDtypeStruct((BLOCKS, SPAN, D), HALF16),
            jax.ShapeDtypeStruct((BLOCKS, 72, WIDE), HALF16),
        ),
        in_specs=whole(2) + [pl.BlockSpec(memory_space=pltpu.SMEM)] + whole(3),
        out_specs=tuple(whole(2)),
        scratch_shapes=[
            vmem((BLOCKS, SPAN, D)),
            vmem((ROWS, D), wide),
            vmem((ROWS, D), wide),
            vmem((ROWS, D)),
            vmem((ROWS, QKV)),
            vmem((3 * HEADS, ROWS, HEAD_DIM)),
            vmem((ROWS, D)),
            vmem((ROWS, INNER)),
            vmem((HEADS, ROWS, HEAD_DIM)),
            vmem((3 * HEADS, ROWS, HEAD_DIM)),
            vmem((ROWS, ROWS), wide),
            vmem((INNER, ROWS), wide),
            vmem((ROWS, QKV)),
            vmem((D, ROWS)),
            vmem((D, ROWS), wide),
            vmem((D, ROWS), wide),
            vmem((ROWS, D), wide),
        ]
        + exchange_sems(),
        compiler_params=talking(1),
    )(resid_blocks, cot_blocks, lengths, mod, w_qkv, w_out)


def back(tokens, grad_blocks, packed, mixed, mod, w_qkv, w_out, temporal):
    wide = jnp.float32
    return pl.pallas_call(
        back_kernel,
        out_shape=(
            jax.ShapeDtypeStruct((ROWS, D), HALF16),
            jax.ShapeDtypeStruct((2, 72, WIDE), HALF16),
        ),
        in_specs=whole(8),
        out_specs=tuple(whole(2)),
        scratch_shapes=[
            vmem((BLOCKS, 72, WIDE)),
            vmem((ROWS, D), wide),
            vmem((ROWS, D)),
            vmem((3 * HEADS, ROWS, HEAD_DIM)),
            vmem((ROWS, D)),
            vmem((ROWS, INNER)),
            vmem((HEADS, ROWS, HEAD_DIM)),
            vmem((3 * HEADS, ROWS, HEAD_DIM)),
            vmem((INNER, ROWS), wide),
            vmem((ROWS, QKV)),
            vmem((D, ROWS)),
            vmem((D, ROWS), wide),
            vmem((D, ROWS), wide),
            vmem((ROWS, D), wide),
        ]
        + z_scratch()
        + z_sems()
        + reduction_buffers()
        + reduction_sems()
        + reduction_buffers()
        + reduction_sems(),
        compiler_params=talking(2),
    )(tokens, grad_blocks, packed, mixed, mod, w_qkv, w_out, temporal)


def unpack_grads(summed, item):
    left, right = (half[:, item * HALF : (item + 1) * HALF] for half in (summed[0], summed[1]))
    tall = right[:, QKV - HALF :]
    return (
        jnp.concatenate([left, right[:, : QKV - HALF]], axis=-1),
        jnp.concatenate([tall[:36], tall[36:]], axis=-1),
    )


def local(
    tokens,
    cotangent,
    modulation,
    lengths,
    w_spatial_qkv,
    w_spatial_out,
    w_temporal_qkv,
    w_temporal_out,
):
    mod = modulation[0]
    source = tokens.reshape(ROWS, D)
    w_spatial_qkv, w_temporal_qkv = w_spatial_qkv.T, w_temporal_qkv.T
    packed, mixed, residual, cot_place = front(
        source, cotangent.reshape(ROWS, D), mod, w_spatial_qkv, w_spatial_out
    )
    grad_residual, temporal = middle(
        residual, cot_place, lengths, mod, w_temporal_qkv, w_temporal_out
    )
    grad_tokens, summed = back(
        source, grad_residual, packed, mixed, mod, w_spatial_qkv, w_spatial_out, temporal
    )
    temporal_qkv, temporal_out = unpack_grads(summed, 0)
    spatial_qkv, spatial_out = unpack_grads(summed, 1)
    return (
        grad_tokens.reshape(tokens.shape),
        spatial_qkv,
        spatial_out,
        temporal_qkv,
        temporal_out,
    )


def solution(mesh):
    placed = (
        P("dp", "seq", None, None),
        P("dp", "seq", None, None),
        P("dp", None, None),
        P("dp"),
        P(),
        P(),
        P(),
        P(),
    )
    return jax.shard_map(
        local,
        mesh=mesh,
        in_specs=placed,
        out_specs=(
            P("dp", "seq", None, None),
            P("seq", None),
            P("seq", None),
            P("seq", None),
            P("seq", None),
        ),
        check_vma=False,
    )
```

```python
import jax
import jax.numpy as jnp
from jax import lax
from jax.experimental import pallas as pl
from jax.experimental.pallas import tpu as pltpu
from jax.sharding import PartitionSpec as P

HEADS = 8
HEAD_DIM = 72
F = 16
SIDE = 4
NZ = 8
BLOCKS = 16
WIDE = 2304
HALF = 1152
VMEM_LIMIT = 63 * 1024 * 1024


def remote(src, dst, send, recv, device):
    return pltpu.make_async_remote_copy(
        src_ref=src,
        dst_ref=dst,
        send_sem=send,
        recv_sem=recv,
        device_id=device,
        device_id_type=pl.DeviceIdType.MESH,
    )


def hail(devices):
    barrier = pltpu.get_barrier_semaphore()
    for device in devices:
        pl.semaphore_signal(barrier, inc=1, device_id=device, device_id_type=pl.DeviceIdType.MESH)


def meet(devices):
    pl.semaphore_wait(pltpu.get_barrier_semaphore(), len(devices))


class Exchange:
    def __init__(self, place, source, into, own_sem, send_sems, recv_sems):
        self.place, self.source, self.into = place, source, into
        self.own_sem, self.send_sems, self.recv_sems = own_sem, send_sems, recv_sems

    def to(self, d):
        return lax.rem(self.place.seq + d, BLOCKS)

    def copy(self, d):
        at = self.place
        return remote(
            self.source.at[self.to(d)],
            self.into.at[at.seq],
            self.send_sems.at[d],
            self.recv_sems.at[d],
            (at.dp, self.to(d)),
        )

    def own(self):
        me = self.place.seq
        return pltpu.make_async_copy(self.source.at[me], self.into.at[me], self.own_sem)

    def start(self):
        self.own().start()
        for d in range(1, BLOCKS):
            self.copy(d).start()

    def arrive(self):
        at = self.place
        for d in range(1, BLOCKS):
            origin = lax.rem(at.seq + BLOCKS - d, BLOCKS)
            remote(
                self.source.at[origin],
                self.into.at[origin],
                self.send_sems.at[d],
                self.recv_sems.at[d],
                (at.dp, origin),
            ).wait_recv()
        self.own().wait()

    def settle(self):
        for d in range(1, BLOCKS):
            self.copy(d).wait_send()


def exchange_sems():
    dma = pltpu.SemaphoreType.DMA
    return [dma, dma((BLOCKS,)), dma((BLOCKS,))]


def plus(*refs):
    total = refs[0].astype(jnp.float32)
    for ref in refs[1:]:
        total = total + ref.astype(jnp.float32)
    return total.astype(jnp.bfloat16)


CUTS = ((0, 640), (640, 512))
LAST_CUTS = (((0, 384), (384, 256)), ((0, 256), (256, 256)))
DMA_COUNTS = (
    (BLOCKS, 2),
    (2, 2, 2),
    (2, 2, SIDE),
    (2, 2),
    (2, 2),
)


class Place:
    def __init__(self):
        dp, seq = lax.axis_index("dp"), lax.axis_index("seq")
        self.dp, self.seq = dp, seq
        self.z, self.c = lax.div(dp, 2), lax.rem(dp, 2)
        self.y, self.x = lax.div(seq, SIDE), lax.rem(seq, SIDE)
        self.twin = (self.z * 2 + 1 - self.c, seq)

    def neighbour(self, axis, dirn):
        step = 1 if dirn == 0 else SIDE - 1
        if axis == 0:
            return (self.dp, self.y * SIDE + lax.rem(self.x + step, SIDE))
        return (self.dp, lax.rem(self.y + step, SIDE) * SIDE + self.x)

    def along_z(self, d):
        return (lax.rem(self.z + d, NZ) * 2 + self.c, self.seq)

    def line(self):
        return [(self.dp, lax.rem(self.seq + d, BLOCKS)) for d in range(1, BLOCKS)]

    def friends(self):
        return [self.twin] + self.line() + [self.along_z(d) for d in range(1, NZ)]


class Reduction:
    def __init__(self, place, grads, buffers, sems):
        self.place, self.grads = place, grads
        self.acc, self.near, self.far, self.near_last, self.far_last = buffers
        (
            self.core_send,
            self.core_recv,
            self.near_send,
            self.near_recv,
            self.far_send,
            self.far_recv,
            self.near_last_send,
            self.near_last_recv,
            self.far_last_send,
            self.far_last_recv,
        ) = sems

    def lanes(self, part):
        return pl.ds(CUTS[part][0], CUTS[part][1])

    def lanes_of(self, part, core):
        return pl.ds(pl.multiple_of(core * HALF + CUTS[part][0], 128), CUTS[part][1])

    def block(self, part, j, d):
        at = self.place
        if part == 0:
            return j * SIDE + lax.rem(at.x + d, SIDE)
        return lax.rem(at.y + d, SIDE) * SIDE + j

    def core_copy(self, part, b):
        at = self.place
        return remote(
            self.grads.at[b, :, self.lanes_of(part, 1 - at.c)],
            self.acc.at[b, :, self.lanes(part)],
            self.core_send.at[b, part],
            self.core_recv.at[b, part],
            at.twin,
        )

    def near_copy(self, part, dirn, k, b):
        return remote(
            self.acc.at[b, :, self.lanes(part)],
            self.near.at[part, dirn, k, :, pl.ds(0, CUTS[part][1])],
            self.near_send.at[part, dirn, k],
            self.near_recv.at[part, dirn, k],
            self.place.neighbour(part, dirn),
        )

    def far_copy(self, part, dirn, j, b):
        return remote(
            self.acc.at[b, :, self.lanes(part)],
            self.far.at[part, dirn, j, :, pl.ds(0, CUTS[part][1])],
            self.far_send.at[part, dirn, j],
            self.far_recv.at[part, dirn, j],
            self.place.neighbour(part, dirn),
        )

    def last_lanes(self, part, dirn):
        start, width = LAST_CUTS[part][dirn]
        return pl.ds(CUTS[part][0] + start, width)

    def near_last_copy(self, part, dirn, b):
        width = LAST_CUTS[part][dirn][1]
        return remote(
            self.acc.at[b, :, self.last_lanes(part, dirn)],
            self.near_last.at[part, dirn, :, pl.ds(0, width)],
            self.near_last_send.at[part, dirn],
            self.near_last_recv.at[part, dirn],
            self.place.neighbour(1 - part, dirn),
        )

    def far_last_copy(self, part, dirn, b):
        return remote(
            self.acc.at[b, :, self.lanes(part)],
            self.far_last.at[part, dirn, :, pl.ds(0, CUTS[part][1])],
            self.far_last_send.at[part, dirn],
            self.far_last_recv.at[part, dirn],
            self.place.neighbour(1 - part, dirn),
        )

    def gather(self, part, b, *more):
        self.core_copy(part, b).wait_recv()
        lanes = self.lanes(part)
        mine = self.grads[b, :, self.lanes_of(part, self.place.c)]
        self.acc[b, :, lanes] = plus(mine, self.acc[b, :, lanes], *more)

    def start(self):
        for d in (2, 1, 3, 0):

            @pl.loop(0, SIDE)
            def _(j):
                for part in range(2):
                    self.core_copy(part, self.block(part, j, d)).start()

    def first(self):
        for dirn in range(2):

            @pl.loop(0, 2)
            def _(k):
                for part in range(2):
                    b = self.block(part, 2 * dirn + k, 2)
                    self.gather(part, b)
                    self.near_copy(part, dirn, k, b).start()

    def second(self):
        for dirn in range(2):

            @pl.loop(0, 2)
            def _(k):
                for part in range(2):
                    j = 2 * (1 - dirn) + k
                    b = self.block(part, j, 1 + 2 * dirn)
                    self.gather(part, b)
                    self.far_copy(part, dirn, j, b).start()

    def third(self):
        for dirn in range(2):

            @pl.loop(0, 2)
            def _(k):
                for part in range(2):
                    j = 2 * dirn + k
                    b = self.block(part, j, 1 + 2 * dirn)
                    self.near_copy(part, dirn, k, b).wait_recv()
                    self.gather(part, b, self.near[part, dirn, k, :, pl.ds(0, CUTS[part][1])])
                    self.far_copy(part, dirn, j, b).start()

    def finish(self, part, d):
        at = self.place
        b = self.block(1 - part, (at.x, at.y)[part], d)
        j = lax.rem((at.y, at.x)[part] + d, SIDE)
        for dirn in range(2):
            self.far_copy(part, dirn, j, b).wait_recv()
        width = pl.ds(0, CUTS[part][1])
        self.gather(part, b, self.far[part, 0, j, :, width], self.far[part, 1, j, :, width])
        return b

    def fourth(self):
        for part in range(2):
            b = self.finish(part, 2)
            for dirn in range(2):
                self.near_last_copy(part, dirn, b).start()

    def fifth(self):
        for dirn in range(2):
            for part in range(2):
                b = self.finish(part, 1 + 2 * dirn)
                self.near_last_copy(part, dirn, b).wait_recv()
                lanes = self.last_lanes(part, dirn)
                width = LAST_CUTS[part][dirn][1]
                self.acc[b, :, lanes] = plus(
                    self.acc[b, :, lanes], self.near_last[part, dirn, :, pl.ds(0, width)]
                )
                self.far_last_copy(part, dirn, b).start()

    def sixth(self, final, offset):
        for part in range(2):
            b = self.finish(part, 0)
            for dirn in range(2):
                self.far_last_copy(part, dirn, b).wait_recv()
            start, width = CUTS[part]
            final[:, offset + start : offset + start + width] = plus(
                self.acc[b, :, self.lanes(part)],
                self.far_last[part, 0, :, pl.ds(0, width)],
                self.far_last[part, 1, :, pl.ds(0, width)],
            )

    def settle(self):
        for part in range(2):

            @pl.loop(0, BLOCKS)
            def _(b):
                self.core_copy(part, b).wait_send()

            for dirn in range(2):

                @pl.loop(0, 2)
                def _(k):
                    self.near_copy(part, dirn, k, 0).wait_send()

                @pl.loop(0, SIDE)
                def _(j):
                    self.far_copy(part, dirn, j, 0).wait_send()

                self.near_last_copy(part, dirn, 0).wait_send()
                self.far_last_copy(part, dirn, 0).wait_send()


def reduction_buffers():
    half = jnp.bfloat16
    return [
        pltpu.VMEM((BLOCKS, 72, HALF), half),
        pltpu.VMEM((2, 2, 2, 72, 640), half),
        pltpu.VMEM((2, 2, SIDE, 72, 640), half),
        pltpu.VMEM((2, 2, 72, 640), half),
        pltpu.VMEM((2, 2, 72, 640), half),
    ]


def reduction_sems():
    return [pltpu.SemaphoreType.DMA(counts) for counts in DMA_COUNTS for _ in range(2)]


class Depth:
    def __init__(self, place, final, out, offset, extra, buffers, sems):
        self.place, self.final, self.out = place, final, out
        self.offset, self.extra = offset, extra
        self.arrived, self.arrived_extra = buffers
        self.send, self.recv, self.send_extra, self.recv_extra = sems[:4]
        self.out_send, self.out_recv, self.last_send, self.last_recv = sems[4:8]
        self.pair_send, self.pair_recv = sems[8:]

    def tile(self, k):
        return pl.ds(pl.multiple_of(k * 128, 128), 128)

    def spot(self, k, core):
        return self.out.at[core, :, pl.ds(pl.multiple_of(self.offset + k * 128, 128), 128)]

    def owner(self, k):
        return (k * 2 + self.place.c, self.place.seq)

    def up(self, d):
        to = lax.rem(self.place.z + d, NZ)
        return remote(
            self.final.at[:, self.tile(to)],
            self.arrived.at[d],
            self.send.at[d],
            self.recv.at[d],
            self.owner(to),
        )

    def up_extra(self, d):
        return remote(
            self.final.at[:, self.tile(NZ)],
            self.arrived_extra.at[d],
            self.send_extra,
            self.recv_extra.at[d],
            self.owner(self.extra),
        )

    def down(self, d):
        at = self.place
        spot = self.spot(at.z, at.c)
        return remote(spot, spot, self.out_send.at[d], self.out_recv.at[d], at.along_z(d))

    def down_extra(self, d):
        at = self.place
        spot = self.spot(NZ, at.c)
        return remote(spot, spot, self.last_send.at[d], self.last_recv, self.owner((self.extra + d) % NZ))

    def across(self, d):
        at = self.place
        k = NZ if d == NZ else lax.rem(at.z + NZ - d, NZ)
        spot = self.spot(k, at.c)
        return remote(spot, spot, self.pair_send.at[d], self.pair_recv.at[d], at.twin)

    def is_extra(self):
        return self.place.z == self.extra

    def rank(self):
        return lax.rem(self.place.z + NZ - self.extra, NZ)

    def start(self):
        for d in range(1, NZ):
            self.up(d).start()

        @pl.when(jnp.logical_not(self.is_extra()))
        def _():
            self.up_extra(self.rank()).start()

    def middle(self):
        at = self.place
        total = self.final[:, self.tile(at.z)].astype(jnp.float32)
        for d in range(1, NZ):
            self.up(d).wait_recv()
            total = total + self.arrived[d].astype(jnp.float32)
        self.spot(at.z, at.c)[...] = total.astype(jnp.bfloat16)
        for d in range(1, NZ):
            self.down(d).start()

        @pl.when(self.is_extra())
        def _():
            last = self.final[:, self.tile(NZ)].astype(jnp.float32)
            for d in range(1, NZ):
                self.up_extra(d).wait_recv()
                last = last + self.arrived_extra[d].astype(jnp.float32)
            self.spot(NZ, at.c)[...] = last.astype(jnp.bfloat16)
            for d in range(1, NZ):
                self.down_extra(d).start()

        self.across(0).start()

    def end(self):
        at = self.place
        for d in range(1, NZ):
            spot = self.spot(lax.rem(at.z + NZ - d, NZ), at.c)
            remote(
                spot, spot, self.out_send.at[d], self.out_recv.at[d], at.along_z(d)
            ).wait_recv()
            self.across(d).start()

        @pl.when(jnp.logical_not(self.is_extra()))
        def _():
            self.down_extra(1).wait_recv()

        self.across(NZ).start()
        for d in range(NZ + 1):
            k = NZ if d == NZ else lax.rem(at.z + NZ - d, NZ)
            spot = self.spot(k, 1 - at.c)
            remote(
                spot, spot, self.pair_send.at[d], self.pair_recv.at[d], at.twin
            ).wait_recv()

    def settle(self):
        for d in range(1, NZ):
            self.up(d).wait_send()
            self.down(d).wait_send()
        for d in range(NZ + 1):
            self.across(d).wait_send()

        @pl.when(jnp.logical_not(self.is_extra()))
        def _():
            self.up_extra(self.rank()).wait_send()

        @pl.when(self.is_extra())
        def _():
            for d in range(1, NZ):
                self.down_extra(d).wait_send()


def depth_buffers():
    return [pltpu.VMEM((NZ, 72, 128), jnp.bfloat16)] * 2


def depth_sems():
    dma = pltpu.SemaphoreType.DMA
    return [
        dma((NZ,)),
        dma((NZ,)),
        dma,
        dma((NZ,)),
        dma((NZ,)),
        dma((NZ,)),
        dma((NZ,)),
        dma,
        dma((NZ + 1,)),
        dma((NZ + 1,)),
    ]


NORM_EPS = 1e-06
MASKED = -1e30
ROWS = 320
SPAN = 8
GROUPS = 3
GROUP = SPAN * BLOCKS
SPREAD = GROUPS * GROUP
ODD = 4
D = 1152
INNER = 576
QKV = 1728
STEP = 32
UNROLL = 2
SHARP = HEAD_DIM ** (-0.5)
SHARP2 = SHARP * 1.4426950408889634
NN = (((1,), (0,)), ((), ()))
NT = (((1,), (1,)), ((), ()))
TN = (((0,), (0,)), ((), ()))
HALF16 = jnp.bfloat16


def matmul(left, right, dims=NN):
    return lax.dot_general(left, right, dims, preferred_element_type=jnp.float32)


def columns(total, width=256):
    return [(start, min(width, total - start)) for start in range(0, total, width)]


def by_rows(body, first=0, last=ROWS, step=STEP):
    @pl.loop(first, last, step=step)
    def _(start):
        body(pl.ds(pl.multiple_of(start, step), step))


def normalise(source):
    average = jnp.mean(source, axis=-1, keepdims=True)
    centred = source - average
    variance = jnp.mean(centred * centred, axis=-1, keepdims=True)
    spread = lax.rsqrt(variance + NORM_EPS)
    return centred * spread, spread


def modulated(source, mod, first):
    unit, _ = normalise(source)
    return (unit * (1.0 + mod[first + 1]) + mod[first]).astype(HALF16)


def norm_pullback(source, upstream, gain):
    unit, spread = normalise(source)
    grad = upstream * gain
    along = jnp.mean(grad * unit, axis=-1, keepdims=True)
    return spread * (grad - jnp.mean(grad, axis=-1, keepdims=True) - unit * along)


def wide(ref_value):
    return ref_value.astype(jnp.float32)


def project_rows(rows_ref, rows, weight_ref, out_ref, out_rows):
    for start, width in columns(weight_ref.shape[0]):
        cols = slice(start, start + width)
        out_ref[out_rows, cols] = matmul(rows_ref[rows, :], weight_ref[cols, :], NT).astype(HALF16)


def spread_heads(wide_ref, heads_ref, count, rows):
    for i in range(count):
        heads_ref[i, rows] = wide_ref[rows, i * HEAD_DIM : (i + 1) * HEAD_DIM]


def softmax(scores, axis):
    exponent = jnp.exp2((scores - jnp.max(scores, axis=axis, keepdims=True)) * SHARP2)
    return exponent * (1.0 / jnp.sum(exponent, axis=axis, keepdims=True))


def attend_spatial(heads, mixed_heads, rows):
    def body(h, _):
        scores = matmul(heads[h, rows], heads[HEADS + h], NT)
        soft = softmax(scores, -1).astype(HALF16)
        mixed_heads[h, rows] = matmul(soft, heads[2 * HEADS + h]).astype(HALF16)
        return 0

    lax.fori_loop(0, HEADS, body, 0, unroll=UNROLL)


def head_back(queries, keys, values, upstream, bias=None):
    scores = matmul(keys, queries, NT)
    if bias is not None:
        scores = scores + bias
    soft = softmax(scores, 0)
    soft_rounded = soft.astype(HALF16)
    raw = matmul(values, upstream, NT)
    centred = raw - jnp.sum(raw * soft, axis=0, keepdims=True)
    grad_scores = (soft * centred).astype(HALF16)
    grad_values = matmul(soft_rounded, upstream).astype(HALF16)
    grad_keys = (matmul(grad_scores, queries) * SHARP).astype(HALF16)
    grad_queries = (matmul(grad_scores, keys, TN) * SHARP).astype(HALF16)
    return grad_queries, grad_keys, grad_values, soft_rounded


def weight_blocks(depth, tall, packed_grads, inner_tall, cot, low, high, grads):
    deep = slice(0, depth)
    for start, width in columns(QKV):
        cols = slice(start, start + width)
        product = matmul(tall[:, deep], packed_grads[deep, cols])
        grads[:, :, cols] = product.reshape(BLOCKS, 72, width).astype(HALF16)
    low[:, deep] = jnp.zeros((D, depth), jnp.float32)
    high[:, deep] = jnp.zeros((D, depth), jnp.float32)
    for s in range(BLOCKS):
        rows = inner_tall[s * 36 : (s + 1) * 36, deep]
        low[s * 72 : s * 72 + 36, deep] = rows
        high[s * 72 + 36 : (s + 1) * 72, deep] = rows
    low_rows, high_rows = low[:, deep].astype(HALF16), high[:, deep].astype(HALF16)
    for start, width in ((0, 192), (192, 192), (384, 192)):
        product = matmul(low_rows, cot[deep, start : start + width]) + matmul(
            high_rows, cot[deep, INNER + start : INNER + start + width]
        )
        grads[:, :, QKV + start : QKV + start + width] = product.reshape(BLOCKS, 72, width).astype(
            HALF16
        )


def transposed(rows_ref, count, tall_ref):
    for start, width in columns(D, 128):
        cols = slice(start, start + width)
        tall_ref[cols, 0:count] = rows_ref[0:count, cols].T


def upstream_of(packed_grads, rows, w_qkv, into, count):
    for n in range(3):
        cols = slice(n * SPREAD, (n + 1) * SPREAD)
        into[n * SPREAD : n * SPREAD + count, :] = matmul(packed_grads[rows, :], w_qkv[:, cols])


def upstream_rows(into, start, step):
    return jnp.concatenate(
        [into[pl.ds(pl.multiple_of(n * SPREAD + start, step), step), :] for n in range(3)], axis=-1
    )


def pack_odd(flat, blocks):
    flat[0:GROUP, :] = jnp.zeros((GROUP, D), jnp.float32)
    for i in range(BLOCKS):
        start = 2 * GROUP + i * ODD
        flat[i * SPAN : i * SPAN + ODD, :] = flat[start : start + ODD, :]
    blocks[2] = flat[0:GROUP, :].reshape(BLOCKS, SPAN, D).astype(HALF16)


def kernel(
    lengths,
    mod,
    tokens_far,
    cot_far,
    w_spatial_qkv_far,
    w_spatial_out_far,
    w_temporal_qkv_far,
    w_temporal_out_far,
    grad_tokens,
    out,
    tokens,
    cot,
    w_spatial_qkv,
    w_spatial_out,
    w_temporal_qkv,
    w_temporal_out,
    load_sems,
    cot_blocks,
    cot_place,
    resid_blocks,
    resid_place,
    grad_place,
    flat,
    normed,
    packed,
    heads,
    mixed_heads,
    mixed,
    normed_time,
    packed_time,
    heads_time,
    scaled,
    grad_inner,
    grad_heads,
    out_heads,
    packed_grads,
    inner_tall,
    tall,
    low,
    high,
    bias,
    grads_time,
    grads_space,
    final_time,
    final_space,
    *scratch,
):
    at = Place()
    loads = [
        pltpu.make_async_copy(far, near, load_sems.at[i])
        for i, (far, near) in enumerate(
            (
                (cot_far, cot),
                (tokens_far, tokens),
                (w_spatial_qkv_far, w_spatial_qkv),
                (w_spatial_out_far, w_spatial_out),
                (w_temporal_out_far, w_temporal_out),
                (w_temporal_qkv_far, w_temporal_qkv),
            )
        )
    ]
    for load in loads:
        load.start()
    hail(at.friends())

    taken = 0

    def take(count):
        nonlocal taken
        taken += count
        return scratch[taken - count : taken]

    def trips(source, into):
        return [Exchange(at, source.at[g], into.at[g], *take(3)) for g in range(GROUPS)]

    cot_trips = trips(cot_blocks, cot_place)
    resid_trips = trips(resid_blocks, resid_place)
    grad_trips = trips(cot_blocks, grad_place)
    one = Reduction(at, grads_time, take(5), take(10))
    two = Reduction(at, grads_space, take(5), take(10))
    one_z = Depth(at, final_time, out, 0, 0, take(2), take(10))
    two_z = Depth(at, final_space, out, HALF, 4, take(2), take(10))

    loads[0].wait()
    for g in range(2):
        rows = slice(g * GROUP, (g + 1) * GROUP)
        cot_blocks[g] = wide(cot[rows, :]).reshape(BLOCKS, SPAN, D).astype(HALF16)
    flat[2 * GROUP : ROWS, :] = wide(cot[2 * GROUP : ROWS, :])
    pack_odd(flat, cot_blocks)
    meet(at.friends())
    for trip in cot_trips:
        trip.start()

    loads[1].wait()

    def norm_rows(rows):
        normed[rows, :] = modulated(wide(tokens[rows, :]), mod, 0)

    by_rows(norm_rows)
    loads[2].wait()
    project_rows(normed, slice(0, ROWS), w_spatial_qkv, packed, slice(0, ROWS))
    spread_heads(packed, heads, 3 * HEADS, slice(0, ROWS))
    loads[3].wait()

    def residual(first, last):
        rows = slice(first, last)
        attend_spatial(heads, mixed_heads, rows)
        for h in range(HEADS):
            mixed[rows, h * HEAD_DIM : (h + 1) * HEAD_DIM] = mixed_heads[h, rows]
        for start, width in columns(D):
            cols = slice(start, start + width)
            product = matmul(mixed[rows, :], w_spatial_out[:, cols])
            flat[rows, cols] = wide(tokens[rows, cols]) + mod[2][:, cols] * product

    residual(0, GROUP)
    resid_blocks[0] = flat[0:GROUP, :].reshape(BLOCKS, SPAN, D).astype(HALF16)
    resid_trips[0].start()
    residual(GROUP, ROWS)
    resid_blocks[1] = flat[GROUP : 2 * GROUP, :].reshape(BLOCKS, SPAN, D).astype(HALF16)
    resid_trips[1].start()
    pack_odd(flat, resid_blocks)
    resid_trips[2].start()

    limit = lengths[0].astype(jnp.float32)

    def frame_of(index):
        return jnp.floor(index * (1.0 / SPAN))

    keys = lax.broadcasted_iota(jnp.int32, (GROUP, 1), 0).astype(jnp.float32)
    queries = lax.broadcasted_iota(jnp.int32, (1, GROUP), 1).astype(jnp.float32)
    same = (keys - SPAN * frame_of(keys)) == (queries - SPAN * frame_of(queries))
    bias[...] = jnp.where(same & (frame_of(keys) < limit), 0.0, MASKED)

    def masked_rows(g, start):
        index = lax.broadcasted_iota(jnp.int32, (STEP, 1), 0) + start
        live = jnp.where(frame_of(index.astype(jnp.float32)) < limit, 1.0, 0.0)
        return live * frames(cot_place, g, start)

    def frames(place, g, start):
        count = STEP // SPAN
        return wide(place[g, pl.ds(lax.div(start, SPAN), count)]).reshape(STEP, D)

    def by_group(g, body):
        @pl.loop(0, GROUP, step=STEP)
        def _(start):
            body(g, start, pl.ds(pl.multiple_of(g * GROUP + start, STEP), STEP))

    def scale_cot(g, start, rows):
        scaled[rows, :] = (mod[5] * masked_rows(g, start)).astype(HALF16)

    for g in range(GROUPS):
        cot_trips[g].arrive()
        by_group(g, scale_cot)
    loads[4].wait()
    grad_inner[...] = matmul(scaled[...], w_temporal_out[...], NT).astype(HALF16)
    spread_heads(grad_inner, grad_heads, HEADS, slice(0, SPREAD))
    for trip in cot_trips:
        trip.settle()
    loads[5].wait()

    def norm_time(g, start, rows):
        normed_time[rows, :] = modulated(frames(resid_place, g, start), mod, 3)

    def temporal(members):
        count = len(members) * GROUP
        here, rows = slice(0, count), slice(members[0] * GROUP, members[0] * GROUP + count)
        for g in members:
            resid_trips[g].arrive()
            by_group(g, norm_time)
        project_rows(normed_time, rows, w_temporal_qkv, packed_time, here)
        spread_heads(packed_time, heads_time, 3 * HEADS, here)

        def body(h, _):
            inner = pl.ds(pl.multiple_of(h * HEAD_DIM, 8), HEAD_DIM)
            for i, g in enumerate(members):
                part, whole_rows = slice(i * GROUP, (i + 1) * GROUP), slice(g * GROUP, (g + 1) * GROUP)
                values = heads_time[2 * HEADS + h, part]
                grad_queries, grad_keys, grad_values, soft = head_back(
                    heads_time[h, part],
                    heads_time[HEADS + h, part],
                    values,
                    grad_heads[h, whole_rows],
                    bias[...],
                )
                inner_tall[inner, whole_rows] = matmul(values, soft, TN)
                out_heads[h, part] = grad_queries
                out_heads[HEADS + h, part] = grad_keys
                out_heads[2 * HEADS + h, part] = grad_values
            return 0

        lax.fori_loop(0, HEADS, body, 0, unroll=UNROLL)
        for i in range(3 * HEADS):
            packed_grads[rows, i * HEAD_DIM : (i + 1) * HEAD_DIM] = out_heads[i, here]
        upstream_of(packed_grads, rows, w_temporal_qkv, low, count)

        for i, g in enumerate(members):

            def pull(g, start, _, i=i):
                grad = upstream_rows(low, i * GROUP + start, STEP)
                total = masked_rows(g, start) + norm_pullback(
                    frames(resid_place, g, start), grad, 1.0 + mod[4]
                )
                cot_blocks[g, pl.ds(lax.div(start, SPAN), STEP // SPAN)] = total.reshape(
                    STEP // SPAN, SPAN, D
                ).astype(HALF16)

            by_group(g, pull)
            grad_trips[g].start()

    temporal((0,))
    temporal((1, 2))
    transposed(normed_time, SPREAD, tall)
    weight_blocks(SPREAD, tall, packed_grads, inner_tall, scaled, low, high, grads_time)
    one.start()

    for g in range(GROUPS):
        grad_trips[g].arrive()
    for g in range(2):
        flat[g * GROUP : (g + 1) * GROUP, :] = wide(grad_place[g]).reshape(GROUP, D)
    for i in range(BLOCKS):
        start = 2 * GROUP + i * ODD
        flat[start : start + ODD, :] = wide(grad_place[2, i])[0:ODD]

    def scale(rows):
        scaled[rows, :] = (mod[2] * flat[rows, :]).astype(HALF16)

    by_rows(scale)
    every = slice(0, ROWS)
    grad_inner[every, :] = matmul(scaled[every, :], w_spatial_out[...], NT).astype(HALF16)
    spread_heads(grad_inner, grad_heads, HEADS, every)
    one.first()
    one.second()

    def attend_back(h, _):
        grad_queries, grad_keys, grad_values, _ = head_back(
            heads[h], heads[HEADS + h], heads[2 * HEADS + h], grad_heads[h, every]
        )
        out_heads[h] = grad_queries
        out_heads[HEADS + h] = grad_keys
        out_heads[2 * HEADS + h] = grad_values
        return 0

    lax.fori_loop(0, 4, attend_back, 0, unroll=UNROLL)
    one.third()
    lax.fori_loop(4, HEADS, attend_back, 0, unroll=UNROLL)
    one.fourth()
    for i in range(3 * HEADS):
        packed_grads[every, i * HEAD_DIM : (i + 1) * HEAD_DIM] = out_heads[i]
    transposed(normed, ROWS, tall)
    inner_tall[:, every] = wide(mixed[...]).T
    one.fifth()
    weight_blocks(ROWS, tall, packed_grads, inner_tall, scaled, low, high, grads_space)
    two.start()
    one.sixth(final_time, 0)
    one_z.start()
    two.first()
    two.second()
    upstream_of(packed_grads, every, w_spatial_qkv, low, ROWS)

    def last(start):
        rows = pl.ds(pl.multiple_of(start, STEP), STEP)
        grad = upstream_rows(low, start, STEP)
        grad_tokens[rows, :] = (
            flat[rows, :] + norm_pullback(wide(tokens[rows, :]), grad, 1.0 + mod[1])
        ).astype(HALF16)

    pl.loop(0, ROWS, step=STEP)(last)
    one_z.middle()
    two.third()
    two.fourth()
    one_z.end()
    two.fifth()
    two.sixth(final_space, 0)
    two_z.start()
    two_z.middle()
    two_z.end()
    for user in resid_trips + grad_trips + [one, two, one_z, two_z]:
        user.settle()


def vmem(shape, dtype=HALF16):
    return pltpu.VMEM(shape, dtype)


def run(lengths, mod, tokens, cotangent, w_spatial_qkv, w_spatial_out, w_temporal_qkv, w_temporal_out):
    full = jnp.float32
    place = vmem((GROUPS, BLOCKS, SPAN, D))
    scratch = [
        vmem((ROWS, D)),
        vmem((ROWS, D)),
        vmem((QKV, D)),
        vmem((INNER, D)),
        vmem((QKV, D)),
        vmem((INNER, D)),
        pltpu.SemaphoreType.DMA((6,)),
        place,
        place,
        place,
        place,
        place,
        vmem((ROWS, D), full),
        vmem((ROWS, D)),
        vmem((ROWS, QKV)),
        vmem((3 * HEADS, ROWS, HEAD_DIM)),
        vmem((HEADS, ROWS, HEAD_DIM)),
        vmem((ROWS, INNER)),
        vmem((SPREAD, D)),
        vmem((2 * GROUP, QKV)),
        vmem((3 * HEADS, 2 * GROUP, HEAD_DIM)),
        vmem((SPREAD, D)),
        vmem((SPREAD, INNER)),
        vmem((HEADS, SPREAD, HEAD_DIM)),
        vmem((3 * HEADS, ROWS, HEAD_DIM)),
        vmem((SPREAD, QKV)),
        vmem((INNER, SPREAD), full),
        vmem((D, SPREAD)),
        vmem((D, SPREAD), full),
        vmem((D, SPREAD), full),
        vmem((GROUP, GROUP), full),
        vmem((BLOCKS, 72, WIDE)),
        vmem((BLOCKS, 72, WIDE)),
        vmem((72, HALF)),
        vmem((72, HALF)),
    ]
    for _ in range(3 * GROUPS):
        scratch += exchange_sems()
    for _ in range(2):
        scratch += reduction_buffers() + reduction_sems()
    for _ in range(2):
        scratch += depth_buffers() + depth_sems()
    return pl.pallas_call(
        kernel,
        out_shape=(
            jax.ShapeDtypeStruct((ROWS, D), HALF16),
            jax.ShapeDtypeStruct((2, 72, WIDE), HALF16),
        ),
        in_specs=[pl.BlockSpec(memory_space=pltpu.SMEM), pl.BlockSpec(memory_space=pltpu.VMEM)]
        + [pl.BlockSpec(memory_space=pl.ANY)] * 6,
        out_specs=(pl.BlockSpec(memory_space=pltpu.VMEM), pl.BlockSpec(memory_space=pltpu.VMEM)),
        scratch_shapes=scratch,
        compiler_params=pltpu.CompilerParams(
            collective_id=0, has_side_effects=True, vmem_limit_bytes=VMEM_LIMIT
        ),
    )(lengths, mod, tokens, cotangent, w_spatial_qkv, w_spatial_out, w_temporal_qkv, w_temporal_out)


def unpack_grads(summed, item):
    left, right = (half[:, item * HALF : (item + 1) * HALF] for half in (summed[0], summed[1]))
    tall = right[:, QKV - HALF :]
    return (
        jnp.concatenate([left, right[:, : QKV - HALF]], axis=-1),
        jnp.concatenate([tall[:36], tall[36:]], axis=-1),
    )


def local(
    tokens,
    cotangent,
    modulation,
    lengths,
    w_spatial_qkv,
    w_spatial_out,
    w_temporal_qkv,
    w_temporal_out,
):
    grad_tokens, summed = run(
        lengths,
        modulation.reshape(6, 1, D),
        tokens.reshape(ROWS, D),
        cotangent.reshape(ROWS, D),
        w_spatial_qkv.T,
        w_spatial_out,
        w_temporal_qkv.T,
        w_temporal_out,
    )
    temporal_qkv, temporal_out = unpack_grads(summed, 0)
    spatial_qkv, spatial_out = unpack_grads(summed, 1)
    return (
        grad_tokens.reshape(tokens.shape),
        spatial_qkv,
        spatial_out,
        temporal_qkv,
        temporal_out,
    )


def solution(mesh):
    placed = (
        P("dp", "seq", None, None),
        P("dp", "seq", None, None),
        P("dp", None, None),
        P("dp"),
        P(),
        P(),
        P(),
        P(),
    )
    return jax.shard_map(
        local,
        mesh=mesh,
        in_specs=placed,
        out_specs=(
            P("dp", "seq", None, None),
            P("seq", None),
            P("seq", None),
            P("seq", None),
            P("seq", None),
        ),
        check_vma=False,
    )
```

```python
import jax
import jax.numpy as jnp
from jax import lax
from jax.experimental import pallas as pl
from jax.experimental.pallas import tpu as pltpu
from jax.sharding import PartitionSpec as P

HEADS = 8
HEAD_DIM = 72
F = 16
SIDE = 4
NZ = 8
BLOCKS = 16
WIDE = 2304
HALF = 1152
VMEM_LIMIT = 63 * 1024 * 1024


def remote(src, dst, send, recv, device):
    return pltpu.make_async_remote_copy(
        src_ref=src,
        dst_ref=dst,
        send_sem=send,
        recv_sem=recv,
        device_id=device,
        device_id_type=pl.DeviceIdType.MESH,
    )


def hail(devices):
    barrier = pltpu.get_barrier_semaphore()
    for device in devices:
        pl.semaphore_signal(barrier, inc=1, device_id=device, device_id_type=pl.DeviceIdType.MESH)


def meet(devices):
    pl.semaphore_wait(pltpu.get_barrier_semaphore(), len(devices))


class Exchange:
    def __init__(self, place, source, into, own_sem, send_sems, recv_sems):
        self.place, self.source, self.into = place, source, into
        self.own_sem, self.send_sems, self.recv_sems = own_sem, send_sems, recv_sems

    def to(self, d):
        return lax.rem(self.place.seq + d, BLOCKS)

    def copy(self, d):
        at = self.place
        return remote(
            self.source.at[self.to(d)],
            self.into.at[at.seq],
            self.send_sems.at[d],
            self.recv_sems.at[d],
            (at.dp, self.to(d)),
        )

    def own(self):
        me = self.place.seq
        return pltpu.make_async_copy(self.source.at[me], self.into.at[me], self.own_sem)

    def start(self):
        self.own().start()
        for d in range(1, BLOCKS):
            self.copy(d).start()

    def arrive(self):
        at = self.place
        for d in range(1, BLOCKS):
            origin = lax.rem(at.seq + BLOCKS - d, BLOCKS)
            remote(
                self.source.at[origin],
                self.into.at[origin],
                self.send_sems.at[d],
                self.recv_sems.at[d],
                (at.dp, origin),
            ).wait_recv()
        self.own().wait()

    def settle(self):
        for d in range(1, BLOCKS):
            self.copy(d).wait_send()


def exchange_sems():
    dma = pltpu.SemaphoreType.DMA
    return [dma, dma((BLOCKS,)), dma((BLOCKS,))]


def plus(*refs):
    total = refs[0].astype(jnp.float32)
    for ref in refs[1:]:
        total = total + ref.astype(jnp.float32)
    return total.astype(jnp.bfloat16)


WHOLE = (((0, 640), (640, 512)), (((0, 384), (384, 256)), ((0, 256), (256, 256))))
UPPER = (((512, 384), (896, 256)), (((0, 256), (256, 128)), ((0, 128), (128, 128))))
LOWER = (((0, 256), (256, 256)), (((0, 128), (128, 128)), ((0, 128), (128, 128))))
DMA_COUNTS = (
    (BLOCKS, 2),
    (2, 2, 2),
    (2, 2, SIDE),
    (2, 2),
    (2, 2),
)


class Place:
    def __init__(self):
        dp, seq = lax.axis_index("dp"), lax.axis_index("seq")
        self.dp, self.seq = dp, seq
        self.z, self.c = lax.div(dp, 2), lax.rem(dp, 2)
        self.y, self.x = lax.div(seq, SIDE), lax.rem(seq, SIDE)
        self.twin = (self.z * 2 + 1 - self.c, seq)

    def neighbour(self, axis, dirn):
        step = 1 if dirn == 0 else SIDE - 1
        if axis == 0:
            return (self.dp, self.y * SIDE + lax.rem(self.x + step, SIDE))
        return (self.dp, lax.rem(self.y + step, SIDE) * SIDE + self.x)

    def along_z(self, d):
        return (lax.rem(self.z + d, NZ) * 2 + self.c, self.seq)

    def line(self):
        return [(self.dp, lax.rem(self.seq + d, BLOCKS)) for d in range(1, BLOCKS)]

    def friends(self):
        return [self.twin] + self.line() + [self.along_z(d) for d in range(1, NZ)]


class Reduction:
    def __init__(self, place, grads, cuts, buffers, sems):
        self.place, self.grads = place, grads
        self.cuts, self.last_cuts = cuts
        self.acc, self.near, self.far, self.near_last, self.far_last = buffers
        (
            self.core_send,
            self.core_recv,
            self.near_send,
            self.near_recv,
            self.far_send,
            self.far_recv,
            self.near_last_send,
            self.near_last_recv,
            self.far_last_send,
            self.far_last_recv,
        ) = sems

    def lanes(self, part):
        return pl.ds(self.cuts[part][0], self.cuts[part][1])

    def lanes_of(self, part, core):
        return pl.ds(pl.multiple_of(core * HALF + self.cuts[part][0], 128), self.cuts[part][1])

    def block(self, part, j, d):
        at = self.place
        if part == 0:
            return j * SIDE + lax.rem(at.x + d, SIDE)
        return lax.rem(at.y + d, SIDE) * SIDE + j

    def core_copy(self, part, b):
        at = self.place
        return remote(
            self.grads.at[b, :, self.lanes_of(part, 1 - at.c)],
            self.acc.at[b, :, self.lanes(part)],
            self.core_send.at[b, part],
            self.core_recv.at[b, part],
            at.twin,
        )

    def near_copy(self, part, dirn, k, b):
        return remote(
            self.acc.at[b, :, self.lanes(part)],
            self.near.at[part, dirn, k, :, pl.ds(0, self.cuts[part][1])],
            self.near_send.at[part, dirn, k],
            self.near_recv.at[part, dirn, k],
            self.place.neighbour(part, dirn),
        )

    def far_copy(self, part, dirn, j, b):
        return remote(
            self.acc.at[b, :, self.lanes(part)],
            self.far.at[part, dirn, j, :, pl.ds(0, self.cuts[part][1])],
            self.far_send.at[part, dirn, j],
            self.far_recv.at[part, dirn, j],
            self.place.neighbour(part, dirn),
        )

    def last_lanes(self, part, dirn):
        start, width = self.last_cuts[part][dirn]
        return pl.ds(self.cuts[part][0] + start, width)

    def near_last_copy(self, part, dirn, b):
        width = self.last_cuts[part][dirn][1]
        return remote(
            self.acc.at[b, :, self.last_lanes(part, dirn)],
            self.near_last.at[part, dirn, :, pl.ds(0, width)],
            self.near_last_send.at[part, dirn],
            self.near_last_recv.at[part, dirn],
            self.place.neighbour(1 - part, dirn),
        )

    def far_last_copy(self, part, dirn, b):
        return remote(
            self.acc.at[b, :, self.lanes(part)],
            self.far_last.at[part, dirn, :, pl.ds(0, self.cuts[part][1])],
            self.far_last_send.at[part, dirn],
            self.far_last_recv.at[part, dirn],
            self.place.neighbour(1 - part, dirn),
        )

    def gather(self, part, b, *more):
        self.core_copy(part, b).wait_recv()
        lanes = self.lanes(part)
        mine = self.grads[b, :, self.lanes_of(part, self.place.c)]
        self.acc[b, :, lanes] = plus(mine, self.acc[b, :, lanes], *more)

    def start(self):
        for d in (2, 1, 3, 0):

            @pl.loop(0, SIDE)
            def _(j):
                for part in range(2):
                    self.core_copy(part, self.block(part, j, d)).start()

    def first(self):
        for dirn in range(2):

            @pl.loop(0, 2)
            def _(k):
                for part in range(2):
                    b = self.block(part, 2 * dirn + k, 2)
                    self.gather(part, b)
                    self.near_copy(part, dirn, k, b).start()

    def second(self):
        for dirn in range(2):

            @pl.loop(0, 2)
            def _(k):
                for part in range(2):
                    j = 2 * (1 - dirn) + k
                    b = self.block(part, j, 1 + 2 * dirn)
                    self.gather(part, b)
                    self.far_copy(part, dirn, j, b).start()

    def third(self):
        for dirn in range(2):

            @pl.loop(0, 2)
            def _(k):
                for part in range(2):
                    j = 2 * dirn + k
                    b = self.block(part, j, 1 + 2 * dirn)
                    self.near_copy(part, dirn, k, b).wait_recv()
                    self.gather(part, b, self.near[part, dirn, k, :, pl.ds(0, self.cuts[part][1])])
                    self.far_copy(part, dirn, j, b).start()

    def finish(self, part, d):
        at = self.place
        b = self.block(1 - part, (at.x, at.y)[part], d)
        j = lax.rem((at.y, at.x)[part] + d, SIDE)
        for dirn in range(2):
            self.far_copy(part, dirn, j, b).wait_recv()
        width = pl.ds(0, self.cuts[part][1])
        self.gather(part, b, self.far[part, 0, j, :, width], self.far[part, 1, j, :, width])
        return b

    def fourth(self):
        for part in range(2):
            b = self.finish(part, 2)
            for dirn in range(2):
                self.near_last_copy(part, dirn, b).start()

    def fifth(self):
        for dirn in range(2):
            for part in range(2):
                b = self.finish(part, 1 + 2 * dirn)
                self.near_last_copy(part, dirn, b).wait_recv()
                lanes = self.last_lanes(part, dirn)
                width = self.last_cuts[part][dirn][1]
                self.acc[b, :, lanes] = plus(
                    self.acc[b, :, lanes], self.near_last[part, dirn, :, pl.ds(0, width)]
                )
                self.far_last_copy(part, dirn, b).start()

    def sixth(self, final):
        for part in range(2):
            b = self.finish(part, 0)
            for dirn in range(2):
                self.far_last_copy(part, dirn, b).wait_recv()
            start, width = self.cuts[part]
            final[:, start : start + width] = plus(
                self.acc[b, :, self.lanes(part)],
                self.far_last[part, 0, :, pl.ds(0, width)],
                self.far_last[part, 1, :, pl.ds(0, width)],
            )

    def settle(self):
        for part in range(2):

            @pl.loop(0, BLOCKS)
            def _(b):
                self.core_copy(part, b).wait_send()

            for dirn in range(2):

                @pl.loop(0, 2)
                def _(k):
                    self.near_copy(part, dirn, k, 0).wait_send()

                @pl.loop(0, SIDE)
                def _(j):
                    self.far_copy(part, dirn, j, 0).wait_send()

                self.near_last_copy(part, dirn, 0).wait_send()
                self.far_last_copy(part, dirn, 0).wait_send()


def reduction_buffers(width):
    half = jnp.bfloat16
    return [
        pltpu.VMEM((2, 2, 2, 72, width), half),
        pltpu.VMEM((2, 2, SIDE, 72, width), half),
        pltpu.VMEM((2, 2, 72, width), half),
        pltpu.VMEM((2, 2, 72, width), half),
    ]


def reduction_sems():
    return [pltpu.SemaphoreType.DMA(counts) for counts in DMA_COUNTS for _ in range(2)]


class Depth:
    def __init__(self, place, final, out, offset, tiles, arrived, sems):
        self.place, self.final, self.out = place, final, out
        self.offset, self.tiles, self.arrived = offset, tiles, arrived
        self.up_send, self.up_recv, self.down_send, self.down_recv, self.pair_send, self.pair_recv = sems

    def spot(self, i, core):
        start = self.offset + self.tiles[i][0] * 128
        return self.out.at[core, :, pl.ds(start, 128)]

    def device(self, z):
        return (z * 2 + self.place.c, self.place.seq)

    def up(self, i, z):
        tile, owner, slot = self.tiles[i]
        return remote(
            self.final.at[:, pl.ds(tile * 128, 128)],
            self.arrived.at[slot, z],
            self.up_send.at[i],
            self.up_recv.at[i, z],
            self.device(owner),
        )

    def down(self, i, z):
        spot = self.spot(i, self.place.c)
        return remote(spot, spot, self.down_send.at[i, z], self.down_recv.at[i], self.device(z))

    def pair(self, i, core):
        spot = self.spot(i, core)
        return remote(spot, spot, self.pair_send.at[i], self.pair_recv.at[i], self.place.twin)

    def owned(self, body):
        for i, (_, owner, _) in enumerate(self.tiles):
            pl.when(self.place.z == owner)(lambda i=i: body(i))

    def others(self, body):
        for i, (_, owner, _) in enumerate(self.tiles):
            pl.when(self.place.z != owner)(lambda i=i: body(i))

    def away(self, i):
        return [z for z in range(NZ) if z != self.tiles[i][1]]

    def start(self):
        self.others(lambda i: self.up(i, self.place.z).start())

    def middle(self):
        def add(i):
            tile, _, slot = self.tiles[i]
            total = self.final[:, tile * 128 : tile * 128 + 128].astype(jnp.float32)
            for z in self.away(i):
                self.up(i, z).wait_recv()
                total = total + self.arrived[slot, z].astype(jnp.float32)
            self.spot(i, self.place.c)[...] = total.astype(jnp.bfloat16)
            for z in self.away(i):
                self.down(i, z).start()
            self.pair(i, self.place.c).start()

        self.owned(add)

    def end(self):
        def forward(i):
            self.down(i, self.place.z).wait_recv()
            self.pair(i, self.place.c).start()

        self.others(forward)
        for i in range(len(self.tiles)):
            self.pair(i, 1 - self.place.c).wait_recv()

    def settle(self):
        self.others(lambda i: self.up(i, self.place.z).wait_send())

        def left(i):
            for z in self.away(i):
                self.down(i, z).wait_send()

        self.owned(left)
        for i in range(len(self.tiles)):
            self.pair(i, self.place.c).wait_send()


TILES_TIME = tuple((k, k % NZ, k // NZ) for k in range(9))
TILES_UPPER = tuple((k, k - 4, 0) for k in range(4, 9))
TILES_LOWER = tuple((k, (5, 6, 7, 2)[k], 0) for k in range(4))


def depth_sems(tiles):
    dma = pltpu.SemaphoreType.DMA
    n = len(tiles)
    return [dma((n,)), dma((n, NZ)), dma((n, NZ)), dma((n,)), dma((n,)), dma((n,))]


NORM_EPS = 1e-06
MASKED = -1e30
ROWS = 320
SPAN = 8
GROUPS = 3
GROUP = SPAN * BLOCKS
SPREAD = GROUPS * GROUP
ODD = 4
D = 1152
INNER = 576
QKV = 1728
UNROLL = 4
NARROW = 640
REST = D - NARROW
SHARP = HEAD_DIM ** (-0.5)
SHARP2 = SHARP * 1.4426950408889634
NN = (((1,), (0,)), ((), ()))
NT = (((1,), (1,)), ((), ()))
TN = (((0,), (0,)), ((), ()))
HALF16 = jnp.bfloat16


def matmul(left, right, dims=NN):
    return lax.dot_general(left, right, dims, preferred_element_type=jnp.float32)


def columns(total, width=256):
    return [(start, min(width, total - start)) for start in range(0, total, width)]


def normalise(source):
    average = jnp.mean(source, axis=-1, keepdims=True)
    centred = source - average
    variance = jnp.mean(centred * centred, axis=-1, keepdims=True)
    spread = lax.rsqrt(variance + NORM_EPS)
    return centred * spread, spread


def modulated(source, mod, first):
    unit, _ = normalise(source)
    return (unit * (1.0 + mod[first + 1]) + mod[first]).astype(HALF16)


def norm_pullback(source, upstream, gain):
    unit, spread = normalise(source)
    grad = upstream * gain
    along = jnp.mean(grad * unit, axis=-1, keepdims=True)
    return spread * (grad - jnp.mean(grad, axis=-1, keepdims=True) - unit * along)


def wide(ref_value):
    return ref_value.astype(jnp.float32)


def project_rows(rows_ref, rows, weight_ref, out_ref, out_rows):
    for start, width in columns(weight_ref.shape[0]):
        cols = slice(start, start + width)
        out_ref[out_rows, cols] = matmul(rows_ref[rows, :], weight_ref[cols, :], NT).astype(HALF16)


def spread_heads(wide_ref, heads_ref, count, rows):
    for i in range(count):
        heads_ref[i, rows] = wide_ref[rows, i * HEAD_DIM : (i + 1) * HEAD_DIM]


def softmax(scores, axis):
    exponent = jnp.exp2((scores - jnp.max(scores, axis=axis, keepdims=True)) * SHARP2)
    return exponent * (1.0 / jnp.sum(exponent, axis=axis, keepdims=True))


def attend_spatial(heads, mixed_heads, rows):
    def body(h, _):
        scores = matmul(heads[h, rows], heads[HEADS + h], NT)
        soft = softmax(scores, -1).astype(HALF16)
        mixed_heads[h, rows] = matmul(soft, heads[2 * HEADS + h]).astype(HALF16)
        return 0

    lax.fori_loop(0, HEADS, body, 0, unroll=UNROLL)


def head_back(queries, keys, values, upstream, bias=None):
    scores = matmul(keys, queries, NT)
    if bias is not None:
        scores = scores + bias
    soft = softmax(scores, 0)
    soft_rounded = soft.astype(HALF16)
    raw = matmul(values, upstream, NT)
    centred = raw - jnp.sum(raw * soft, axis=0, keepdims=True)
    grad_scores = (soft * centred).astype(HALF16)
    grad_values = matmul(soft_rounded, upstream).astype(HALF16)
    grad_keys = (matmul(grad_scores, queries) * SHARP).astype(HALF16)
    grad_queries = (matmul(grad_scores, keys, TN) * SHARP).astype(HALF16)
    return grad_queries, grad_keys, grad_values, soft_rounded


def qkv_blocks(depth, cuts, tall, packed_grads, grads):
    deep = slice(0, depth)
    for start, width in cuts:
        cols = slice(start, start + width)
        product = matmul(tall[:, deep], packed_grads[deep, cols])
        grads[:, :, cols] = product.reshape(BLOCKS, 72, width).astype(HALF16)


def out_blocks(depth, inner_tall, cot, low, high, grads):
    deep = slice(0, depth)
    low[:, deep] = jnp.zeros((D, depth), jnp.float32)
    high[:, deep] = jnp.zeros((D, depth), jnp.float32)
    for s in range(BLOCKS):
        rows = inner_tall[s * 36 : (s + 1) * 36, deep]
        low[s * 72 : s * 72 + 36, deep] = rows
        high[s * 72 + 36 : (s + 1) * 72, deep] = rows
    low_rows, high_rows = low[:, deep].astype(HALF16), high[:, deep].astype(HALF16)
    for start, width in ((0, 192), (192, 192), (384, 192)):
        product = matmul(low_rows, cot[deep, start : start + width]) + matmul(
            high_rows, cot[deep, INNER + start : INNER + start + width]
        )
        grads[:, :, QKV + start : QKV + start + width] = product.reshape(BLOCKS, 72, width).astype(
            HALF16
        )


def transposed(rows_ref, count, tall_ref):
    for start, width in columns(D, 128):
        cols = slice(start, start + width)
        tall_ref[cols, 0:count] = rows_ref[0:count, cols].T


def upstream_of(packed_grads, rows, w_qkv, into, count):
    for n in range(3):
        cols = slice(n * SPREAD, (n + 1) * SPREAD)
        into[n * SPREAD : n * SPREAD + count, :] = matmul(packed_grads[rows, :], w_qkv[:, cols])


def upstream_rows(into, start, count):
    return jnp.concatenate(
        [into[n * SPREAD + start : n * SPREAD + start + count, :] for n in range(3)], axis=-1
    )


def fold_odd(flat, first, step, pad, blocks):
    for i in range(BLOCKS):
        rows = slice(first + i * step, first + i * step + ODD)
        pad[i * SPAN : i * SPAN + ODD, :] = flat[rows, 0:NARROW]
        pad[i * SPAN + ODD : (i + 1) * SPAN, 0:REST] = flat[rows, NARROW:D]
    blocks[...] = pad[...].reshape(BLOCKS, SPAN, NARROW).astype(HALF16)


def unfold_odd(blocks, pad, flat, first, step):
    pad[...] = wide(blocks[...]).reshape(GROUP, NARROW)
    for i in range(BLOCKS):
        rows = slice(first + i * step, first + i * step + ODD)
        flat[rows, 0:NARROW] = pad[i * SPAN : i * SPAN + ODD, :]
        flat[rows, NARROW:D] = pad[i * SPAN + ODD : (i + 1) * SPAN, 0:REST]


def as_blocks(rows):
    return rows.reshape(BLOCKS, SPAN, D).astype(HALF16)


def kernel(
    lengths,
    mod,
    tokens_far,
    cot_far,
    w_spatial_qkv_far,
    w_spatial_out_far,
    w_temporal_qkv_far,
    w_temporal_out_far,
    grad_tokens,
    out,
    tokens,
    cot,
    w_spatial_qkv,
    w_spatial_out,
    w_temporal_qkv,
    w_temporal_out,
    load_sems,
    cot_blocks,
    cot_place,
    resid_blocks,
    resid_place,
    grad_place,
    cot_odd,
    cot_odd_place,
    resid_odd,
    resid_odd_place,
    grad_odd_place,
    pad,
    flat,
    packed,
    heads,
    mixed_heads,
    mixed,
    normed_time,
    packed_time,
    heads_time,
    scaled,
    grad_inner,
    grad_heads,
    out_heads,
    packed_grads,
    inner_tall,
    tall,
    low,
    high,
    bias,
    grads_time,
    grads_space,
    final_time,
    final_space,
    acc_time,
    acc_space,
    *scratch,
):
    at = Place()
    loads = [
        pltpu.make_async_copy(far, near, load_sems.at[i])
        for i, (far, near) in enumerate(
            (
                (cot_far, cot),
                (tokens_far, tokens),
                (w_spatial_qkv_far, w_spatial_qkv),
                (w_spatial_out_far, w_spatial_out),
                (w_temporal_out_far, w_temporal_out),
                (w_temporal_qkv_far, w_temporal_qkv),
            )
        )
    ]
    for load in loads:
        load.start()
    hail(at.friends())

    taken = 0

    def take(count):
        nonlocal taken
        taken += count
        return scratch[taken - count : taken]

    def trips(source, into, odd, odd_into):
        pairs = [(source.at[g], into.at[g]) for g in range(2)] + [(odd, odd_into)]
        return [Exchange(at, left, right, *take(3)) for left, right in pairs]

    cot_trips = trips(cot_blocks, cot_place, cot_odd, cot_odd_place)
    resid_trips = trips(resid_blocks, resid_place, resid_odd, resid_odd_place)
    grad_trips = trips(cot_blocks, grad_place, cot_odd, grad_odd_place)
    one = Reduction(at, grads_time, WHOLE, [acc_time, *take(4)], take(10))
    two = Reduction(at, grads_space, UPPER, [acc_space, *take(4)], take(10))
    three = Reduction(at, grads_space, LOWER, [acc_space, *take(4)], take(10))
    one_z = Depth(at, final_time, out, 0, TILES_TIME, *take(1), take(6))
    two_z = Depth(at, final_space, out, HALF, TILES_UPPER, *take(1), take(6))
    three_z = Depth(at, final_space, out, HALF, TILES_LOWER, *take(1), take(6))

    pad[...] = jnp.zeros_like(pad)
    loads[0].wait()
    for g in range(2):
        cot_blocks[g] = as_blocks(wide(cot[g * GROUP : (g + 1) * GROUP, :]))
    flat[2 * GROUP : ROWS, :] = wide(cot[2 * GROUP : ROWS, :])
    fold_odd(flat, 2 * GROUP, ODD, pad, cot_odd)
    meet(at.friends())
    for trip in cot_trips:
        trip.start()

    every = slice(0, ROWS)
    normed = cot
    loads[1].wait()
    normed[...] = modulated(wide(tokens[...]), mod, 0)
    loads[2].wait()
    project_rows(normed, every, w_spatial_qkv, packed, every)
    spread_heads(packed, heads, 3 * HEADS, every)
    loads[3].wait()

    def residual(first, last):
        rows = slice(first, last)
        attend_spatial(heads, mixed_heads, rows)
        for h in range(HEADS):
            mixed[rows, h * HEAD_DIM : (h + 1) * HEAD_DIM] = mixed_heads[h, rows]
        for start, width in columns(D):
            cols = slice(start, start + width)
            product = matmul(mixed[rows, :], w_spatial_out[:, cols])
            flat[rows, cols] = wide(tokens[rows, cols]) + mod[2][:, cols] * product

    residual(GROUP, ROWS)
    resid_blocks[1] = as_blocks(flat[GROUP : 2 * GROUP, :])
    resid_trips[1].start()
    fold_odd(flat, 2 * GROUP, ODD, pad, resid_odd)
    resid_trips[2].start()
    residual(0, GROUP)
    resid_blocks[0] = as_blocks(flat[0:GROUP, :])
    resid_trips[0].start()

    limit = lengths[0].astype(jnp.float32)

    def frame_of(index):
        return jnp.floor(index * (1.0 / SPAN))

    keys = lax.broadcasted_iota(jnp.int32, (GROUP, 1), 0).astype(jnp.float32)
    queries = lax.broadcasted_iota(jnp.int32, (1, GROUP), 1).astype(jnp.float32)
    same = (keys - SPAN * frame_of(keys)) == (queries - SPAN * frame_of(queries))
    bias[...] = jnp.where(same & (frame_of(keys) < limit), 0.0, MASKED)

    def frames(place, g):
        return wide(place[g]).reshape(GROUP, D)

    def masked_rows(g):
        return jnp.where(frame_of(keys) < limit, 1.0, 0.0) * frames(cot_place, g)

    def settle_odd(trip, odd_place, place):
        trip.arrive()
        flat[0:GROUP, :] = jnp.zeros((GROUP, D), jnp.float32)
        unfold_odd(odd_place, pad, flat, 0, SPAN)
        place[2] = as_blocks(flat[0:GROUP, :])

    for g in range(2):
        cot_trips[g].arrive()
    settle_odd(cot_trips[2], cot_odd_place, cot_place)
    for g in range(GROUPS):
        scaled[g * GROUP : (g + 1) * GROUP, :] = (mod[5] * masked_rows(g)).astype(HALF16)
    loads[4].wait()
    grad_inner[...] = matmul(scaled[...], w_temporal_out[...], NT).astype(HALF16)
    spread_heads(grad_inner, grad_heads, HEADS, slice(0, SPREAD))
    for trip in cot_trips:
        trip.settle()
    loads[5].wait()

    def temporal(members):
        count = len(members) * GROUP
        here, rows = slice(0, count), slice(members[0] * GROUP, members[0] * GROUP + count)
        for g in members:
            if g == 2:
                settle_odd(resid_trips[g], resid_odd_place, resid_place)
            else:
                resid_trips[g].arrive()
            normed_time[g * GROUP : (g + 1) * GROUP, :] = modulated(frames(resid_place, g), mod, 3)
        project_rows(normed_time, rows, w_temporal_qkv, packed_time, here)
        spread_heads(packed_time, heads_time, 3 * HEADS, here)

        def body(h, _):
            inner = pl.ds(pl.multiple_of(h * HEAD_DIM, 8), HEAD_DIM)
            for i, g in enumerate(members):
                part, whole_rows = slice(i * GROUP, (i + 1) * GROUP), slice(g * GROUP, (g + 1) * GROUP)
                values = heads_time[2 * HEADS + h, part]
                grad_queries, grad_keys, grad_values, soft = head_back(
                    heads_time[h, part],
                    heads_time[HEADS + h, part],
                    values,
                    grad_heads[h, whole_rows],
                    bias[...],
                )
                inner_tall[inner, whole_rows] = matmul(values, soft, TN)
                out_heads[h, part] = grad_queries
                out_heads[HEADS + h, part] = grad_keys
                out_heads[2 * HEADS + h, part] = grad_values
            return 0

        lax.fori_loop(0, HEADS, body, 0, unroll=UNROLL)
        for i in range(3 * HEADS):
            packed_grads[rows, i * HEAD_DIM : (i + 1) * HEAD_DIM] = out_heads[i, here]
        upstream_of(packed_grads, rows, w_temporal_qkv, low, count)
        for i, g in enumerate(members):
            total = masked_rows(g) + norm_pullback(
                frames(resid_place, g), upstream_rows(low, i * GROUP, GROUP), 1.0 + mod[4]
            )
            if g == 2:
                flat[0:GROUP, :] = total
                fold_odd(flat, 0, SPAN, pad, cot_odd)
            else:
                cot_blocks[g] = as_blocks(total)
            grad_trips[g].start()

    temporal((1, 2))
    temporal((0,))
    transposed(normed_time, SPREAD, tall)
    qkv_blocks(SPREAD, columns(QKV), tall, packed_grads, grads_time)
    out_blocks(SPREAD, inner_tall, scaled, low, high, grads_time)
    one.start()

    transposed(normed, ROWS, tall)
    inner_tall[:, every] = wide(mixed[...]).T
    for g in (1, 2, 0):
        grad_trips[g].arrive()
    unfold_odd(grad_odd_place, pad, flat, 2 * GROUP, ODD)
    for g in range(2):
        flat[g * GROUP : (g + 1) * GROUP, :] = frames(grad_place, g)
    scaled[every, :] = (mod[2] * flat[...]).astype(HALF16)
    grad_inner[every, :] = matmul(scaled[every, :], w_spatial_out[...], NT).astype(HALF16)
    spread_heads(grad_inner, grad_heads, HEADS, every)
    one.first()
    one.second()
    out_blocks(ROWS, inner_tall, scaled, low, high, grads_space)

    def attend_back(h, _):
        grad_queries, grad_keys, grad_values, _ = head_back(
            heads[h], heads[HEADS + h], heads[2 * HEADS + h], grad_heads[h, every]
        )
        out_heads[h] = grad_queries
        out_heads[HEADS + h] = grad_keys
        out_heads[2 * HEADS + h] = grad_values
        return 0

    lax.fori_loop(0, HEADS, attend_back, 0, unroll=UNROLL)
    one.third()
    for i in range(3 * HEADS):
        packed_grads[every, i * HEAD_DIM : (i + 1) * HEAD_DIM] = out_heads[i]
    upper = ((512, 256), (768, 256), (1024, 128), (1664, 64))
    lower = ((0, 256), (256, 256), (1152, 256), (1408, 256))
    qkv_blocks(ROWS, upper, tall, packed_grads, grads_space)
    two.start()
    qkv_blocks(ROWS, lower, tall, packed_grads, grads_space)
    three.start()
    upstream_of(packed_grads, every, w_spatial_qkv, low, ROWS)
    one.fourth()
    two.first()
    two.second()
    grad_tokens[...] = (
        flat[...]
        + norm_pullback(wide(tokens[...]), upstream_rows(low, 0, ROWS), 1.0 + mod[1])
    ).astype(HALF16)
    one.fifth()
    three.first()
    three.second()
    two.third()
    one.sixth(final_time)
    one_z.start()
    three.third()
    two.fourth()
    one_z.middle()
    two.fifth()
    three.fourth()
    two.sixth(final_space)
    two_z.start()
    one_z.end()
    three.fifth()
    two_z.middle()
    three.sixth(final_space)
    three_z.start()
    two_z.end()
    three_z.middle()
    three_z.end()
    for user in resid_trips + grad_trips + [one, two, three, one_z, two_z, three_z]:
        user.settle()


def vmem(shape, dtype=HALF16):
    return pltpu.VMEM(shape, dtype)


def run(lengths, mod, tokens, cotangent, w_spatial_qkv, w_spatial_out, w_temporal_qkv, w_temporal_out):
    full = jnp.float32
    sent, place, odd = vmem((2, BLOCKS, SPAN, D)), vmem((GROUPS, BLOCKS, SPAN, D)), vmem((BLOCKS, SPAN, NARROW))
    scratch = [
        vmem((ROWS, D)),
        vmem((ROWS, D)),
        vmem((QKV, D)),
        vmem((INNER, D)),
        vmem((QKV, D)),
        vmem((INNER, D)),
        pltpu.SemaphoreType.DMA((6,)),
        sent,
        place,
        sent,
        place,
        sent,
        odd,
        odd,
        odd,
        odd,
        odd,
        vmem((GROUP, NARROW), full),
        vmem((ROWS, D), full),
        vmem((ROWS, QKV)),
        vmem((3 * HEADS, ROWS, HEAD_DIM)),
        vmem((HEADS, ROWS, HEAD_DIM)),
        vmem((ROWS, INNER)),
        vmem((SPREAD, D)),
        vmem((2 * GROUP, QKV)),
        vmem((3 * HEADS, 2 * GROUP, HEAD_DIM)),
        vmem((SPREAD, D)),
        vmem((SPREAD, INNER)),
        vmem((HEADS, SPREAD, HEAD_DIM)),
        vmem((3 * HEADS, ROWS, HEAD_DIM)),
        vmem((SPREAD, QKV)),
        vmem((INNER, SPREAD), full),
        vmem((D, SPREAD)),
        vmem((D, SPREAD), full),
        vmem((D, SPREAD), full),
        vmem((GROUP, GROUP), full),
        vmem((BLOCKS, 72, WIDE)),
        vmem((BLOCKS, 72, WIDE)),
        vmem((72, HALF)),
        vmem((72, HALF)),
        vmem((BLOCKS, 72, HALF)),
        vmem((BLOCKS, 72, HALF)),
    ]
    for _ in range(3 * GROUPS):
        scratch += exchange_sems()
    for width in (640, 384, 256):
        scratch += reduction_buffers(width) + reduction_sems()
    for tiles in (TILES_TIME, TILES_UPPER, TILES_LOWER):
        scratch += [vmem((2, NZ, 72, 128))] + depth_sems(tiles)
    return pl.pallas_call(
        kernel,
        out_shape=(
            jax.ShapeDtypeStruct((ROWS, D), HALF16),
            jax.ShapeDtypeStruct((2, 72, WIDE), HALF16),
        ),
        in_specs=[pl.BlockSpec(memory_space=pltpu.SMEM), pl.BlockSpec(memory_space=pltpu.VMEM)]
        + [pl.BlockSpec(memory_space=pl.ANY)] * 6,
        out_specs=(pl.BlockSpec(memory_space=pltpu.VMEM), pl.BlockSpec(memory_space=pltpu.VMEM)),
        scratch_shapes=scratch,
        compiler_params=pltpu.CompilerParams(
            collective_id=0, has_side_effects=True, vmem_limit_bytes=VMEM_LIMIT
        ),
    )(lengths, mod, tokens, cotangent, w_spatial_qkv, w_spatial_out, w_temporal_qkv, w_temporal_out)


def unpack_grads(summed, item):
    left, right = (half[:, item * HALF : (item + 1) * HALF] for half in (summed[0], summed[1]))
    tall = right[:, QKV - HALF :]
    return (
        jnp.concatenate([left, right[:, : QKV - HALF]], axis=-1),
        jnp.concatenate([tall[:36], tall[36:]], axis=-1),
    )


def local(
    tokens,
    cotangent,
    modulation,
    lengths,
    w_spatial_qkv,
    w_spatial_out,
    w_temporal_qkv,
    w_temporal_out,
):
    grad_tokens, summed = run(
        lengths,
        modulation.reshape(6, 1, D),
        tokens.reshape(ROWS, D),
        cotangent.reshape(ROWS, D),
        w_spatial_qkv.T,
        w_spatial_out,
        w_temporal_qkv.T,
        w_temporal_out,
    )
    temporal_qkv, temporal_out = unpack_grads(summed, 0)
    spatial_qkv, spatial_out = unpack_grads(summed, 1)
    return (
        grad_tokens.reshape(tokens.shape),
        spatial_qkv,
        spatial_out,
        temporal_qkv,
        temporal_out,
    )


def solution(mesh):
    placed = (
        P("dp", "seq", None, None),
        P("dp", "seq", None, None),
        P("dp", None, None),
        P("dp"),
        P(),
        P(),
        P(),
        P(),
    )
    return jax.shard_map(
        local,
        mesh=mesh,
        in_specs=placed,
        out_specs=(
            P("dp", "seq", None, None),
            P("seq", None),
            P("seq", None),
            P("seq", None),
            P("seq", None),
        ),
        check_vma=False,
    )
```

```python
import jax
import jax.numpy as jnp
from jax import lax
from jax.experimental import pallas as pl
from jax.experimental.pallas import tpu as pltpu
from jax.sharding import PartitionSpec as P

HEADS = 8
HEAD_DIM = 72
F = 16
SIDE = 4
NZ = 8
BLOCKS = 16
WIDE = 2304
HALF = 1152
VMEM_LIMIT = 63 * 1024 * 1024


def remote(src, dst, send, recv, device):
    return pltpu.make_async_remote_copy(
        src_ref=src,
        dst_ref=dst,
        send_sem=send,
        recv_sem=recv,
        device_id=device,
        device_id_type=pl.DeviceIdType.MESH,
    )


def hail(devices):
    barrier = pltpu.get_barrier_semaphore()
    for device in devices:
        pl.semaphore_signal(barrier, inc=1, device_id=device, device_id_type=pl.DeviceIdType.MESH)


def meet(devices):
    pl.semaphore_wait(pltpu.get_barrier_semaphore(), len(devices))


class Exchange:
    def __init__(self, place, source, into, own_sem, send_sems, recv_sems):
        self.place, self.source, self.into = place, source, into
        self.own_sem, self.send_sems, self.recv_sems = own_sem, send_sems, recv_sems

    def to(self, d):
        return lax.rem(self.place.seq + d, BLOCKS)

    def copy(self, d):
        at = self.place
        return remote(
            self.source.at[self.to(d)],
            self.into.at[at.seq],
            self.send_sems.at[d],
            self.recv_sems.at[d],
            (at.dp, self.to(d)),
        )

    def own(self):
        me = self.place.seq
        return pltpu.make_async_copy(self.source.at[me], self.into.at[me], self.own_sem)

    def start(self):
        self.own().start()
        for d in range(1, BLOCKS):
            self.copy(d).start()

    def arrive(self):
        at = self.place
        for d in range(1, BLOCKS):
            origin = lax.rem(at.seq + BLOCKS - d, BLOCKS)
            remote(
                self.source.at[origin],
                self.into.at[origin],
                self.send_sems.at[d],
                self.recv_sems.at[d],
                (at.dp, origin),
            ).wait_recv()
        self.own().wait()

    def settle(self):
        for d in range(1, BLOCKS):
            self.copy(d).wait_send()


def exchange_sems():
    dma = pltpu.SemaphoreType.DMA
    return [dma, dma((BLOCKS,)), dma((BLOCKS,))]


def plus(*refs):
    total = refs[0].astype(jnp.float32)
    for ref in refs[1:]:
        total = total + ref.astype(jnp.float32)
    return total.astype(jnp.bfloat16)


CUTS = ((0, 640), (640, 512))
DMA_COUNTS = (
    (BLOCKS, 2),
    (2, 2, 2),
    (2, 2, SIDE),
    (2, SIDE),
)


class Place:
    def __init__(self):
        dp, seq = lax.axis_index("dp"), lax.axis_index("seq")
        self.dp, self.seq = dp, seq
        self.z, self.c = lax.div(dp, 2), lax.rem(dp, 2)
        self.y, self.x = lax.div(seq, SIDE), lax.rem(seq, SIDE)
        self.twin = (self.z * 2 + 1 - self.c, seq)

    def neighbour(self, axis, dirn):
        step = 1 if dirn == 0 else SIDE - 1
        if axis == 0:
            return (self.dp, self.y * SIDE + lax.rem(self.x + step, SIDE))
        return (self.dp, lax.rem(self.y + step, SIDE) * SIDE + self.x)

    def along_z(self, d):
        return (lax.rem(self.z + d, NZ) * 2 + self.c, self.seq)

    def line(self):
        return [(self.dp, lax.rem(self.seq + d, BLOCKS)) for d in range(1, BLOCKS)]

    def friends(self):
        return [self.twin] + self.line() + [self.along_z(d) for d in range(1, NZ)]


class Reduction:
    def __init__(self, place, grads, buffers, sems):
        self.place, self.grads = place, grads
        self.acc, self.near, self.far, self.last = buffers
        (
            self.core_send,
            self.core_recv,
            self.near_send,
            self.near_recv,
            self.far_send,
            self.far_recv,
            self.last_send,
            self.last_recv,
        ) = sems

    def lanes(self, part):
        return pl.ds(CUTS[part][0], CUTS[part][1])

    def lanes_of(self, part, core):
        return pl.ds(pl.multiple_of(core * HALF + CUTS[part][0], 128), CUTS[part][1])

    def block(self, part, j, d):
        at = self.place
        if part == 0:
            return j * SIDE + lax.rem(at.x + d, SIDE)
        return lax.rem(at.y + d, SIDE) * SIDE + j

    def core_copy(self, part, b):
        at = self.place
        return remote(
            self.grads.at[b, :, self.lanes_of(part, 1 - at.c)],
            self.acc.at[b, :, self.lanes(part)],
            self.core_send.at[b, part],
            self.core_recv.at[b, part],
            at.twin,
        )

    def near_copy(self, part, dirn, k, b):
        return remote(
            self.acc.at[b, :, self.lanes(part)],
            self.near.at[part, dirn, k, :, pl.ds(0, CUTS[part][1])],
            self.near_send.at[part, dirn, k],
            self.near_recv.at[part, dirn, k],
            self.place.neighbour(part, dirn),
        )

    def far_copy(self, part, dirn, j, b):
        return remote(
            self.acc.at[b, :, self.lanes(part)],
            self.far.at[part, dirn, j, :, pl.ds(0, CUTS[part][1])],
            self.far_send.at[part, dirn, j],
            self.far_recv.at[part, dirn, j],
            self.place.neighbour(part, dirn),
        )

    def last_copy(self, part, d, b):
        at = self.place
        if part == 0:
            to = (at.dp, lax.rem(at.y + d, SIDE) * SIDE + at.x)
        else:
            to = (at.dp, at.y * SIDE + lax.rem(at.x + d, SIDE))
        return remote(
            self.acc.at[b, :, self.lanes(part)],
            self.last.at[part, d, :, pl.ds(0, CUTS[part][1])],
            self.last_send.at[part, d],
            self.last_recv.at[part, d],
            to,
        )

    def gather(self, part, b, *more):
        self.core_copy(part, b).wait_recv()
        lanes = self.lanes(part)
        mine = self.grads[b, :, self.lanes_of(part, self.place.c)]
        self.acc[b, :, lanes] = plus(mine, self.acc[b, :, lanes], *more)

    def start(self):
        for d in (2, 1, 3, 0):

            @pl.loop(0, SIDE)
            def _(j):
                for part in range(2):
                    self.core_copy(part, self.block(part, j, d)).start()

    def first(self):
        for dirn in range(2):

            @pl.loop(0, 2)
            def _(k):
                for part in range(2):
                    b = self.block(part, 2 * dirn + k, 2)
                    self.gather(part, b)
                    self.near_copy(part, dirn, k, b).start()

    def second(self):
        for dirn in range(2):

            @pl.loop(0, 2)
            def _(k):
                for part in range(2):
                    j = 2 * (1 - dirn) + k
                    b = self.block(part, j, 1 + 2 * dirn)
                    self.gather(part, b)
                    self.far_copy(part, dirn, j, b).start()

    def third(self):
        for dirn in range(2):

            @pl.loop(0, 2)
            def _(k):
                for part in range(2):
                    j = 2 * dirn + k
                    b = self.block(part, j, 1 + 2 * dirn)
                    self.near_copy(part, dirn, k, b).wait_recv()
                    self.gather(part, b, self.near[part, dirn, k, :, pl.ds(0, CUTS[part][1])])
                    self.far_copy(part, dirn, j, b).start()

    def finish(self, part, d):
        at = self.place
        b = self.block(1 - part, (at.x, at.y)[part], d)
        j = lax.rem((at.y, at.x)[part] + d, SIDE)
        for dirn in range(2):
            self.far_copy(part, dirn, j, b).wait_recv()
        width = pl.ds(0, CUTS[part][1])
        self.gather(part, b, self.far[part, 0, j, :, width], self.far[part, 1, j, :, width])
        return b

    def fourth(self):
        for d in (2, 1, 3):
            for part in range(2):
                self.last_copy(part, d, self.finish(part, d)).start()

    def fifth(self, final):
        for part in range(2):
            b = self.finish(part, 0)
            total = wide(self.acc[b, :, self.lanes(part)])
            start, width = CUTS[part]
            for d in range(1, SIDE):
                self.last_copy(part, d, b).wait_recv()
                total = total + wide(self.last[part, d, :, pl.ds(0, width)])
            for n in range(0, width, 128):
                final[(start + n) // 128] = total[:, n : n + 128].astype(jnp.bfloat16)

    def settle(self):
        for part in range(2):

            @pl.loop(0, BLOCKS)
            def _(b):
                self.core_copy(part, b).wait_send()

            for dirn in range(2):

                @pl.loop(0, 2)
                def _(k):
                    self.near_copy(part, dirn, k, 0).wait_send()

                @pl.loop(0, SIDE)
                def _(j):
                    self.far_copy(part, dirn, j, 0).wait_send()

            for d in range(1, SIDE):
                self.last_copy(part, d, 0).wait_send()


def reduction_buffers():
    half = jnp.bfloat16
    return [
        pltpu.VMEM((2, 2, 2, 72, 640), half),
        pltpu.VMEM((2, 2, SIDE, 72, 640), half),
        pltpu.VMEM((2, SIDE, 72, 640), half),
    ]


def reduction_sems():
    return [pltpu.SemaphoreType.DMA(counts) for counts in DMA_COUNTS for _ in range(2)]


class Depth:
    def __init__(self, place, final, out, arrived, sems):
        self.place, self.final, self.out = place, final, out
        self.arrived = arrived
        self.up_send, self.up_recv, self.down_send, self.down_recv, self.pair_send, self.pair_recv = sems

    def spot(self, i, core):
        return self.out.at[core, TILES[i][0]]

    def device(self, z):
        return (z * 2 + self.place.c, self.place.seq)

    def up(self, i, z):
        tile, owner, slot = TILES[i]
        return remote(
            self.final.at[tile],
            self.arrived.at[slot, z],
            self.up_send.at[i],
            self.up_recv.at[i, z],
            self.device(owner),
        )

    def down(self, i, z):
        spot = self.spot(i, self.place.c)
        return remote(spot, spot, self.down_send.at[i, z], self.down_recv.at[i], self.device(z))

    def pair(self, i, core):
        spot = self.spot(i, core)
        return remote(spot, spot, self.pair_send.at[i], self.pair_recv.at[i], self.place.twin)

    def owned(self, body):
        for i, (_, owner, _) in enumerate(TILES):
            pl.when(self.place.z == owner)(lambda i=i: body(i))

    def others(self, body):
        for i, (_, owner, _) in enumerate(TILES):
            pl.when(self.place.z != owner)(lambda i=i: body(i))

    def away(self, i):
        return [z for z in range(NZ) if z != TILES[i][1]]

    def start(self):
        self.others(lambda i: self.up(i, self.place.z).start())

    def middle(self):
        def add(i):
            tile, _, slot = TILES[i]
            total = self.final[tile].astype(jnp.float32)
            for z in self.away(i):
                self.up(i, z).wait_recv()
                total = total + self.arrived[slot, z].astype(jnp.float32)
            self.spot(i, self.place.c)[...] = total.astype(jnp.bfloat16)
            for z in self.away(i):
                self.down(i, z).start()
            self.pair(i, self.place.c).start()

        self.owned(add)

    def end(self):
        def forward(i):
            self.down(i, self.place.z).wait_recv()
            self.pair(i, self.place.c).start()

        self.others(forward)
        for i in range(len(TILES)):
            self.pair(i, 1 - self.place.c).wait_recv()

    def settle(self):
        self.others(lambda i: self.up(i, self.place.z).wait_send())

        def left(i):
            for z in self.away(i):
                self.down(i, z).wait_send()

        self.owned(left)
        for i in range(len(TILES)):
            self.pair(i, self.place.c).wait_send()


TILES = tuple((k, k % NZ, k // NZ) for k in range(9))


def depth_sems():
    dma = pltpu.SemaphoreType.DMA
    n = len(TILES)
    return [dma((n,)), dma((n, NZ)), dma((n, NZ)), dma((n,)), dma((n,)), dma((n,))]


NORM_EPS = 1e-06
MASKED = -1e30
ROWS = 320
SPAN = 8
GROUPS = 3
GROUP = SPAN * BLOCKS
SPREAD = GROUPS * GROUP
ODD = 4
D = 1152
INNER = 576
QKV = 1728
UNROLL = 4
NARROW = 640
REST = D - NARROW
SHARP = HEAD_DIM ** (-0.5)
SHARP2 = SHARP * 1.4426950408889634
NN = (((1,), (0,)), ((), ()))
NT = (((1,), (1,)), ((), ()))
TN = (((0,), (0,)), ((), ()))
HALF16 = jnp.bfloat16


def matmul(left, right, dims=NN):
    return lax.dot_general(left, right, dims, preferred_element_type=jnp.float32)


def columns(total, width=256):
    return [(start, min(width, total - start)) for start in range(0, total, width)]


def normalise(source):
    average = jnp.mean(source, axis=-1, keepdims=True)
    centred = source - average
    variance = jnp.mean(centred * centred, axis=-1, keepdims=True)
    spread = lax.rsqrt(variance + NORM_EPS)
    return centred * spread, spread


def modulated(source, mod, first):
    unit, _ = normalise(source)
    return (unit * (1.0 + mod[first + 1]) + mod[first]).astype(HALF16)


def norm_pullback(source, upstream, gain):
    unit, spread = normalise(source)
    grad = upstream * gain
    along = jnp.mean(grad * unit, axis=-1, keepdims=True)
    return spread * (grad - jnp.mean(grad, axis=-1, keepdims=True) - unit * along)


def wide(ref_value):
    return ref_value.astype(jnp.float32)


def project_rows(rows_ref, rows, weight_ref, out_ref, out_rows):
    for start, width in columns(weight_ref.shape[0]):
        cols = slice(start, start + width)
        out_ref[out_rows, cols] = matmul(rows_ref[rows, :], weight_ref[cols, :], NT).astype(HALF16)


def spread_heads(wide_ref, heads_ref, count, rows):
    for i in range(count):
        heads_ref[i, rows] = wide_ref[rows, i * HEAD_DIM : (i + 1) * HEAD_DIM]


def softmax(scores, axis):
    exponent = jnp.exp2((scores - jnp.max(scores, axis=axis, keepdims=True)) * SHARP2)
    return exponent * (1.0 / jnp.sum(exponent, axis=axis, keepdims=True))


def attend_spatial(heads, mixed_heads, rows):
    def body(h, _):
        scores = matmul(heads[h, rows], heads[HEADS + h], NT)
        soft = softmax(scores, -1).astype(HALF16)
        mixed_heads[h, rows] = matmul(soft, heads[2 * HEADS + h]).astype(HALF16)
        return 0

    lax.fori_loop(0, HEADS, body, 0, unroll=UNROLL)


def head_back(queries, keys, values, upstream, bias=None):
    scores = matmul(keys, queries, NT)
    if bias is not None:
        scores = scores + bias
    soft = softmax(scores, 0)
    soft_rounded = soft.astype(HALF16)
    raw = matmul(values, upstream, NT)
    centred = raw - jnp.sum(raw * soft, axis=0, keepdims=True)
    grad_scores = (soft * centred).astype(HALF16)
    grad_values = matmul(soft_rounded, upstream).astype(HALF16)
    grad_keys = (matmul(grad_scores, queries) * SHARP).astype(HALF16)
    grad_queries = (matmul(grad_scores, keys, TN) * SHARP).astype(HALF16)
    return grad_queries, grad_keys, grad_values, soft_rounded


def qkv_blocks(depth, cuts, tall, packed_grads, grads):
    deep = slice(0, depth)
    for start, width in cuts:
        cols = slice(start, start + width)
        product = matmul(tall[:, deep], packed_grads[deep, cols])
        grads[:, :, cols] = product.reshape(BLOCKS, 72, width).astype(HALF16)


def out_blocks(depth, inner_tall, cot, low, high, grads):
    deep = slice(0, depth)
    low[:, deep] = jnp.zeros((D, depth), jnp.float32)
    high[:, deep] = jnp.zeros((D, depth), jnp.float32)
    for s in range(BLOCKS):
        rows = inner_tall[s * 36 : (s + 1) * 36, deep]
        low[s * 72 : s * 72 + 36, deep] = rows
        high[s * 72 + 36 : (s + 1) * 72, deep] = rows
    low_rows, high_rows = low[:, deep].astype(HALF16), high[:, deep].astype(HALF16)
    for start, width in ((0, 192), (192, 192), (384, 192)):
        product = matmul(low_rows, cot[deep, start : start + width]) + matmul(
            high_rows, cot[deep, INNER + start : INNER + start + width]
        )
        grads[:, :, QKV + start : QKV + start + width] = product.reshape(BLOCKS, 72, width).astype(
            HALF16
        )


def transposed(rows_ref, count, tall_ref):
    for start, width in columns(D, 128):
        cols = slice(start, start + width)
        tall_ref[cols, 0:count] = rows_ref[0:count, cols].T


def upstream_of(packed_grads, rows, w_qkv, into, count):
    for n in range(3):
        cols = slice(n * SPREAD, (n + 1) * SPREAD)
        into[n * SPREAD : n * SPREAD + count, :] = matmul(packed_grads[rows, :], w_qkv[:, cols])


def upstream_rows(into, start, count):
    return jnp.concatenate(
        [into[n * SPREAD + start : n * SPREAD + start + count, :] for n in range(3)], axis=-1
    )


def fold_odd(flat, first, step, pad, blocks):
    for i in range(BLOCKS):
        rows = slice(first + i * step, first + i * step + ODD)
        pad[i * SPAN : i * SPAN + ODD, :] = flat[rows, 0:NARROW]
        pad[i * SPAN + ODD : (i + 1) * SPAN, 0:REST] = flat[rows, NARROW:D]
    blocks[...] = pad[...].reshape(BLOCKS, SPAN, NARROW).astype(HALF16)


def unfold_odd(blocks, pad, flat, first, step):
    pad[...] = wide(blocks[...]).reshape(GROUP, NARROW)
    for i in range(BLOCKS):
        rows = slice(first + i * step, first + i * step + ODD)
        flat[rows, 0:NARROW] = pad[i * SPAN : i * SPAN + ODD, :]
        flat[rows, NARROW:D] = pad[i * SPAN + ODD : (i + 1) * SPAN, 0:REST]


def assemble(tiles, tall, qkv, out):
    for k in range(13):
        qkv[:, k * 128 : (k + 1) * 128] = tiles[k // 9, k % 9]
    mixed_tile = tiles[1, 4]
    qkv[:, 1664:QKV] = mixed_tile[:, 0:64]
    rows = slice(0, 72)
    tall[rows, 0:64] = wide(mixed_tile[:, 64:128])
    for k in range(4):
        tall[rows, 64 + k * 128 : 192 + k * 128] = wide(tiles[1, 5 + k])
    out[:, 0:INNER] = tall[0:36, 0:INNER].astype(HALF16)
    out[:, INNER:D] = tall[36:72, 0:INNER].astype(HALF16)


def as_blocks(rows):
    return rows.reshape(BLOCKS, SPAN, D).astype(HALF16)


def kernel(
    lengths,
    mod,
    tokens_far,
    cot_far,
    w_spatial_qkv_far,
    w_spatial_out_far,
    w_temporal_qkv_far,
    w_temporal_out_far,
    grad_tokens,
    spatial_qkv,
    spatial_out,
    temporal_qkv,
    temporal_out,
    tokens,
    cot,
    w_spatial_qkv,
    w_spatial_out,
    w_temporal_qkv,
    w_temporal_out,
    load_sems,
    cot_blocks,
    cot_place,
    resid_blocks,
    resid_place,
    grad_place,
    cot_odd,
    cot_odd_place,
    resid_odd,
    resid_odd_place,
    grad_odd_place,
    pad,
    flat,
    packed,
    heads,
    mixed_heads,
    mixed,
    normed_time,
    packed_time,
    heads_time,
    scaled,
    grad_inner,
    grad_heads,
    out_heads,
    packed_grads,
    inner_tall,
    tall,
    low,
    high,
    bias,
    grads_time,
    grads_space,
    final_time,
    final_space,
    out_time,
    out_space,
    acc_time,
    acc_space,
    *scratch,
):
    at = Place()
    loads = [
        pltpu.make_async_copy(far, near, load_sems.at[i])
        for i, (far, near) in enumerate(
            (
                (cot_far, cot),
                (tokens_far, tokens),
                (w_spatial_qkv_far, w_spatial_qkv),
                (w_spatial_out_far, w_spatial_out),
                (w_temporal_out_far, w_temporal_out),
                (w_temporal_qkv_far, w_temporal_qkv),
            )
        )
    ]
    for load in loads:
        load.start()
    hail(at.friends())

    taken = 0

    def take(count):
        nonlocal taken
        taken += count
        return scratch[taken - count : taken]

    def trips(source, into, odd, odd_into):
        pairs = [(source.at[g], into.at[g]) for g in range(2)] + [(odd, odd_into)]
        return [Exchange(at, left, right, *take(3)) for left, right in pairs]

    cot_trips = trips(cot_blocks, cot_place, cot_odd, cot_odd_place)
    resid_trips = trips(resid_blocks, resid_place, resid_odd, resid_odd_place)
    grad_trips = trips(cot_blocks, grad_place, cot_odd, grad_odd_place)
    one = Reduction(at, grads_time, [acc_time, *take(3)], take(8))
    two = Reduction(at, grads_space, [acc_space, *take(3)], take(8))
    one_z = Depth(at, final_time, out_time, *take(1), take(6))
    two_z = Depth(at, final_space, out_space, *take(1), take(6))

    pad[...] = jnp.zeros_like(pad)
    loads[0].wait()
    for g in range(2):
        cot_blocks[g] = as_blocks(wide(cot[g * GROUP : (g + 1) * GROUP, :]))
    flat[2 * GROUP : ROWS, :] = wide(cot[2 * GROUP : ROWS, :])
    fold_odd(flat, 2 * GROUP, ODD, pad, cot_odd)
    meet(at.friends())
    for trip in cot_trips:
        trip.start()

    every = slice(0, ROWS)
    normed = cot
    loads[1].wait()
    normed[...] = modulated(wide(tokens[...]), mod, 0)
    loads[2].wait()
    project_rows(normed, every, w_spatial_qkv, packed, every)
    spread_heads(packed, heads, 3 * HEADS, every)
    loads[3].wait()

    def residual(first, last):
        rows = slice(first, last)
        attend_spatial(heads, mixed_heads, rows)
        for h in range(HEADS):
            mixed[rows, h * HEAD_DIM : (h + 1) * HEAD_DIM] = mixed_heads[h, rows]
        for start, width in columns(D):
            cols = slice(start, start + width)
            product = matmul(mixed[rows, :], w_spatial_out[:, cols])
            flat[rows, cols] = wide(tokens[rows, cols]) + mod[2][:, cols] * product

    residual(GROUP, ROWS)
    resid_blocks[1] = as_blocks(flat[GROUP : 2 * GROUP, :])
    resid_trips[1].start()
    fold_odd(flat, 2 * GROUP, ODD, pad, resid_odd)
    resid_trips[2].start()
    residual(0, GROUP)
    resid_blocks[0] = as_blocks(flat[0:GROUP, :])
    resid_trips[0].start()

    limit = lengths[0].astype(jnp.float32)

    def frame_of(index):
        return jnp.floor(index * (1.0 / SPAN))

    keys = lax.broadcasted_iota(jnp.int32, (GROUP, 1), 0).astype(jnp.float32)
    queries = lax.broadcasted_iota(jnp.int32, (1, GROUP), 1).astype(jnp.float32)
    same = (keys - SPAN * frame_of(keys)) == (queries - SPAN * frame_of(queries))
    bias[...] = jnp.where(same & (frame_of(keys) < limit), 0.0, MASKED)

    def frames(place, g):
        return wide(place[g]).reshape(GROUP, D)

    def masked_rows(g):
        return jnp.where(frame_of(keys) < limit, 1.0, 0.0) * frames(cot_place, g)

    def settle_odd(trip, odd_place, place):
        trip.arrive()
        flat[0:GROUP, :] = jnp.zeros((GROUP, D), jnp.float32)
        unfold_odd(odd_place, pad, flat, 0, SPAN)
        place[2] = as_blocks(flat[0:GROUP, :])

    for g in range(2):
        cot_trips[g].arrive()
    settle_odd(cot_trips[2], cot_odd_place, cot_place)
    for g in range(GROUPS):
        scaled[g * GROUP : (g + 1) * GROUP, :] = (mod[5] * masked_rows(g)).astype(HALF16)
    loads[4].wait()
    grad_inner[...] = matmul(scaled[...], w_temporal_out[...], NT).astype(HALF16)
    spread_heads(grad_inner, grad_heads, HEADS, slice(0, SPREAD))
    for trip in cot_trips:
        trip.settle()
    loads[5].wait()

    def temporal(members):
        count = len(members) * GROUP
        here, rows = slice(0, count), slice(members[0] * GROUP, members[0] * GROUP + count)
        for g in members:
            if g == 2:
                settle_odd(resid_trips[g], resid_odd_place, resid_place)
            else:
                resid_trips[g].arrive()
            normed_time[g * GROUP : (g + 1) * GROUP, :] = modulated(frames(resid_place, g), mod, 3)
        project_rows(normed_time, rows, w_temporal_qkv, packed_time, here)
        spread_heads(packed_time, heads_time, 3 * HEADS, here)

        def body(h, _):
            inner = pl.ds(pl.multiple_of(h * HEAD_DIM, 8), HEAD_DIM)
            for i, g in enumerate(members):
                part, whole_rows = slice(i * GROUP, (i + 1) * GROUP), slice(g * GROUP, (g + 1) * GROUP)
                values = heads_time[2 * HEADS + h, part]
                grad_queries, grad_keys, grad_values, soft = head_back(
                    heads_time[h, part],
                    heads_time[HEADS + h, part],
                    values,
                    grad_heads[h, whole_rows],
                    bias[...],
                )
                inner_tall[inner, whole_rows] = matmul(values, soft, TN)
                out_heads[h, part] = grad_queries
                out_heads[HEADS + h, part] = grad_keys
                out_heads[2 * HEADS + h, part] = grad_values
            return 0

        lax.fori_loop(0, HEADS, body, 0, unroll=UNROLL)
        for i in range(3 * HEADS):
            packed_grads[rows, i * HEAD_DIM : (i + 1) * HEAD_DIM] = out_heads[i, here]
        upstream_of(packed_grads, rows, w_temporal_qkv, low, count)
        for i, g in enumerate(members):
            total = masked_rows(g) + norm_pullback(
                frames(resid_place, g), upstream_rows(low, i * GROUP, GROUP), 1.0 + mod[4]
            )
            if g == 2:
                flat[0:GROUP, :] = total
                fold_odd(flat, 0, SPAN, pad, cot_odd)
            else:
                cot_blocks[g] = as_blocks(total)
            grad_trips[g].start()

    temporal((1, 2))
    temporal((0,))
    transposed(normed_time, SPREAD, tall)
    qkv_blocks(SPREAD, columns(QKV), tall, packed_grads, grads_time)
    out_blocks(SPREAD, inner_tall, scaled, low, high, grads_time)
    one.start()

    transposed(normed, ROWS, tall)
    inner_tall[:, every] = wide(mixed[...]).T
    for g in (1, 2, 0):
        grad_trips[g].arrive()
    unfold_odd(grad_odd_place, pad, flat, 2 * GROUP, ODD)
    for g in range(2):
        flat[g * GROUP : (g + 1) * GROUP, :] = frames(grad_place, g)
    scaled[every, :] = (mod[2] * flat[...]).astype(HALF16)
    grad_inner[every, :] = matmul(scaled[every, :], w_spatial_out[...], NT).astype(HALF16)
    spread_heads(grad_inner, grad_heads, HEADS, every)
    one.first()
    one.second()
    out_blocks(ROWS, inner_tall, scaled, low, high, grads_space)

    def attend_back(h, _):
        grad_queries, grad_keys, grad_values, _ = head_back(
            heads[h], heads[HEADS + h], heads[2 * HEADS + h], grad_heads[h, every]
        )
        out_heads[h] = grad_queries
        out_heads[HEADS + h] = grad_keys
        out_heads[2 * HEADS + h] = grad_values
        return 0

    lax.fori_loop(0, HEADS, attend_back, 0, unroll=UNROLL)
    one.third()
    for i in range(3 * HEADS):
        packed_grads[every, i * HEAD_DIM : (i + 1) * HEAD_DIM] = out_heads[i]
    qkv_blocks(ROWS, columns(QKV), tall, packed_grads, grads_space)
    two.start()
    upstream_of(packed_grads, every, w_spatial_qkv, low, ROWS)
    one.fourth()
    two.first()
    two.second()
    grad_tokens[...] = (
        flat[...]
        + norm_pullback(wide(tokens[...]), upstream_rows(low, 0, ROWS), 1.0 + mod[1])
    ).astype(HALF16)
    one.fifth(final_time)
    one_z.start()
    two.third()
    one_z.middle()
    two.fourth()
    one_z.end()
    two.fifth(final_space)
    two_z.start()
    assemble(out_time, pad, temporal_qkv, temporal_out)
    two_z.middle()
    two_z.end()
    assemble(out_space, pad, spatial_qkv, spatial_out)
    for user in resid_trips + grad_trips + [one, two, one_z, two_z]:
        user.settle()


def vmem(shape, dtype=HALF16):
    return pltpu.VMEM(shape, dtype)


def run(lengths, mod, tokens, cotangent, w_spatial_qkv, w_spatial_out, w_temporal_qkv, w_temporal_out):
    full = jnp.float32
    sent, place, odd = vmem((2, BLOCKS, SPAN, D)), vmem((GROUPS, BLOCKS, SPAN, D)), vmem((BLOCKS, SPAN, NARROW))
    scratch = [
        vmem((ROWS, D)),
        vmem((ROWS, D)),
        vmem((QKV, D)),
        vmem((INNER, D)),
        vmem((QKV, D)),
        vmem((INNER, D)),
        pltpu.SemaphoreType.DMA((6,)),
        sent,
        place,
        sent,
        place,
        sent,
        odd,
        odd,
        odd,
        odd,
        odd,
        vmem((GROUP, NARROW), full),
        vmem((ROWS, D), full),
        vmem((ROWS, QKV)),
        vmem((3 * HEADS, ROWS, HEAD_DIM)),
        vmem((HEADS, ROWS, HEAD_DIM)),
        vmem((ROWS, INNER)),
        vmem((SPREAD, D)),
        vmem((2 * GROUP, QKV)),
        vmem((3 * HEADS, 2 * GROUP, HEAD_DIM)),
        vmem((SPREAD, D)),
        vmem((SPREAD, INNER)),
        vmem((HEADS, SPREAD, HEAD_DIM)),
        vmem((3 * HEADS, ROWS, HEAD_DIM)),
        vmem((SPREAD, QKV)),
        vmem((INNER, SPREAD), full),
        vmem((D, SPREAD)),
        vmem((D, SPREAD), full),
        vmem((D, SPREAD), full),
        vmem((GROUP, GROUP), full),
        vmem((BLOCKS, 72, WIDE)),
        vmem((BLOCKS, 72, WIDE)),
        vmem((9, 72, 128)),
        vmem((9, 72, 128)),
        vmem((2, 9, 72, 128)),
        vmem((2, 9, 72, 128)),
        vmem((BLOCKS, 72, HALF)),
        vmem((BLOCKS, 72, HALF)),
    ]
    for _ in range(3 * GROUPS):
        scratch += exchange_sems()
    for _ in range(2):
        scratch += reduction_buffers() + reduction_sems()
    for _ in range(2):
        scratch += [vmem((2, NZ, 72, 128))] + depth_sems()
    return pl.pallas_call(
        kernel,
        out_shape=(
            jax.ShapeDtypeStruct((ROWS, D), HALF16),
            jax.ShapeDtypeStruct((72, QKV), HALF16),
            jax.ShapeDtypeStruct((36, D), HALF16),
            jax.ShapeDtypeStruct((72, QKV), HALF16),
            jax.ShapeDtypeStruct((36, D), HALF16),
        ),
        in_specs=[pl.BlockSpec(memory_space=pltpu.SMEM), pl.BlockSpec(memory_space=pltpu.VMEM)]
        + [pl.BlockSpec(memory_space=pl.ANY)] * 6,
        out_specs=(pl.BlockSpec(memory_space=pltpu.VMEM),) * 5,
        scratch_shapes=scratch,
        compiler_params=pltpu.CompilerParams(
            collective_id=0, has_side_effects=True, vmem_limit_bytes=VMEM_LIMIT
        ),
    )(lengths, mod, tokens, cotangent, w_spatial_qkv, w_spatial_out, w_temporal_qkv, w_temporal_out)


def local(
    tokens,
    cotangent,
    modulation,
    lengths,
    w_spatial_qkv,
    w_spatial_out,
    w_temporal_qkv,
    w_temporal_out,
):
    grad_tokens, *weights = run(
        lengths,
        modulation.reshape(6, 1, D),
        tokens.reshape(ROWS, D),
        cotangent.reshape(ROWS, D),
        w_spatial_qkv.T,
        w_spatial_out,
        w_temporal_qkv.T,
        w_temporal_out,
    )
    return (grad_tokens.reshape(tokens.shape), *weights)


def solution(mesh):
    placed = (
        P("dp", "seq", None, None),
        P("dp", "seq", None, None),
        P("dp", None, None),
        P("dp"),
        P(),
        P(),
        P(),
        P(),
    )
    return jax.shard_map(
        local,
        mesh=mesh,
        in_specs=placed,
        out_specs=(
            P("dp", "seq", None, None),
            P("seq", None),
            P("seq", None),
            P("seq", None),
            P("seq", None),
        ),
        check_vma=False,
    )
```

```python
import jax
import jax.numpy as jnp
from jax import lax
from jax.experimental import pallas as pl
from jax.experimental.pallas import tpu as pltpu
from jax.sharding import PartitionSpec as P

HEADS = 8
HEAD_DIM = 72
F = 16
SIDE = 4
NZ = 8
BLOCKS = 16
WIDE = 2304
HALF = 1152
VMEM_LIMIT = 63 * 1024 * 1024


def remote(src, dst, send, recv, device):
    return pltpu.make_async_remote_copy(
        src_ref=src,
        dst_ref=dst,
        send_sem=send,
        recv_sem=recv,
        device_id=device,
        device_id_type=pl.DeviceIdType.MESH,
    )


def hail(devices):
    barrier = pltpu.get_barrier_semaphore()
    for device in devices:
        pl.semaphore_signal(barrier, inc=1, device_id=device, device_id_type=pl.DeviceIdType.MESH)


def meet(devices):
    pl.semaphore_wait(pltpu.get_barrier_semaphore(), len(devices))


class Exchange:
    def __init__(self, place, source, into, own_sem, send_sems, recv_sems):
        self.place, self.source, self.into = place, source, into
        self.own_sem, self.send_sems, self.recv_sems = own_sem, send_sems, recv_sems

    def to(self, d):
        return lax.rem(self.place.seq + d, BLOCKS)

    def copy(self, d):
        at = self.place
        return remote(
            self.source.at[self.to(d)],
            self.into.at[at.seq],
            self.send_sems.at[d],
            self.recv_sems.at[d],
            (at.dp, self.to(d)),
        )

    def own(self):
        me = self.place.seq
        return pltpu.make_async_copy(self.source.at[me], self.into.at[me], self.own_sem)

    def start(self):
        self.own().start()
        for d in range(1, BLOCKS):
            self.copy(d).start()

    def arrive(self):
        at = self.place
        for d in range(1, BLOCKS):
            origin = lax.rem(at.seq + BLOCKS - d, BLOCKS)
            remote(
                self.source.at[origin],
                self.into.at[origin],
                self.send_sems.at[d],
                self.recv_sems.at[d],
                (at.dp, origin),
            ).wait_recv()
        self.own().wait()

    def settle(self):
        for d in range(1, BLOCKS):
            self.copy(d).wait_send()


def exchange_sems():
    dma = pltpu.SemaphoreType.DMA
    return [dma, dma((BLOCKS,)), dma((BLOCKS,))]


def plus(*refs):
    total = refs[0].astype(jnp.float32)
    for ref in refs[1:]:
        total = total + ref.astype(jnp.float32)
    return total.astype(jnp.bfloat16)


CUTS = ((0, 640), (640, 512))
DMA_COUNTS = (
    (BLOCKS, 2),
    (2, 2, 2),
    (2, 2, SIDE),
    (2, SIDE),
)


class Place:
    def __init__(self):
        dp, seq = lax.axis_index("dp"), lax.axis_index("seq")
        self.dp, self.seq = dp, seq
        self.z, self.c = lax.div(dp, 2), lax.rem(dp, 2)
        self.y, self.x = lax.div(seq, SIDE), lax.rem(seq, SIDE)
        self.twin = (self.z * 2 + 1 - self.c, seq)

    def neighbour(self, axis, dirn):
        step = 1 if dirn == 0 else SIDE - 1
        if axis == 0:
            return (self.dp, self.y * SIDE + lax.rem(self.x + step, SIDE))
        return (self.dp, lax.rem(self.y + step, SIDE) * SIDE + self.x)

    def along_z(self, d):
        return (lax.rem(self.z + d, NZ) * 2 + self.c, self.seq)

    def line(self):
        return [(self.dp, lax.rem(self.seq + d, BLOCKS)) for d in range(1, BLOCKS)]

    def friends(self):
        return [self.twin] + self.line() + [self.along_z(d) for d in range(1, NZ)]


class Reduction:
    def __init__(self, place, grads, buffers, sems):
        self.place, self.grads = place, grads
        self.acc, self.near, self.far, self.last = buffers
        (
            self.core_send,
            self.core_recv,
            self.near_send,
            self.near_recv,
            self.far_send,
            self.far_recv,
            self.last_send,
            self.last_recv,
        ) = sems

    def lanes(self, part):
        return pl.ds(CUTS[part][0], CUTS[part][1])

    def lanes_of(self, part, core):
        return pl.ds(pl.multiple_of(core * HALF + CUTS[part][0], 128), CUTS[part][1])

    def block(self, part, j, d):
        at = self.place
        if part == 0:
            return j * SIDE + lax.rem(at.x + d, SIDE)
        return lax.rem(at.y + d, SIDE) * SIDE + j

    def core_copy(self, part, b):
        at = self.place
        return remote(
            self.grads.at[b, :, self.lanes_of(part, 1 - at.c)],
            self.acc.at[b, :, self.lanes(part)],
            self.core_send.at[b, part],
            self.core_recv.at[b, part],
            at.twin,
        )

    def near_copy(self, part, dirn, k, b):
        return remote(
            self.acc.at[b, :, self.lanes(part)],
            self.near.at[part, dirn, k, :, pl.ds(0, CUTS[part][1])],
            self.near_send.at[part, dirn, k],
            self.near_recv.at[part, dirn, k],
            self.place.neighbour(part, dirn),
        )

    def far_copy(self, part, dirn, j, b):
        return remote(
            self.acc.at[b, :, self.lanes(part)],
            self.far.at[part, dirn, j, :, pl.ds(0, CUTS[part][1])],
            self.far_send.at[part, dirn, j],
            self.far_recv.at[part, dirn, j],
            self.place.neighbour(part, dirn),
        )

    def last_copy(self, part, d, b):
        at = self.place
        if part == 0:
            to = (at.dp, lax.rem(at.y + d, SIDE) * SIDE + at.x)
        else:
            to = (at.dp, at.y * SIDE + lax.rem(at.x + d, SIDE))
        return remote(
            self.acc.at[b, :, self.lanes(part)],
            self.last.at[part, d, :, pl.ds(0, CUTS[part][1])],
            self.last_send.at[part, d],
            self.last_recv.at[part, d],
            to,
        )

    def gather(self, part, b, *more):
        self.core_copy(part, b).wait_recv()
        lanes = self.lanes(part)
        mine = self.grads[b, :, self.lanes_of(part, self.place.c)]
        self.acc[b, :, lanes] = plus(mine, self.acc[b, :, lanes], *more)

    def start(self):
        for d in (2, 1, 3, 0):

            @pl.loop(0, SIDE)
            def _(j):
                for part in range(2):
                    self.core_copy(part, self.block(part, j, d)).start()

    def first(self):
        for dirn in range(2):

            @pl.loop(0, 2)
            def _(k):
                for part in range(2):
                    b = self.block(part, 2 * dirn + k, 2)
                    self.gather(part, b)
                    self.near_copy(part, dirn, k, b).start()

    def second(self):
        for dirn in range(2):

            @pl.loop(0, 2)
            def _(k):
                for part in range(2):
                    j = 2 * (1 - dirn) + k
                    b = self.block(part, j, 1 + 2 * dirn)
                    self.gather(part, b)
                    self.far_copy(part, dirn, j, b).start()

    def third(self):
        for dirn in range(2):

            @pl.loop(0, 2)
            def _(k):
                for part in range(2):
                    j = 2 * dirn + k
                    b = self.block(part, j, 1 + 2 * dirn)
                    self.near_copy(part, dirn, k, b).wait_recv()
                    self.gather(part, b, self.near[part, dirn, k, :, pl.ds(0, CUTS[part][1])])
                    self.far_copy(part, dirn, j, b).start()

    def finish(self, part, d):
        at = self.place
        b = self.block(1 - part, (at.x, at.y)[part], d)
        j = lax.rem((at.y, at.x)[part] + d, SIDE)
        for dirn in range(2):
            self.far_copy(part, dirn, j, b).wait_recv()
        width = pl.ds(0, CUTS[part][1])
        self.gather(part, b, self.far[part, 0, j, :, width], self.far[part, 1, j, :, width])
        return b

    def fourth(self):
        for d in (2, 1, 3):
            for part in range(2):
                self.last_copy(part, d, self.finish(part, d)).start()

    def fifth(self, final):
        for part in range(2):
            b = self.finish(part, 0)
            total = wide(self.acc[b, :, self.lanes(part)])
            start, width = CUTS[part]
            for d in range(1, SIDE):
                self.last_copy(part, d, b).wait_recv()
                total = total + wide(self.last[part, d, :, pl.ds(0, width)])
            for n in range(0, width, 128):
                final[(start + n) // 128] = total[:, n : n + 128].astype(jnp.bfloat16)

    def settle(self):
        for part in range(2):

            @pl.loop(0, BLOCKS)
            def _(b):
                self.core_copy(part, b).wait_send()

            for dirn in range(2):

                @pl.loop(0, 2)
                def _(k):
                    self.near_copy(part, dirn, k, 0).wait_send()

                @pl.loop(0, SIDE)
                def _(j):
                    self.far_copy(part, dirn, j, 0).wait_send()

            for d in range(1, SIDE):
                self.last_copy(part, d, 0).wait_send()


def reduction_buffers():
    half = jnp.bfloat16
    return [
        pltpu.VMEM((2, 2, 2, 72, 640), half),
        pltpu.VMEM((2, 2, SIDE, 72, 640), half),
        pltpu.VMEM((2, SIDE, 72, 640), half),
    ]


def reduction_sems():
    return [pltpu.SemaphoreType.DMA(counts) for counts in DMA_COUNTS for _ in range(2)]


class Depth:
    def __init__(self, place, final, out, arrived, sems):
        self.place, self.final, self.out = place, final, out
        self.arrived = arrived
        self.up_send, self.up_recv, self.down_send, self.down_recv, self.pair_send, self.pair_recv = sems

    def spot(self, i, core):
        return self.out.at[core, TILES[i][0]]

    def device(self, z):
        return (z * 2 + self.place.c, self.place.seq)

    def up(self, i, z):
        tile, owner, slot = TILES[i]
        return remote(
            self.final.at[tile],
            self.arrived.at[slot, z],
            self.up_send.at[i],
            self.up_recv.at[i, z],
            self.device(owner),
        )

    def down(self, i, z):
        spot = self.spot(i, self.place.c)
        return remote(spot, spot, self.down_send.at[i, z], self.down_recv.at[i], self.device(z))

    def pair(self, i, core):
        spot = self.spot(i, core)
        return remote(spot, spot, self.pair_send.at[i], self.pair_recv.at[i], self.place.twin)

    def owned(self, body):
        for i, (_, owner, _) in enumerate(TILES):
            pl.when(self.place.z == owner)(lambda i=i: body(i))

    def others(self, body):
        for i, (_, owner, _) in enumerate(TILES):
            pl.when(self.place.z != owner)(lambda i=i: body(i))

    def away(self, i):
        return [z for z in range(NZ) if z != TILES[i][1]]

    def start(self):
        self.others(lambda i: self.up(i, self.place.z).start())

    def middle(self):
        def add(i):
            tile, _, slot = TILES[i]
            total = self.final[tile].astype(jnp.float32)
            for z in self.away(i):
                self.up(i, z).wait_recv()
                total = total + self.arrived[slot, z].astype(jnp.float32)
            self.spot(i, self.place.c)[...] = total.astype(jnp.bfloat16)
            for z in self.away(i):
                self.down(i, z).start()
            self.pair(i, self.place.c).start()

        self.owned(add)

    def end(self):
        def forward(i):
            self.down(i, self.place.z).wait_recv()
            self.pair(i, self.place.c).start()

        self.others(forward)
        for i in range(len(TILES)):
            self.pair(i, 1 - self.place.c).wait_recv()

    def settle(self):
        self.others(lambda i: self.up(i, self.place.z).wait_send())

        def left(i):
            for z in self.away(i):
                self.down(i, z).wait_send()

        self.owned(left)
        for i in range(len(TILES)):
            self.pair(i, self.place.c).wait_send()


TILES = tuple((k, k % NZ, k // NZ) for k in range(9))


def depth_sems():
    dma = pltpu.SemaphoreType.DMA
    n = len(TILES)
    return [dma((n,)), dma((n, NZ)), dma((n, NZ)), dma((n,)), dma((n,)), dma((n,))]


NORM_EPS = 1e-06
MASKED = -1e30
ROWS = 320
SPAN = 8
GROUPS = 3
GROUP = SPAN * BLOCKS
SPREAD = GROUPS * GROUP
ODD = 4
D = 1152
INNER = 576
QKV = 1728
UNROLL = 2
NARROW = 640
REST = D - NARROW
SHARP = HEAD_DIM ** (-0.5)
SHARP2 = SHARP * 1.4426950408889634
NN = (((1,), (0,)), ((), ()))
NT = (((1,), (1,)), ((), ()))
TN = (((0,), (0,)), ((), ()))
HALF16 = jnp.bfloat16


def matmul(left, right, dims=NN):
    return lax.dot_general(left, right, dims, preferred_element_type=jnp.float32)


def columns(total, width=256):
    return [(start, min(width, total - start)) for start in range(0, total, width)]


def normalise(source):
    average = jnp.mean(source, axis=-1, keepdims=True)
    centred = source - average
    variance = jnp.mean(centred * centred, axis=-1, keepdims=True)
    spread = lax.rsqrt(variance + NORM_EPS)
    return centred * spread, spread


def modulated(source, mod, first):
    unit, _ = normalise(source)
    return (unit * (1.0 + mod[first + 1]) + mod[first]).astype(HALF16)


def norm_pullback(source, upstream, gain):
    unit, spread = normalise(source)
    grad = upstream * gain
    along = jnp.mean(grad * unit, axis=-1, keepdims=True)
    return spread * (grad - jnp.mean(grad, axis=-1, keepdims=True) - unit * along)


def wide(ref_value):
    return ref_value.astype(jnp.float32)


def by_columns(total, width, body):
    even = total // width * width

    @pl.loop(0, even, step=width)
    def _(start):
        body(pl.multiple_of(start, width), width)

    if even < total:
        body(even, total - even)


def project_rows(rows_ref, rows, weight_ref, out_ref, out_rows):
    def body(start, width):
        cols = pl.ds(start, width)
        out_ref[out_rows, cols] = matmul(rows_ref[rows, :], weight_ref[cols, :], NT).astype(HALF16)

    by_columns(weight_ref.shape[0], 512, body)


def spread_heads(wide_ref, heads_ref, count, rows):
    for i in range(count):
        heads_ref[i, rows] = wide_ref[rows, i * HEAD_DIM : (i + 1) * HEAD_DIM]


def softmax(scores, axis):
    exponent = jnp.exp2((scores - jnp.max(scores, axis=axis, keepdims=True)) * SHARP2)
    return exponent * (1.0 / jnp.sum(exponent, axis=axis, keepdims=True))


def attend_spatial(heads, mixed_heads, rows):
    def body(h, _):
        scores = matmul(heads[h, rows], heads[HEADS + h], NT)
        soft = softmax(scores, -1).astype(HALF16)
        mixed_heads[h, rows] = matmul(soft, heads[2 * HEADS + h]).astype(HALF16)
        return 0

    lax.fori_loop(0, HEADS, body, 0, unroll=UNROLL)


def head_back(queries, keys, values, upstream, bias=None):
    scores = matmul(keys, queries, NT)
    if bias is not None:
        scores = scores + bias
    soft = softmax(scores, 0)
    soft_rounded = soft.astype(HALF16)
    raw = matmul(values, upstream, NT)
    centred = raw - jnp.sum(raw * soft, axis=0, keepdims=True)
    grad_scores = (soft * centred).astype(HALF16)
    grad_values = matmul(soft_rounded, upstream).astype(HALF16)
    grad_keys = (matmul(grad_scores, queries) * SHARP).astype(HALF16)
    grad_queries = (matmul(grad_scores, keys, TN) * SHARP).astype(HALF16)
    return grad_queries, grad_keys, grad_values, soft_rounded


def qkv_blocks(depth, tall, packed_grads, grads):
    deep = slice(0, depth)

    def body(start, width):
        cols = pl.ds(start, width)
        product = matmul(tall[:, deep], packed_grads[deep, cols])
        grads[:, :, cols] = product.reshape(BLOCKS, 72, width).astype(HALF16)

    by_columns(QKV, 256, body)


def out_blocks(depth, inner_tall, cot, low, high, grads):
    deep = slice(0, depth)
    low[:, deep] = jnp.zeros((D, depth), jnp.float32)
    high[:, deep] = jnp.zeros((D, depth), jnp.float32)
    for s in range(BLOCKS):
        rows = inner_tall[s * 36 : (s + 1) * 36, deep]
        low[s * 72 : s * 72 + 36, deep] = rows
        high[s * 72 + 36 : (s + 1) * 72, deep] = rows
    low_rows, high_rows = low[:, deep].astype(HALF16), high[:, deep].astype(HALF16)
    for start, width in ((0, 192), (192, 192), (384, 192)):
        product = matmul(low_rows, cot[deep, start : start + width]) + matmul(
            high_rows, cot[deep, INNER + start : INNER + start + width]
        )
        grads[:, :, QKV + start : QKV + start + width] = product.reshape(BLOCKS, 72, width).astype(
            HALF16
        )


def transposed(rows_ref, count, tall_ref):
    for start, width in columns(D, 128):
        cols = slice(start, start + width)
        tall_ref[cols, 0:count] = rows_ref[0:count, cols].T


def upstream_of(packed_grads, rows, w_qkv, into, count):
    def body(start, width):
        into[pl.ds(start, count), :] = matmul(packed_grads[rows, :], w_qkv[:, pl.ds(start, width)])

    by_columns(D, SPREAD, body)


def upstream_rows(into, start, count):
    return jnp.concatenate(
        [into[n * SPREAD + start : n * SPREAD + start + count, :] for n in range(3)], axis=-1
    )


def fold_odd(flat, first, step, pad, blocks):
    for i in range(BLOCKS):
        rows = slice(first + i * step, first + i * step + ODD)
        pad[i * SPAN : i * SPAN + ODD, :] = flat[rows, 0:NARROW]
        pad[i * SPAN + ODD : (i + 1) * SPAN, 0:REST] = flat[rows, NARROW:D]
    blocks[...] = pad[...].reshape(BLOCKS, SPAN, NARROW).astype(HALF16)


def unfold_odd(blocks, pad, flat, first, step):
    pad[...] = wide(blocks[...]).reshape(GROUP, NARROW)
    for i in range(BLOCKS):
        rows = slice(first + i * step, first + i * step + ODD)
        flat[rows, 0:NARROW] = pad[i * SPAN : i * SPAN + ODD, :]
        flat[rows, NARROW:D] = pad[i * SPAN + ODD : (i + 1) * SPAN, 0:REST]


def assemble(tiles, summed, start):
    for k in range(18):
        summed[:, start + k * 128 : start + (k + 1) * 128] = tiles[k // 9, k % 9]


def as_blocks(rows):
    return rows.reshape(BLOCKS, SPAN, D).astype(HALF16)


def kernel(
    lengths,
    mod,
    tokens_far,
    cot_far,
    w_spatial_qkv_far,
    w_spatial_out_far,
    w_temporal_qkv_far,
    w_temporal_out_far,
    grad_tokens,
    summed,
    tokens,
    cot,
    w_spatial_qkv,
    w_spatial_out,
    w_temporal_qkv,
    w_temporal_out,
    load_sems,
    cot_blocks,
    cot_place,
    resid_blocks,
    resid_place,
    grad_place,
    cot_odd,
    cot_odd_place,
    resid_odd,
    resid_odd_place,
    grad_odd_place,
    pad,
    flat,
    packed,
    heads,
    mixed_heads,
    mixed,
    normed_time,
    packed_time,
    heads_time,
    scaled,
    grad_inner,
    grad_heads,
    out_heads,
    packed_grads,
    inner_tall,
    tall,
    low,
    high,
    bias,
    grads_time,
    grads_space,
    final_time,
    final_space,
    out_time,
    out_space,
    acc_time,
    acc_space,
    *scratch,
):
    at = Place()
    loads = [
        pltpu.make_async_copy(far, near, load_sems.at[i])
        for i, (far, near) in enumerate(
            (
                (cot_far, cot),
                (tokens_far, tokens),
                (w_spatial_qkv_far, w_spatial_qkv),
                (w_spatial_out_far, w_spatial_out),
                (w_temporal_out_far, w_temporal_out),
                (w_temporal_qkv_far, w_temporal_qkv),
            )
        )
    ]
    for load in loads:
        load.start()
    hail(at.friends())

    taken = 0

    def take(count):
        nonlocal taken
        taken += count
        return scratch[taken - count : taken]

    def trips(source, into, odd, odd_into):
        pairs = [(source.at[g], into.at[g]) for g in range(2)] + [(odd, odd_into)]
        return [Exchange(at, left, right, *take(3)) for left, right in pairs]

    cot_trips = trips(cot_blocks, cot_place, cot_odd, cot_odd_place)
    resid_trips = trips(resid_blocks, resid_place, resid_odd, resid_odd_place)
    grad_trips = trips(cot_blocks, grad_place, cot_odd, grad_odd_place)
    one = Reduction(at, grads_time, [acc_time, *take(3)], take(8))
    two = Reduction(at, grads_space, [acc_space, *take(3)], take(8))
    one_z = Depth(at, final_time, out_time, *take(1), take(6))
    two_z = Depth(at, final_space, out_space, *take(1), take(6))

    pad[...] = jnp.zeros_like(pad)
    loads[0].wait()
    for g in range(2):
        cot_blocks[g] = as_blocks(wide(cot[g * GROUP : (g + 1) * GROUP, :]))
    flat[2 * GROUP : ROWS, :] = wide(cot[2 * GROUP : ROWS, :])
    fold_odd(flat, 2 * GROUP, ODD, pad, cot_odd)
    meet(at.friends())
    for trip in cot_trips:
        trip.start()

    every = slice(0, ROWS)
    normed = cot
    loads[1].wait()
    normed[...] = modulated(wide(tokens[...]), mod, 0)
    loads[2].wait()
    project_rows(normed, every, w_spatial_qkv, packed, every)
    spread_heads(packed, heads, 3 * HEADS, every)
    loads[3].wait()

    def residual(first, last):
        rows = slice(first, last)
        attend_spatial(heads, mixed_heads, rows)
        for h in range(HEADS):
            mixed[rows, h * HEAD_DIM : (h + 1) * HEAD_DIM] = mixed_heads[h, rows]
        for start, width in columns(D):
            cols = slice(start, start + width)
            product = matmul(mixed[rows, :], w_spatial_out[:, cols])
            flat[rows, cols] = wide(tokens[rows, cols]) + mod[2][:, cols] * product

    residual(GROUP, ROWS)
    resid_blocks[1] = as_blocks(flat[GROUP : 2 * GROUP, :])
    resid_trips[1].start()
    fold_odd(flat, 2 * GROUP, ODD, pad, resid_odd)
    resid_trips[2].start()
    residual(0, GROUP)
    resid_blocks[0] = as_blocks(flat[0:GROUP, :])
    resid_trips[0].start()

    limit = lengths[0].astype(jnp.float32)

    def frame_of(index):
        return jnp.floor(index * (1.0 / SPAN))

    keys = lax.broadcasted_iota(jnp.int32, (GROUP, 1), 0).astype(jnp.float32)
    queries = lax.broadcasted_iota(jnp.int32, (1, GROUP), 1).astype(jnp.float32)
    same = (keys - SPAN * frame_of(keys)) == (queries - SPAN * frame_of(queries))
    bias[...] = jnp.where(same & (frame_of(keys) < limit), 0.0, MASKED)

    def frames(place, g):
        return wide(place[g]).reshape(GROUP, D)

    def masked_rows(g):
        return jnp.where(frame_of(keys) < limit, 1.0, 0.0) * frames(cot_place, g)

    def settle_odd(trip, odd_place, place):
        trip.arrive()
        flat[0:GROUP, :] = jnp.zeros((GROUP, D), jnp.float32)
        unfold_odd(odd_place, pad, flat, 0, SPAN)
        place[2] = as_blocks(flat[0:GROUP, :])

    for g in range(2):
        cot_trips[g].arrive()
    settle_odd(cot_trips[2], cot_odd_place, cot_place)
    for g in range(GROUPS):
        scaled[g * GROUP : (g + 1) * GROUP, :] = (mod[5] * masked_rows(g)).astype(HALF16)
    loads[4].wait()
    grad_inner[...] = matmul(scaled[...], w_temporal_out[...], NT).astype(HALF16)
    spread_heads(grad_inner, grad_heads, HEADS, slice(0, SPREAD))
    for trip in cot_trips:
        trip.settle()
    loads[5].wait()

    def temporal(members):
        count = len(members) * GROUP
        here, rows = slice(0, count), slice(members[0] * GROUP, members[0] * GROUP + count)
        for g in members:
            if g == 2:
                settle_odd(resid_trips[g], resid_odd_place, resid_place)
            else:
                resid_trips[g].arrive()
            normed_time[g * GROUP : (g + 1) * GROUP, :] = modulated(frames(resid_place, g), mod, 3)
        project_rows(normed_time, rows, w_temporal_qkv, packed_time, here)
        spread_heads(packed_time, heads_time, 3 * HEADS, here)

        def body(h, _):
            inner = pl.ds(pl.multiple_of(h * HEAD_DIM, 8), HEAD_DIM)
            for i, g in enumerate(members):
                part, whole_rows = slice(i * GROUP, (i + 1) * GROUP), slice(g * GROUP, (g + 1) * GROUP)
                values = heads_time[2 * HEADS + h, part]
                grad_queries, grad_keys, grad_values, soft = head_back(
                    heads_time[h, part],
                    heads_time[HEADS + h, part],
                    values,
                    grad_heads[h, whole_rows],
                    bias[...],
                )
                inner_tall[inner, whole_rows] = matmul(values, soft, TN)
                out_heads[h, part] = grad_queries
                out_heads[HEADS + h, part] = grad_keys
                out_heads[2 * HEADS + h, part] = grad_values
            return 0

        lax.fori_loop(0, HEADS, body, 0, unroll=UNROLL)
        for i in range(3 * HEADS):
            packed_grads[rows, i * HEAD_DIM : (i + 1) * HEAD_DIM] = out_heads[i, here]
        upstream_of(packed_grads, rows, w_temporal_qkv, low, count)
        for i, g in enumerate(members):
            total = masked_rows(g) + norm_pullback(
                frames(resid_place, g), upstream_rows(low, i * GROUP, GROUP), 1.0 + mod[4]
            )
            if g == 2:
                flat[0:GROUP, :] = total
                fold_odd(flat, 0, SPAN, pad, cot_odd)
            else:
                cot_blocks[g] = as_blocks(total)
            grad_trips[g].start()

    temporal((1, 2))
    temporal((0,))
    transposed(normed_time, SPREAD, tall)
    qkv_blocks(SPREAD, tall, packed_grads, grads_time)
    out_blocks(SPREAD, inner_tall, scaled, low, high, grads_time)
    one.start()

    transposed(normed, ROWS, tall)
    inner_tall[:, every] = wide(mixed[...]).T
    for g in (1, 2, 0):
        grad_trips[g].arrive()
    unfold_odd(grad_odd_place, pad, flat, 2 * GROUP, ODD)
    for g in range(2):
        flat[g * GROUP : (g + 1) * GROUP, :] = frames(grad_place, g)
    scaled[every, :] = (mod[2] * flat[...]).astype(HALF16)
    grad_inner[every, :] = matmul(scaled[every, :], w_spatial_out[...], NT).astype(HALF16)
    spread_heads(grad_inner, grad_heads, HEADS, every)
    one.first()
    one.second()
    out_blocks(ROWS, inner_tall, scaled, low, high, grads_space)

    def attend_back(h, _):
        grad_queries, grad_keys, grad_values, _ = head_back(
            heads[h], heads[HEADS + h], heads[2 * HEADS + h], grad_heads[h, every]
        )
        out_heads[h] = grad_queries
        out_heads[HEADS + h] = grad_keys
        out_heads[2 * HEADS + h] = grad_values
        return 0

    lax.fori_loop(0, HEADS, attend_back, 0, unroll=UNROLL)
    one.third()
    for i in range(3 * HEADS):
        packed_grads[every, i * HEAD_DIM : (i + 1) * HEAD_DIM] = out_heads[i]
    qkv_blocks(ROWS, tall, packed_grads, grads_space)
    two.start()
    upstream_of(packed_grads, every, w_spatial_qkv, low, ROWS)
    one.fourth()
    two.first()
    two.second()
    grad_tokens[...] = (
        flat[...]
        + norm_pullback(wide(tokens[...]), upstream_rows(low, 0, ROWS), 1.0 + mod[1])
    ).astype(HALF16)
    one.fifth(final_time)
    one_z.start()
    two.third()
    one_z.middle()
    two.fourth()
    one_z.end()
    two.fifth(final_space)
    two_z.start()
    assemble(out_time, summed, 0)
    two_z.middle()
    two_z.end()
    assemble(out_space, summed, WIDE)
    for user in resid_trips + grad_trips + [one, two, one_z, two_z]:
        user.settle()


def vmem(shape, dtype=HALF16):
    return pltpu.VMEM(shape, dtype)


def run(lengths, mod, tokens, cotangent, w_spatial_qkv, w_spatial_out, w_temporal_qkv, w_temporal_out):
    full = jnp.float32
    sent, place, odd = vmem((2, BLOCKS, SPAN, D)), vmem((GROUPS, BLOCKS, SPAN, D)), vmem((BLOCKS, SPAN, NARROW))
    scratch = [
        vmem((ROWS, D)),
        vmem((ROWS, D)),
        vmem((QKV, D)),
        vmem((INNER, D)),
        vmem((QKV, D)),
        vmem((INNER, D)),
        pltpu.SemaphoreType.DMA((6,)),
        sent,
        place,
        sent,
        place,
        sent,
        odd,
        odd,
        odd,
        odd,
        odd,
        vmem((GROUP, NARROW), full),
        vmem((ROWS, D), full),
        vmem((ROWS, QKV)),
        vmem((3 * HEADS, ROWS, HEAD_DIM)),
        vmem((HEADS, ROWS, HEAD_DIM)),
        vmem((ROWS, INNER)),
        vmem((SPREAD, D)),
        vmem((2 * GROUP, QKV)),
        vmem((3 * HEADS, 2 * GROUP, HEAD_DIM)),
        vmem((SPREAD, D)),
        vmem((SPREAD, INNER)),
        vmem((HEADS, SPREAD, HEAD_DIM)),
        vmem((3 * HEADS, ROWS, HEAD_DIM)),
        vmem((SPREAD, QKV)),
        vmem((INNER, SPREAD), full),
        vmem((D, SPREAD)),
        vmem((D, SPREAD), full),
        vmem((D, SPREAD), full),
        vmem((GROUP, GROUP), full),
        vmem((BLOCKS, 72, WIDE)),
        vmem((BLOCKS, 72, WIDE)),
        vmem((9, 72, 128)),
        vmem((9, 72, 128)),
        vmem((2, 9, 72, 128)),
        vmem((2, 9, 72, 128)),
        vmem((BLOCKS, 72, HALF)),
        vmem((BLOCKS, 72, HALF)),
    ]
    for _ in range(3 * GROUPS):
        scratch += exchange_sems()
    for _ in range(2):
        scratch += reduction_buffers() + reduction_sems()
    for _ in range(2):
        scratch += [vmem((2, NZ, 72, 128))] + depth_sems()
    return pl.pallas_call(
        kernel,
        out_shape=(
            jax.ShapeDtypeStruct((ROWS, D), HALF16),
            jax.ShapeDtypeStruct((72, 2 * WIDE), HALF16),
        ),
        in_specs=[pl.BlockSpec(memory_space=pltpu.SMEM), pl.BlockSpec(memory_space=pltpu.VMEM)]
        + [pl.BlockSpec(memory_space=pl.ANY)] * 6,
        out_specs=(pl.BlockSpec(memory_space=pltpu.VMEM),) * 2,
        scratch_shapes=scratch,
        compiler_params=pltpu.CompilerParams(
            collective_id=0, has_side_effects=True, vmem_limit_bytes=VMEM_LIMIT
        ),
    )(lengths, mod, tokens, cotangent, w_spatial_qkv, w_spatial_out, w_temporal_qkv, w_temporal_out)


def unpack_grads(summed):
    tall = summed[:, QKV:]
    return summed[:, :QKV], jnp.concatenate([tall[:36], tall[36:]], axis=-1)


def local(
    tokens,
    cotangent,
    modulation,
    lengths,
    w_spatial_qkv,
    w_spatial_out,
    w_temporal_qkv,
    w_temporal_out,
):
    grad_tokens, summed = run(
        lengths,
        modulation.reshape(6, 1, D),
        tokens.reshape(ROWS, D),
        cotangent.reshape(ROWS, D),
        w_spatial_qkv.T,
        w_spatial_out,
        w_temporal_qkv.T,
        w_temporal_out,
    )
    temporal_qkv, temporal_out = unpack_grads(summed[:, :WIDE])
    spatial_qkv, spatial_out = unpack_grads(summed[:, WIDE:])
    return (
        grad_tokens.reshape(tokens.shape),
        spatial_qkv,
        spatial_out,
        temporal_qkv,
        temporal_out,
    )


def solution(mesh):
    placed = (
        P("dp", "seq", None, None),
        P("dp", "seq", None, None),
        P("dp", None, None),
        P("dp"),
        P(),
        P(),
        P(),
        P(),
    )
    return jax.shard_map(
        local,
        mesh=mesh,
        in_specs=placed,
        out_specs=(
            P("dp", "seq", None, None),
            P("seq", None),
            P("seq", None),
            P("seq", None),
            P("seq", None),
        ),
        check_vma=False,
    )
```

```python
import jax
import jax.numpy as jnp
from jax import lax
from jax.experimental import pallas as pl
from jax.experimental.pallas import tpu as pltpu
from jax.sharding import PartitionSpec as P

HEADS = 8
HEAD_DIM = 72
F = 16
SIDE = 4
NZ = 8
BLOCKS = 16
WIDE = 2304
HALF = 1152
VMEM_LIMIT = 63 * 1024 * 1024


def remote(src, dst, send, recv, device):
    return pltpu.make_async_remote_copy(
        src_ref=src,
        dst_ref=dst,
        send_sem=send,
        recv_sem=recv,
        device_id=device,
        device_id_type=pl.DeviceIdType.MESH,
    )


def hail(devices):
    barrier = pltpu.get_barrier_semaphore()
    for device in devices:
        pl.semaphore_signal(barrier, inc=1, device_id=device, device_id_type=pl.DeviceIdType.MESH)


def meet(devices):
    pl.semaphore_wait(pltpu.get_barrier_semaphore(), len(devices))


class Exchange:
    def __init__(self, place, source, into, own_sem, send_sems, recv_sems):
        self.place, self.source, self.into = place, source, into
        self.own_sem, self.send_sems, self.recv_sems = own_sem, send_sems, recv_sems

    def to(self, d):
        return lax.rem(self.place.seq + d, BLOCKS)

    def copy(self, d):
        at = self.place
        return remote(
            self.source.at[self.to(d)],
            self.into.at[at.seq],
            self.send_sems.at[d],
            self.recv_sems.at[d],
            (at.dp, self.to(d)),
        )

    def own(self):
        me = self.place.seq
        return pltpu.make_async_copy(self.source.at[me], self.into.at[me], self.own_sem)

    def start(self):
        self.own().start()
        for d in range(1, BLOCKS):
            self.copy(d).start()

    def arrive(self):
        at = self.place
        for d in range(1, BLOCKS):
            origin = lax.rem(at.seq + BLOCKS - d, BLOCKS)
            remote(
                self.source.at[origin],
                self.into.at[origin],
                self.send_sems.at[d],
                self.recv_sems.at[d],
                (at.dp, origin),
            ).wait_recv()
        self.own().wait()

    def settle(self):
        for d in range(1, BLOCKS):
            self.copy(d).wait_send()


def exchange_sems():
    dma = pltpu.SemaphoreType.DMA
    return [dma, dma((BLOCKS,)), dma((BLOCKS,))]


def plus(*refs):
    total = refs[0].astype(jnp.float32)
    for ref in refs[1:]:
        total = total + ref.astype(jnp.float32)
    return total.astype(jnp.bfloat16)


CUTS = ((0, 640), (640, 512))
DMA_COUNTS = (
    (BLOCKS, 2),
    (2, 2, 2),
    (2, 2, SIDE),
    (2, SIDE),
)


class Place:
    def __init__(self):
        dp, seq = lax.axis_index("dp"), lax.axis_index("seq")
        self.dp, self.seq = dp, seq
        self.z, self.c = lax.div(dp, 2), lax.rem(dp, 2)
        self.y, self.x = lax.div(seq, SIDE), lax.rem(seq, SIDE)
        self.twin = (self.z * 2 + 1 - self.c, seq)

    def neighbour(self, axis, dirn):
        step = 1 if dirn == 0 else SIDE - 1
        if axis == 0:
            return (self.dp, self.y * SIDE + lax.rem(self.x + step, SIDE))
        return (self.dp, lax.rem(self.y + step, SIDE) * SIDE + self.x)

    def along_z(self, d):
        return (lax.rem(self.z + d, NZ) * 2 + self.c, self.seq)

    def line(self):
        return [(self.dp, lax.rem(self.seq + d, BLOCKS)) for d in range(1, BLOCKS)]

    def friends(self):
        return [self.twin] + self.line() + [self.along_z(d) for d in range(1, NZ)]


class Reduction:
    def __init__(self, place, grads, buffers, sems):
        self.place, self.grads = place, grads
        self.acc, self.near, self.far, self.last = buffers
        (
            self.core_send,
            self.core_recv,
            self.near_send,
            self.near_recv,
            self.far_send,
            self.far_recv,
            self.last_send,
            self.last_recv,
        ) = sems

    def lanes(self, part):
        return pl.ds(CUTS[part][0], CUTS[part][1])

    def lanes_of(self, part, core):
        return pl.ds(pl.multiple_of(core * HALF + CUTS[part][0], 128), CUTS[part][1])

    def block(self, part, j, d):
        at = self.place
        if part == 0:
            return j * SIDE + lax.rem(at.x + d, SIDE)
        return lax.rem(at.y + d, SIDE) * SIDE + j

    def core_copy(self, part, b):
        at = self.place
        return remote(
            self.grads.at[b, :, self.lanes_of(part, 1 - at.c)],
            self.acc.at[b, :, self.lanes(part)],
            self.core_send.at[b, part],
            self.core_recv.at[b, part],
            at.twin,
        )

    def near_copy(self, part, dirn, k, b):
        return remote(
            self.acc.at[b, :, self.lanes(part)],
            self.near.at[part, dirn, k, :, pl.ds(0, CUTS[part][1])],
            self.near_send.at[part, dirn, k],
            self.near_recv.at[part, dirn, k],
            self.place.neighbour(part, dirn),
        )

    def far_copy(self, part, dirn, j, b):
        return remote(
            self.acc.at[b, :, self.lanes(part)],
            self.far.at[part, dirn, j, :, pl.ds(0, CUTS[part][1])],
            self.far_send.at[part, dirn, j],
            self.far_recv.at[part, dirn, j],
            self.place.neighbour(part, dirn),
        )

    def last_copy(self, part, d, b):
        at = self.place
        if part == 0:
            to = (at.dp, lax.rem(at.y + d, SIDE) * SIDE + at.x)
        else:
            to = (at.dp, at.y * SIDE + lax.rem(at.x + d, SIDE))
        return remote(
            self.acc.at[b, :, self.lanes(part)],
            self.last.at[part, d, :, pl.ds(0, CUTS[part][1])],
            self.last_send.at[part, d],
            self.last_recv.at[part, d],
            to,
        )

    def gather(self, part, b, *more):
        self.core_copy(part, b).wait_recv()
        lanes = self.lanes(part)
        mine = self.grads[b, :, self.lanes_of(part, self.place.c)]
        self.acc[b, :, lanes] = plus(mine, self.acc[b, :, lanes], *more)

    def start(self):
        for d in (2, 1, 3, 0):

            @pl.loop(0, SIDE)
            def _(j):
                for part in range(2):
                    self.core_copy(part, self.block(part, j, d)).start()

    def first(self):
        for dirn in range(2):

            @pl.loop(0, 2)
            def _(k):
                for part in range(2):
                    b = self.block(part, 2 * dirn + k, 2)
                    self.gather(part, b)
                    self.near_copy(part, dirn, k, b).start()

    def second(self):
        for dirn in range(2):

            @pl.loop(0, 2)
            def _(k):
                for part in range(2):
                    j = 2 * (1 - dirn) + k
                    b = self.block(part, j, 1 + 2 * dirn)
                    self.gather(part, b)
                    self.far_copy(part, dirn, j, b).start()

    def third(self):
        for dirn in range(2):

            @pl.loop(0, 2)
            def _(k):
                for part in range(2):
                    j = 2 * dirn + k
                    b = self.block(part, j, 1 + 2 * dirn)
                    self.near_copy(part, dirn, k, b).wait_recv()
                    self.gather(part, b, self.near[part, dirn, k, :, pl.ds(0, CUTS[part][1])])
                    self.far_copy(part, dirn, j, b).start()

    def finish(self, part, d):
        at = self.place
        b = self.block(1 - part, (at.x, at.y)[part], d)
        j = lax.rem((at.y, at.x)[part] + d, SIDE)
        for dirn in range(2):
            self.far_copy(part, dirn, j, b).wait_recv()
        width = pl.ds(0, CUTS[part][1])
        self.gather(part, b, self.far[part, 0, j, :, width], self.far[part, 1, j, :, width])
        return b

    def fourth(self):
        for d in (2, 1, 3):
            for part in range(2):
                self.last_copy(part, d, self.finish(part, d)).start()

    def fifth(self, final):
        for part in range(2):
            b = self.finish(part, 0)
            total = wide(self.acc[b, :, self.lanes(part)])
            start, width = CUTS[part]
            for d in range(1, SIDE):
                self.last_copy(part, d, b).wait_recv()
                total = total + wide(self.last[part, d, :, pl.ds(0, width)])
            for n in range(0, width, 128):
                final[(start + n) // 128] = total[:, n : n + 128].astype(jnp.bfloat16)

    def settle(self):
        for part in range(2):

            @pl.loop(0, BLOCKS)
            def _(b):
                self.core_copy(part, b).wait_send()

            for dirn in range(2):

                @pl.loop(0, 2)
                def _(k):
                    self.near_copy(part, dirn, k, 0).wait_send()

                @pl.loop(0, SIDE)
                def _(j):
                    self.far_copy(part, dirn, j, 0).wait_send()

            for d in range(1, SIDE):
                self.last_copy(part, d, 0).wait_send()


def reduction_buffers():
    half = jnp.bfloat16
    return [
        pltpu.VMEM((2, 2, 2, 72, 640), half),
        pltpu.VMEM((2, 2, SIDE, 72, 640), half),
        pltpu.VMEM((2, SIDE, 72, 640), half),
    ]


def reduction_sems():
    return [pltpu.SemaphoreType.DMA(counts) for counts in DMA_COUNTS for _ in range(2)]


class Depth:
    def __init__(self, place, final, out, arrived, sems):
        self.place, self.final, self.out = place, final, out
        self.arrived = arrived
        self.up_send, self.up_recv, self.down_send, self.down_recv, self.pair_send, self.pair_recv = sems

    def spot(self, i, core):
        return self.out.at[core, TILES[i][0]]

    def device(self, z):
        return (z * 2 + self.place.c, self.place.seq)

    def up(self, i, z):
        tile, owner, slot = TILES[i]
        return remote(
            self.final.at[tile],
            self.arrived.at[slot, z],
            self.up_send.at[i],
            self.up_recv.at[i, z],
            self.device(owner),
        )

    def down(self, i, z):
        spot = self.spot(i, self.place.c)
        return remote(spot, spot, self.down_send.at[i, z], self.down_recv.at[i], self.device(z))

    def pair(self, i, core):
        spot = self.spot(i, core)
        return remote(spot, spot, self.pair_send.at[i], self.pair_recv.at[i], self.place.twin)

    def owned(self, body):
        for i, (_, owner, _) in enumerate(TILES):
            pl.when(self.place.z == owner)(lambda i=i: body(i))

    def others(self, body):
        for i, (_, owner, _) in enumerate(TILES):
            pl.when(self.place.z != owner)(lambda i=i: body(i))

    def away(self, i):
        return [z for z in range(NZ) if z != TILES[i][1]]

    def start(self):
        self.others(lambda i: self.up(i, self.place.z).start())

    def add(self, i, tile, owner, slot):
        at = self.place
        spot = self.out.at[at.c, tile]
        total = self.final[tile].astype(jnp.float32)
        for d in range(1, NZ):
            z = lax.rem(owner + d, NZ)
            remote(
                self.final.at[tile],
                self.arrived.at[slot, z],
                self.up_send.at[i],
                self.up_recv.at[i, z],
                self.device(owner),
            ).wait_recv()
            total = total + self.arrived[slot, z].astype(jnp.float32)
        spot[...] = total.astype(jnp.bfloat16)
        for d in range(1, NZ):
            z = lax.rem(owner + d, NZ)
            remote(
                spot, spot, self.down_send.at[i, z], self.down_recv.at[i], self.device(z)
            ).start()
        remote(spot, spot, self.pair_send.at[i], self.pair_recv.at[i], at.twin).start()

    def middle(self):
        z = self.place.z
        self.add(z, z, z, 0)
        pl.when(z == 0)(lambda: self.add(NZ, NZ, 0, 1))

    def end(self):
        def forward(i):
            self.down(i, self.place.z).wait_recv()
            self.pair(i, self.place.c).start()

        self.others(forward)
        for i in range(len(TILES)):
            self.pair(i, 1 - self.place.c).wait_recv()

    def settle(self):
        self.others(lambda i: self.up(i, self.place.z).wait_send())

        def left(i):
            for z in self.away(i):
                self.down(i, z).wait_send()

        self.owned(left)
        for i in range(len(TILES)):
            self.pair(i, self.place.c).wait_send()


TILES = tuple((k, k % NZ, k // NZ) for k in range(9))


def depth_sems():
    dma = pltpu.SemaphoreType.DMA
    n = len(TILES)
    return [dma((n,)), dma((n, NZ)), dma((n, NZ)), dma((n,)), dma((n,)), dma((n,))]


NORM_EPS = 1e-06
MASKED = -1e30
ROWS = 320
SPAN = 8
GROUPS = 3
GROUP = SPAN * BLOCKS
SPREAD = GROUPS * GROUP
ODD = 4
D = 1152
INNER = 576
QKV = 1728
UNROLL = 2
NARROW = 640
REST = D - NARROW
SHARP = HEAD_DIM ** (-0.5)
SHARP2 = SHARP * 1.4426950408889634
NN = (((1,), (0,)), ((), ()))
NT = (((1,), (1,)), ((), ()))
TN = (((0,), (0,)), ((), ()))
HALF16 = jnp.bfloat16


def matmul(left, right, dims=NN):
    return lax.dot_general(left, right, dims, preferred_element_type=jnp.float32)


def columns(total, width=256):
    return [(start, min(width, total - start)) for start in range(0, total, width)]


def normalise(source):
    average = jnp.mean(source, axis=-1, keepdims=True)
    centred = source - average
    variance = jnp.mean(centred * centred, axis=-1, keepdims=True)
    spread = lax.rsqrt(variance + NORM_EPS)
    return centred * spread, spread


def modulated(source, mod, first):
    unit, _ = normalise(source)
    return (unit * (1.0 + mod[first + 1]) + mod[first]).astype(HALF16)


def norm_pullback(source, upstream, gain):
    unit, spread = normalise(source)
    grad = upstream * gain
    along = jnp.mean(grad * unit, axis=-1, keepdims=True)
    return spread * (grad - jnp.mean(grad, axis=-1, keepdims=True) - unit * along)


def wide(ref_value):
    return ref_value.astype(jnp.float32)


def by_columns(total, width, body, looped):
    if not looped:
        for start, part in columns(total, width):
            body(start, part)
        return
    even = total // width * width

    @pl.loop(0, even, step=width)
    def _(start):
        body(pl.multiple_of(start, width), width)

    if even < total:
        body(even, total - even)


def project_rows(rows_ref, rows, weight_ref, out_ref, out_rows):
    def body(start, width):
        cols = pl.ds(start, width)
        out_ref[out_rows, cols] = matmul(rows_ref[rows, :], weight_ref[cols, :], NT).astype(HALF16)

    by_columns(weight_ref.shape[0], 256, body, False)


def spread_heads(wide_ref, heads_ref, count, rows):
    for i in range(count):
        heads_ref[i, rows] = wide_ref[rows, i * HEAD_DIM : (i + 1) * HEAD_DIM]


def softmax(scores, axis):
    exponent = jnp.exp2((scores - jnp.max(scores, axis=axis, keepdims=True)) * SHARP2)
    return exponent * (1.0 / jnp.sum(exponent, axis=axis, keepdims=True))


def attend_spatial(heads, mixed_heads, rows):
    def body(h, _):
        scores = matmul(heads[h, rows], heads[HEADS + h], NT)
        soft = softmax(scores, -1).astype(HALF16)
        mixed_heads[h, rows] = matmul(soft, heads[2 * HEADS + h]).astype(HALF16)
        return 0

    lax.fori_loop(0, HEADS, body, 0, unroll=UNROLL)


def head_back(queries, keys, values, upstream, bias=None):
    scores = matmul(keys, queries, NT)
    if bias is not None:
        scores = scores + bias
    soft = softmax(scores, 0)
    soft_rounded = soft.astype(HALF16)
    raw = matmul(values, upstream, NT)
    centred = raw - jnp.sum(raw * soft, axis=0, keepdims=True)
    grad_scores = (soft * centred).astype(HALF16)
    grad_values = matmul(soft_rounded, upstream).astype(HALF16)
    grad_keys = (matmul(grad_scores, queries) * SHARP).astype(HALF16)
    grad_queries = (matmul(grad_scores, keys, TN) * SHARP).astype(HALF16)
    return grad_queries, grad_keys, grad_values, soft_rounded


def qkv_blocks(depth, tall, packed_grads, grads, looped):
    deep = slice(0, depth)

    def body(start, width):
        cols = pl.ds(start, width)
        product = matmul(tall[:, deep], packed_grads[deep, cols])
        grads[:, :, cols] = product.reshape(BLOCKS, 72, width).astype(HALF16)

    by_columns(QKV, 256, body, looped)


def out_blocks(depth, inner_tall, cot, low, high, grads):
    deep = slice(0, depth)
    low[:, deep] = jnp.zeros((D, depth), jnp.float32)
    high[:, deep] = jnp.zeros((D, depth), jnp.float32)
    for s in range(BLOCKS):
        rows = inner_tall[s * 36 : (s + 1) * 36, deep]
        low[s * 72 : s * 72 + 36, deep] = rows
        high[s * 72 + 36 : (s + 1) * 72, deep] = rows
    low_rows, high_rows = low[:, deep].astype(HALF16), high[:, deep].astype(HALF16)
    for start, width in ((0, 192), (192, 192), (384, 192)):
        product = matmul(low_rows, cot[deep, start : start + width]) + matmul(
            high_rows, cot[deep, INNER + start : INNER + start + width]
        )
        grads[:, :, QKV + start : QKV + start + width] = product.reshape(BLOCKS, 72, width).astype(
            HALF16
        )


def transposed(rows_ref, count, tall_ref):
    for start, width in columns(D, 128):
        cols = slice(start, start + width)
        tall_ref[cols, 0:count] = rows_ref[0:count, cols].T


def upstream_of(packed_grads, rows, w_qkv, into, count, looped):
    def body(start, width):
        into[pl.ds(start, count), :] = matmul(packed_grads[rows, :], w_qkv[:, pl.ds(start, width)])

    by_columns(D, SPREAD, body, looped)


def upstream_rows(into, start, count):
    return jnp.concatenate(
        [into[n * SPREAD + start : n * SPREAD + start + count, :] for n in range(3)], axis=-1
    )


def fold_odd(flat, first, step, pad, blocks):
    for i in range(BLOCKS):
        rows = slice(first + i * step, first + i * step + ODD)
        pad[i * SPAN : i * SPAN + ODD, :] = flat[rows, 0:NARROW]
        pad[i * SPAN + ODD : (i + 1) * SPAN, 0:REST] = flat[rows, NARROW:D]
    blocks[...] = pad[...].reshape(BLOCKS, SPAN, NARROW).astype(HALF16)


def unfold_odd(blocks, pad, flat, first, step):
    pad[...] = wide(blocks[...]).reshape(GROUP, NARROW)
    for i in range(BLOCKS):
        rows = slice(first + i * step, first + i * step + ODD)
        flat[rows, 0:NARROW] = pad[i * SPAN : i * SPAN + ODD, :]
        flat[rows, NARROW:D] = pad[i * SPAN + ODD : (i + 1) * SPAN, 0:REST]


def assemble(tiles, summed, start):
    for core in range(2):
        for k in range(9):
            summed[core, :, start + k * 128 : start + (k + 1) * 128] = tiles[core, k]


def as_blocks(rows):
    return rows.reshape(BLOCKS, SPAN, D).astype(HALF16)


def kernel(
    lengths,
    mod,
    tokens_far,
    cot_far,
    w_spatial_qkv_far,
    w_spatial_out_far,
    w_temporal_qkv_far,
    w_temporal_out_far,
    grad_tokens,
    summed,
    tokens,
    cot,
    w_spatial_qkv,
    w_spatial_out,
    w_temporal_qkv,
    w_temporal_out,
    load_sems,
    cot_blocks,
    cot_place,
    resid_blocks,
    resid_place,
    grad_place,
    cot_odd,
    cot_odd_place,
    resid_odd,
    resid_odd_place,
    grad_odd_place,
    pad,
    flat,
    packed,
    heads,
    mixed_heads,
    mixed,
    normed_time,
    packed_time,
    heads_time,
    scaled,
    grad_inner,
    grad_heads,
    out_heads,
    packed_grads,
    inner_tall,
    tall,
    low,
    high,
    bias,
    grads_time,
    grads_space,
    final_time,
    final_space,
    out_time,
    out_space,
    acc_time,
    acc_space,
    *scratch,
):
    at = Place()
    loads = [
        pltpu.make_async_copy(far, near, load_sems.at[i])
        for i, (far, near) in enumerate(
            (
                (cot_far, cot),
                (tokens_far, tokens),
                (w_spatial_qkv_far, w_spatial_qkv),
                (w_spatial_out_far, w_spatial_out),
                (w_temporal_out_far, w_temporal_out),
                (w_temporal_qkv_far, w_temporal_qkv),
            )
        )
    ]
    for load in loads:
        load.start()
    hail(at.friends())

    taken = 0

    def take(count):
        nonlocal taken
        taken += count
        return scratch[taken - count : taken]

    def trips(source, into, odd, odd_into):
        pairs = [(source.at[g], into.at[g]) for g in range(2)] + [(odd, odd_into)]
        return [Exchange(at, left, right, *take(3)) for left, right in pairs]

    cot_trips = trips(cot_blocks, cot_place, cot_odd, cot_odd_place)
    resid_trips = trips(resid_blocks, resid_place, resid_odd, resid_odd_place)
    grad_trips = trips(cot_blocks, grad_place, cot_odd, grad_odd_place)
    one = Reduction(at, grads_time, [acc_time, *take(3)], take(8))
    two = Reduction(at, grads_space, [acc_space, *take(3)], take(8))
    one_z = Depth(at, final_time, out_time, *take(1), take(6))
    two_z = Depth(at, final_space, out_space, *take(1), take(6))

    pad[...] = jnp.zeros_like(pad)
    loads[0].wait()
    for g in range(2):
        cot_blocks[g] = as_blocks(wide(cot[g * GROUP : (g + 1) * GROUP, :]))
    flat[2 * GROUP : ROWS, :] = wide(cot[2 * GROUP : ROWS, :])
    fold_odd(flat, 2 * GROUP, ODD, pad, cot_odd)
    meet(at.friends())
    for trip in cot_trips:
        trip.start()

    every = slice(0, ROWS)
    normed = cot
    loads[1].wait()

    def norm_rows(start):
        rows = pl.ds(pl.multiple_of(start, ROWS // 2), ROWS // 2)
        normed[rows, :] = modulated(wide(tokens[rows, :]), mod, 0)

    pl.loop(0, ROWS, step=ROWS // 2)(norm_rows)
    loads[2].wait()
    project_rows(normed, every, w_spatial_qkv, packed, every)
    spread_heads(packed, heads, 3 * HEADS, every)
    loads[3].wait()

    def residual(first, last):
        rows = slice(first, last)
        attend_spatial(heads, mixed_heads, rows)
        for h in range(HEADS):
            mixed[rows, h * HEAD_DIM : (h + 1) * HEAD_DIM] = mixed_heads[h, rows]
        for start, width in columns(D):
            cols = slice(start, start + width)
            product = matmul(mixed[rows, :], w_spatial_out[:, cols])
            flat[rows, cols] = wide(tokens[rows, cols]) + mod[2][:, cols] * product

    residual(GROUP, ROWS)
    resid_blocks[1] = as_blocks(flat[GROUP : 2 * GROUP, :])
    resid_trips[1].start()
    fold_odd(flat, 2 * GROUP, ODD, pad, resid_odd)
    resid_trips[2].start()
    residual(0, GROUP)
    resid_blocks[0] = as_blocks(flat[0:GROUP, :])
    resid_trips[0].start()

    limit = lengths[0].astype(jnp.float32)

    def frame_of(index):
        return jnp.floor(index * (1.0 / SPAN))

    keys = lax.broadcasted_iota(jnp.int32, (GROUP, 1), 0).astype(jnp.float32)
    queries = lax.broadcasted_iota(jnp.int32, (1, GROUP), 1).astype(jnp.float32)
    same = (keys - SPAN * frame_of(keys)) == (queries - SPAN * frame_of(queries))
    bias[...] = jnp.where(same & (frame_of(keys) < limit), 0.0, MASKED)

    def frames(place, g):
        return wide(place[g]).reshape(GROUP, D)

    def masked_rows(g):
        return jnp.where(frame_of(keys) < limit, 1.0, 0.0) * frames(cot_place, g)

    def settle_odd(trip, odd_place, place):
        trip.arrive()
        flat[0:GROUP, :] = jnp.zeros((GROUP, D), jnp.float32)
        unfold_odd(odd_place, pad, flat, 0, SPAN)
        place[2] = as_blocks(flat[0:GROUP, :])

    for g in range(2):
        cot_trips[g].arrive()
    settle_odd(cot_trips[2], cot_odd_place, cot_place)
    for g in range(GROUPS):
        scaled[g * GROUP : (g + 1) * GROUP, :] = (mod[5] * masked_rows(g)).astype(HALF16)
    loads[4].wait()
    grad_inner[...] = matmul(scaled[...], w_temporal_out[...], NT).astype(HALF16)
    spread_heads(grad_inner, grad_heads, HEADS, slice(0, SPREAD))
    for trip in cot_trips:
        trip.settle()
    loads[5].wait()

    def temporal(members):
        count = len(members) * GROUP
        here, rows = slice(0, count), slice(members[0] * GROUP, members[0] * GROUP + count)
        for g in members:
            if g == 2:
                settle_odd(resid_trips[g], resid_odd_place, resid_place)
            else:
                resid_trips[g].arrive()
            normed_time[g * GROUP : (g + 1) * GROUP, :] = modulated(frames(resid_place, g), mod, 3)
        project_rows(normed_time, rows, w_temporal_qkv, packed_time, here)
        spread_heads(packed_time, heads_time, 3 * HEADS, here)

        def body(h, _):
            inner = pl.ds(pl.multiple_of(h * HEAD_DIM, 8), HEAD_DIM)
            for i, g in enumerate(members):
                part, whole_rows = slice(i * GROUP, (i + 1) * GROUP), slice(g * GROUP, (g + 1) * GROUP)
                values = heads_time[2 * HEADS + h, part]
                grad_queries, grad_keys, grad_values, soft = head_back(
                    heads_time[h, part],
                    heads_time[HEADS + h, part],
                    values,
                    grad_heads[h, whole_rows],
                    bias[...],
                )
                inner_tall[inner, whole_rows] = matmul(values, soft, TN)
                out_heads[h, part] = grad_queries
                out_heads[HEADS + h, part] = grad_keys
                out_heads[2 * HEADS + h, part] = grad_values
            return 0

        lax.fori_loop(0, HEADS, body, 0, unroll=UNROLL)
        for i in range(3 * HEADS):
            packed_grads[rows, i * HEAD_DIM : (i + 1) * HEAD_DIM] = out_heads[i, here]
        upstream_of(packed_grads, rows, w_temporal_qkv, low, count, False)
        for i, g in enumerate(members):
            total = masked_rows(g) + norm_pullback(
                frames(resid_place, g), upstream_rows(low, i * GROUP, GROUP), 1.0 + mod[4]
            )
            if g == 2:
                flat[0:GROUP, :] = total
                fold_odd(flat, 0, SPAN, pad, cot_odd)
            else:
                cot_blocks[g] = as_blocks(total)
            grad_trips[g].start()

    temporal((1, 2))
    temporal((0,))
    transposed(normed_time, SPREAD, tall)
    qkv_blocks(SPREAD, tall, packed_grads, grads_time, True)
    out_blocks(SPREAD, inner_tall, scaled, low, high, grads_time)
    one.start()

    transposed(normed, ROWS, tall)
    inner_tall[:, every] = wide(mixed[...]).T
    for g in (1, 2, 0):
        grad_trips[g].arrive()
    unfold_odd(grad_odd_place, pad, flat, 2 * GROUP, ODD)
    for g in range(2):
        flat[g * GROUP : (g + 1) * GROUP, :] = frames(grad_place, g)
    scaled[every, :] = (mod[2] * flat[...]).astype(HALF16)
    grad_inner[every, :] = matmul(scaled[every, :], w_spatial_out[...], NT).astype(HALF16)
    spread_heads(grad_inner, grad_heads, HEADS, every)
    one.first()
    one.second()
    out_blocks(ROWS, inner_tall, scaled, low, high, grads_space)

    def attend_back(h, _):
        grad_queries, grad_keys, grad_values, _ = head_back(
            heads[h], heads[HEADS + h], heads[2 * HEADS + h], grad_heads[h, every]
        )
        out_heads[h] = grad_queries
        out_heads[HEADS + h] = grad_keys
        out_heads[2 * HEADS + h] = grad_values
        return 0

    lax.fori_loop(0, HEADS, attend_back, 0, unroll=UNROLL)
    one.third()
    for i in range(3 * HEADS):
        packed_grads[every, i * HEAD_DIM : (i + 1) * HEAD_DIM] = out_heads[i]
    qkv_blocks(ROWS, tall, packed_grads, grads_space, False)
    two.start()
    upstream_of(packed_grads, every, w_spatial_qkv, low, ROWS, True)
    one.fourth()
    two.first()
    two.second()

    def last_rows(start):
        count = ROWS // 2
        rows = pl.ds(pl.multiple_of(start, count), count)
        grad = jnp.concatenate(
            [low[pl.ds(pl.multiple_of(n * SPREAD + start, 32), count), :] for n in range(3)], axis=-1
        )
        grad_tokens[rows, :] = (
            flat[rows, :] + norm_pullback(wide(tokens[rows, :]), grad, 1.0 + mod[1])
        ).astype(HALF16)

    pl.loop(0, ROWS, step=ROWS // 2)(last_rows)
    one.fifth(final_time)
    one_z.start()
    two.third()
    one_z.middle()
    two.fourth()
    one_z.end()
    two.fifth(final_space)
    two_z.start()
    assemble(out_time, summed, 0)
    two_z.middle()
    two_z.end()
    assemble(out_space, summed, HALF)
    for user in resid_trips + grad_trips + [one, two, one_z, two_z]:
        user.settle()


def vmem(shape, dtype=HALF16):
    return pltpu.VMEM(shape, dtype)


def run(lengths, mod, tokens, cotangent, w_spatial_qkv, w_spatial_out, w_temporal_qkv, w_temporal_out):
    full = jnp.float32
    sent, place, odd = vmem((2, BLOCKS, SPAN, D)), vmem((GROUPS, BLOCKS, SPAN, D)), vmem((BLOCKS, SPAN, NARROW))
    scratch = [
        vmem((ROWS, D)),
        vmem((ROWS, D)),
        vmem((QKV, D)),
        vmem((INNER, D)),
        vmem((QKV, D)),
        vmem((INNER, D)),
        pltpu.SemaphoreType.DMA((6,)),
        sent,
        place,
        sent,
        place,
        sent,
        odd,
        odd,
        odd,
        odd,
        odd,
        vmem((GROUP, NARROW), full),
        vmem((ROWS, D), full),
        vmem((ROWS, QKV)),
        vmem((3 * HEADS, ROWS, HEAD_DIM)),
        vmem((HEADS, ROWS, HEAD_DIM)),
        vmem((ROWS, INNER)),
        vmem((SPREAD, D)),
        vmem((2 * GROUP, QKV)),
        vmem((3 * HEADS, 2 * GROUP, HEAD_DIM)),
        vmem((SPREAD, D)),
        vmem((SPREAD, INNER)),
        vmem((HEADS, SPREAD, HEAD_DIM)),
        vmem((3 * HEADS, ROWS, HEAD_DIM)),
        vmem((SPREAD, QKV)),
        vmem((INNER, SPREAD), full),
        vmem((D, SPREAD)),
        vmem((D, SPREAD), full),
        vmem((D, SPREAD), full),
        vmem((GROUP, GROUP), full),
        vmem((BLOCKS, 72, WIDE)),
        vmem((BLOCKS, 72, WIDE)),
        vmem((9, 72, 128)),
        vmem((9, 72, 128)),
        vmem((2, 9, 72, 128)),
        vmem((2, 9, 72, 128)),
        vmem((BLOCKS, 72, HALF)),
        vmem((BLOCKS, 72, HALF)),
    ]
    for _ in range(3 * GROUPS):
        scratch += exchange_sems()
    for _ in range(2):
        scratch += reduction_buffers() + reduction_sems()
    for _ in range(2):
        scratch += [vmem((2, NZ, 72, 128))] + depth_sems()
    return pl.pallas_call(
        kernel,
        out_shape=(
            jax.ShapeDtypeStruct((ROWS, D), HALF16),
            jax.ShapeDtypeStruct((2, 72, WIDE), HALF16),
        ),
        in_specs=[pl.BlockSpec(memory_space=pltpu.SMEM), pl.BlockSpec(memory_space=pltpu.VMEM)]
        + [pl.BlockSpec(memory_space=pl.ANY)] * 6,
        out_specs=(pl.BlockSpec(memory_space=pltpu.VMEM),) * 2,
        scratch_shapes=scratch,
        compiler_params=pltpu.CompilerParams(
            collective_id=0, has_side_effects=True, vmem_limit_bytes=VMEM_LIMIT
        ),
    )(lengths, mod, tokens, cotangent, w_spatial_qkv, w_spatial_out, w_temporal_qkv, w_temporal_out)


def unpack_grads(summed, item):
    left, right = (half[:, item * HALF : (item + 1) * HALF] for half in (summed[0], summed[1]))
    tall = right[:, QKV - HALF :]
    return (
        jnp.concatenate([left, right[:, : QKV - HALF]], axis=-1),
        jnp.concatenate([tall[:36], tall[36:]], axis=-1),
    )


def local(
    tokens,
    cotangent,
    modulation,
    lengths,
    w_spatial_qkv,
    w_spatial_out,
    w_temporal_qkv,
    w_temporal_out,
):
    grad_tokens, summed = run(
        lengths,
        modulation.reshape(6, 1, D),
        tokens.reshape(ROWS, D),
        cotangent.reshape(ROWS, D),
        w_spatial_qkv.T,
        w_spatial_out,
        w_temporal_qkv.T,
        w_temporal_out,
    )
    temporal_qkv, temporal_out = unpack_grads(summed, 0)
    spatial_qkv, spatial_out = unpack_grads(summed, 1)
    return (
        grad_tokens.reshape(tokens.shape),
        spatial_qkv,
        spatial_out,
        temporal_qkv,
        temporal_out,
    )


def solution(mesh):
    placed = (
        P("dp", "seq", None, None),
        P("dp", "seq", None, None),
        P("dp", None, None),
        P("dp"),
        P(),
        P(),
        P(),
        P(),
    )
    return jax.shard_map(
        local,
        mesh=mesh,
        in_specs=placed,
        out_specs=(
            P("dp", "seq", None, None),
            P("seq", None),
            P("seq", None),
            P("seq", None),
            P("seq", None),
        ),
        check_vma=False,
    )
```

```python
import jax
import jax.numpy as jnp
from jax import lax
from jax.experimental import pallas as pl
from jax.experimental.pallas import tpu as pltpu
from jax.sharding import PartitionSpec as P

HEADS = 8
HEAD_DIM = 72
F = 16
SIDE = 4
NZ = 8
BLOCKS = 16
WIDE = 2304
HALF = 1152
VMEM_LIMIT = 63 * 1024 * 1024


def remote(src, dst, send, recv, device):
    return pltpu.make_async_remote_copy(
        src_ref=src,
        dst_ref=dst,
        send_sem=send,
        recv_sem=recv,
        device_id=device,
        device_id_type=pl.DeviceIdType.MESH,
    )


def hail(devices):
    barrier = pltpu.get_barrier_semaphore()
    for device in devices:
        pl.semaphore_signal(barrier, inc=1, device_id=device, device_id_type=pl.DeviceIdType.MESH)


def meet(devices):
    pl.semaphore_wait(pltpu.get_barrier_semaphore(), len(devices))


class Exchange:
    def __init__(self, place, source, into, own_sem, send_sems, recv_sems):
        self.place, self.source, self.into = place, source, into
        self.own_sem, self.send_sems, self.recv_sems = own_sem, send_sems, recv_sems

    def to(self, d):
        return lax.rem(self.place.seq + d, BLOCKS)

    def copy(self, d):
        at = self.place
        return remote(
            self.source.at[self.to(d)],
            self.into.at[at.seq],
            self.send_sems.at[d],
            self.recv_sems.at[d],
            (at.dp, self.to(d)),
        )

    def own(self):
        me = self.place.seq
        return pltpu.make_async_copy(self.source.at[me], self.into.at[me], self.own_sem)

    def start(self):
        self.own().start()
        for d in range(1, BLOCKS):
            self.copy(d).start()

    def arrive(self):
        at = self.place
        for d in range(1, BLOCKS):
            origin = lax.rem(at.seq + BLOCKS - d, BLOCKS)
            remote(
                self.source.at[origin],
                self.into.at[origin],
                self.send_sems.at[d],
                self.recv_sems.at[d],
                (at.dp, origin),
            ).wait_recv()
        self.own().wait()

    def settle(self):
        for d in range(1, BLOCKS):
            self.copy(d).wait_send()


def exchange_sems():
    dma = pltpu.SemaphoreType.DMA
    return [dma, dma((BLOCKS,)), dma((BLOCKS,))]


def plus(*refs):
    total = refs[0].astype(jnp.float32)
    for ref in refs[1:]:
        total = total + ref.astype(jnp.float32)
    return total.astype(jnp.bfloat16)


CUTS = ((0, 640), (640, 512))
DMA_COUNTS = (
    (BLOCKS, 2),
    (2, 2, 2),
    (2, 2, SIDE),
    (2, SIDE),
)


class Place:
    def __init__(self):
        dp, seq = lax.axis_index("dp"), lax.axis_index("seq")
        self.dp, self.seq = dp, seq
        self.z, self.c = lax.div(dp, 2), lax.rem(dp, 2)
        self.y, self.x = lax.div(seq, SIDE), lax.rem(seq, SIDE)
        self.twin = (self.z * 2 + 1 - self.c, seq)

    def neighbour(self, axis, dirn):
        step = 1 if dirn == 0 else SIDE - 1
        if axis == 0:
            return (self.dp, self.y * SIDE + lax.rem(self.x + step, SIDE))
        return (self.dp, lax.rem(self.y + step, SIDE) * SIDE + self.x)

    def along_z(self, d):
        return (lax.rem(self.z + d, NZ) * 2 + self.c, self.seq)

    def line(self):
        return [(self.dp, lax.rem(self.seq + d, BLOCKS)) for d in range(1, BLOCKS)]

    def friends(self):
        return [self.twin] + self.line() + [self.along_z(d) for d in range(1, NZ)]


class Reduction:
    def __init__(self, place, grads, buffers, sems):
        self.place, self.grads = place, grads
        self.acc, self.near, self.far, self.last = buffers
        (
            self.core_send,
            self.core_recv,
            self.near_send,
            self.near_recv,
            self.far_send,
            self.far_recv,
            self.last_send,
            self.last_recv,
        ) = sems

    def lanes(self, part):
        return pl.ds(CUTS[part][0], CUTS[part][1])

    def lanes_of(self, part, core):
        return pl.ds(pl.multiple_of(core * HALF + CUTS[part][0], 128), CUTS[part][1])

    def block(self, part, j, d):
        at = self.place
        if part == 0:
            return j * SIDE + lax.rem(at.x + d, SIDE)
        return lax.rem(at.y + d, SIDE) * SIDE + j

    def core_copy(self, part, b):
        at = self.place
        return remote(
            self.grads.at[b, :, self.lanes_of(part, 1 - at.c)],
            self.acc.at[b, :, self.lanes(part)],
            self.core_send.at[b, part],
            self.core_recv.at[b, part],
            at.twin,
        )

    def near_copy(self, part, dirn, k, b):
        return remote(
            self.acc.at[b, :, self.lanes(part)],
            self.near.at[part, dirn, k, :, pl.ds(0, CUTS[part][1])],
            self.near_send.at[part, dirn, k],
            self.near_recv.at[part, dirn, k],
            self.place.neighbour(part, dirn),
        )

    def far_copy(self, part, dirn, j, b):
        return remote(
            self.acc.at[b, :, self.lanes(part)],
            self.far.at[part, dirn, j, :, pl.ds(0, CUTS[part][1])],
            self.far_send.at[part, dirn, j],
            self.far_recv.at[part, dirn, j],
            self.place.neighbour(part, dirn),
        )

    def last_copy(self, part, d, b):
        at = self.place
        if part == 0:
            to = (at.dp, lax.rem(at.y + d, SIDE) * SIDE + at.x)
        else:
            to = (at.dp, at.y * SIDE + lax.rem(at.x + d, SIDE))
        return remote(
            self.acc.at[b, :, self.lanes(part)],
            self.last.at[part, d, :, pl.ds(0, CUTS[part][1])],
            self.last_send.at[part, d],
            self.last_recv.at[part, d],
            to,
        )

    def gather(self, part, b, *more):
        self.core_copy(part, b).wait_recv()
        lanes = self.lanes(part)
        mine = self.grads[b, :, self.lanes_of(part, self.place.c)]
        self.acc[b, :, lanes] = plus(mine, self.acc[b, :, lanes], *more)

    def start(self):
        for d in (2, 1, 3, 0):

            @pl.loop(0, SIDE)
            def _(j):
                for part in range(2):
                    self.core_copy(part, self.block(part, j, d)).start()

    def first(self):
        for dirn in range(2):

            @pl.loop(0, 2)
            def _(k):
                for part in range(2):
                    b = self.block(part, 2 * dirn + k, 2)
                    self.gather(part, b)
                    self.near_copy(part, dirn, k, b).start()

    def second(self):
        for dirn in range(2):

            @pl.loop(0, 2)
            def _(k):
                for part in range(2):
                    j = 2 * (1 - dirn) + k
                    b = self.block(part, j, 1 + 2 * dirn)
                    self.gather(part, b)
                    self.far_copy(part, dirn, j, b).start()

    def third(self):
        for dirn in range(2):

            @pl.loop(0, 2)
            def _(k):
                for part in range(2):
                    j = 2 * dirn + k
                    b = self.block(part, j, 1 + 2 * dirn)
                    self.near_copy(part, dirn, k, b).wait_recv()
                    self.gather(part, b, self.near[part, dirn, k, :, pl.ds(0, CUTS[part][1])])
                    self.far_copy(part, dirn, j, b).start()

    def finish(self, part, d):
        at = self.place
        b = self.block(1 - part, (at.x, at.y)[part], d)
        j = lax.rem((at.y, at.x)[part] + d, SIDE)
        for dirn in range(2):
            self.far_copy(part, dirn, j, b).wait_recv()
        width = pl.ds(0, CUTS[part][1])
        self.gather(part, b, self.far[part, 0, j, :, width], self.far[part, 1, j, :, width])
        return b

    def fourth(self):
        for d in (2, 1, 3):
            for part in range(2):
                self.last_copy(part, d, self.finish(part, d)).start()

    def fifth(self, final):
        for part in range(2):
            b = self.finish(part, 0)
            total = wide(self.acc[b, :, self.lanes(part)])
            start, width = CUTS[part]
            for d in range(1, SIDE):
                self.last_copy(part, d, b).wait_recv()
                total = total + wide(self.last[part, d, :, pl.ds(0, width)])
            for n in range(0, width, 128):
                final[(start + n) // 128] = total[:, n : n + 128].astype(jnp.bfloat16)

    def settle(self):
        for part in range(2):

            @pl.loop(0, BLOCKS)
            def _(b):
                self.core_copy(part, b).wait_send()

            for dirn in range(2):

                @pl.loop(0, 2)
                def _(k):
                    self.near_copy(part, dirn, k, 0).wait_send()

                @pl.loop(0, SIDE)
                def _(j):
                    self.far_copy(part, dirn, j, 0).wait_send()

            for d in range(1, SIDE):
                self.last_copy(part, d, 0).wait_send()


def reduction_buffers():
    half = jnp.bfloat16
    return [
        pltpu.VMEM((2, 2, 2, 72, 640), half),
        pltpu.VMEM((2, 2, SIDE, 72, 640), half),
        pltpu.VMEM((2, SIDE, 72, 640), half),
    ]


def reduction_sems():
    return [pltpu.SemaphoreType.DMA(counts) for counts in DMA_COUNTS for _ in range(2)]


class Depth:
    def __init__(self, place, final, out, arrived, sems):
        self.place, self.final, self.out = place, final, out
        self.arrived = arrived
        self.up_send, self.up_recv, self.down_send, self.down_recv, self.pair_send, self.pair_recv = sems

    def spot(self, i, core):
        return self.out.at[core, TILES[i][0]]

    def device(self, z):
        return (z * 2 + self.place.c, self.place.seq)

    def up(self, i, z):
        tile, owner, slot = TILES[i]
        return remote(
            self.final.at[tile],
            self.arrived.at[slot, z],
            self.up_send.at[i],
            self.up_recv.at[i, z],
            self.device(owner),
        )

    def down(self, i, z):
        spot = self.spot(i, self.place.c)
        return remote(spot, spot, self.down_send.at[i, z], self.down_recv.at[i], self.device(z))

    def pair(self, i, core):
        spot = self.spot(i, core)
        return remote(spot, spot, self.pair_send.at[i], self.pair_recv.at[i], self.place.twin)

    def owned(self, body):
        for i, (_, owner, _) in enumerate(TILES):
            pl.when(self.place.z == owner)(lambda i=i: body(i))

    def others(self, body):
        for i, (_, owner, _) in enumerate(TILES):
            pl.when(self.place.z != owner)(lambda i=i: body(i))

    def away(self, i):
        return [z for z in range(NZ) if z != TILES[i][1]]

    def start(self):
        self.others(lambda i: self.up(i, self.place.z).start())

    def add(self, i, tile, owner, slot):
        at = self.place
        spot = self.out.at[at.c, tile]
        total = self.final[tile].astype(jnp.float32)
        for d in range(1, NZ):
            z = lax.rem(owner + d, NZ)
            remote(
                self.final.at[tile],
                self.arrived.at[slot, z],
                self.up_send.at[i],
                self.up_recv.at[i, z],
                self.device(owner),
            ).wait_recv()
            total = total + self.arrived[slot, z].astype(jnp.float32)
        spot[...] = total.astype(jnp.bfloat16)
        for d in range(1, NZ):
            z = lax.rem(owner + d, NZ)
            remote(
                spot, spot, self.down_send.at[i, z], self.down_recv.at[i], self.device(z)
            ).start()
        remote(spot, spot, self.pair_send.at[i], self.pair_recv.at[i], at.twin).start()

    def middle(self):
        z = self.place.z
        self.add(z, z, z, 0)
        pl.when(z == 0)(lambda: self.add(NZ, NZ, 0, 1))

    def end(self):
        def forward(i):
            self.down(i, self.place.z).wait_recv()
            self.pair(i, self.place.c).start()

        self.others(forward)
        for i in range(len(TILES)):
            self.pair(i, 1 - self.place.c).wait_recv()

    def settle(self):
        self.others(lambda i: self.up(i, self.place.z).wait_send())

        def left(i):
            for z in self.away(i):
                self.down(i, z).wait_send()

        self.owned(left)
        for i in range(len(TILES)):
            self.pair(i, self.place.c).wait_send()


TILES = tuple((k, k % NZ, k // NZ) for k in range(9))


def depth_sems():
    dma = pltpu.SemaphoreType.DMA
    n = len(TILES)
    return [dma((n,)), dma((n, NZ)), dma((n, NZ)), dma((n,)), dma((n,)), dma((n,))]


NORM_EPS = 1e-06
MASKED = -1e30
ROWS = 320
SPAN = 8
GROUPS = 3
GROUP = SPAN * BLOCKS
SPREAD = GROUPS * GROUP
ODD = 4
D = 1152
INNER = 576
QKV = 1728
UNROLL = 2
NARROW = 640
REST = D - NARROW
SHARP = HEAD_DIM ** (-0.5)
SHARP2 = SHARP * 1.4426950408889634
NN = (((1,), (0,)), ((), ()))
NT = (((1,), (1,)), ((), ()))
TN = (((0,), (0,)), ((), ()))
HALF16 = jnp.bfloat16


def matmul(left, right, dims=NN):
    return lax.dot_general(left, right, dims, preferred_element_type=jnp.float32)


def columns(total, width=256):
    return [(start, min(width, total - start)) for start in range(0, total, width)]


def normalise(source):
    average = jnp.mean(source, axis=-1, keepdims=True)
    centred = source - average
    variance = jnp.mean(centred * centred, axis=-1, keepdims=True)
    spread = lax.rsqrt(variance + NORM_EPS)
    return centred * spread, spread


def modulated(source, mod, first):
    unit, _ = normalise(source)
    return (unit * (1.0 + mod[first + 1]) + mod[first]).astype(HALF16)


def norm_pullback(source, upstream, gain):
    unit, spread = normalise(source)
    grad = upstream * gain
    along = jnp.mean(grad * unit, axis=-1, keepdims=True)
    return spread * (grad - jnp.mean(grad, axis=-1, keepdims=True) - unit * along)


def wide(ref_value):
    return ref_value.astype(jnp.float32)


def by_columns(total, width, body, looped):
    if not looped:
        for start, part in columns(total, width):
            body(start, part)
        return
    even = total // width * width

    @pl.loop(0, even, step=width)
    def _(start):
        body(pl.multiple_of(start, width), width)

    if even < total:
        body(even, total - even)


def project_rows(rows_ref, rows, weight_ref, out_ref, out_rows):
    def body(start, width):
        cols = pl.ds(start, width)
        out_ref[out_rows, cols] = matmul(rows_ref[rows, :], weight_ref[cols, :], NT).astype(HALF16)

    by_columns(weight_ref.shape[0], 256, body, False)


def spread_heads(wide_ref, heads_ref, count, rows):
    for i in range(count):
        heads_ref[i, rows] = wide_ref[rows, i * HEAD_DIM : (i + 1) * HEAD_DIM]


def softmax(scores, axis):
    exponent = jnp.exp2((scores - jnp.max(scores, axis=axis, keepdims=True)) * SHARP2)
    return exponent * (1.0 / jnp.sum(exponent, axis=axis, keepdims=True))


def attend_spatial(heads, mixed_heads, rows):
    def body(h, _):
        scores = matmul(heads[h, rows], heads[HEADS + h], NT)
        soft = softmax(scores, -1).astype(HALF16)
        mixed_heads[h, rows] = matmul(soft, heads[2 * HEADS + h]).astype(HALF16)
        return 0

    lax.fori_loop(0, HEADS, body, 0, unroll=UNROLL)


def head_back(queries, keys, values, upstream, bias=None):
    scores = matmul(keys, queries, NT)
    if bias is not None:
        scores = scores + bias
    soft = softmax(scores, 0)
    soft_rounded = soft.astype(HALF16)
    raw = matmul(values, upstream, NT)
    centred = raw - jnp.sum(raw * soft, axis=0, keepdims=True)
    grad_scores = (soft * centred).astype(HALF16)
    grad_values = matmul(soft_rounded, upstream).astype(HALF16)
    grad_keys = (matmul(grad_scores, queries) * SHARP).astype(HALF16)
    grad_queries = (matmul(grad_scores, keys, TN) * SHARP).astype(HALF16)
    return grad_queries, grad_keys, grad_values, soft_rounded


def qkv_blocks(depth, tall, packed_grads, grads, looped):
    deep = slice(0, depth)

    def body(start, width):
        cols = pl.ds(start, width)
        product = matmul(tall[:, deep], packed_grads[deep, cols])
        grads[:, :, cols] = product.reshape(BLOCKS, 72, width).astype(HALF16)

    by_columns(QKV, 256, body, looped)


def out_blocks(depth, inner_tall, cot, low, high, grads):
    deep = slice(0, depth)
    low[:, deep] = jnp.zeros((D, depth), jnp.float32)
    high[:, deep] = jnp.zeros((D, depth), jnp.float32)
    for s in range(BLOCKS):
        rows = inner_tall[s * 36 : (s + 1) * 36, deep]
        low[s * 72 : s * 72 + 36, deep] = rows
        high[s * 72 + 36 : (s + 1) * 72, deep] = rows
    low_rows, high_rows = low[:, deep].astype(HALF16), high[:, deep].astype(HALF16)
    for start, width in ((0, 192), (192, 192), (384, 192)):
        product = matmul(low_rows, cot[deep, start : start + width]) + matmul(
            high_rows, cot[deep, INNER + start : INNER + start + width]
        )
        grads[:, :, QKV + start : QKV + start + width] = product.reshape(BLOCKS, 72, width).astype(
            HALF16
        )


def transposed(rows_ref, count, tall_ref):
    for start, width in columns(D, 128):
        cols = slice(start, start + width)
        tall_ref[cols, 0:count] = rows_ref[0:count, cols].T


def upstream_of(packed_grads, rows, w_qkv, into, count, looped):
    def body(start, width):
        into[pl.ds(start, count), :] = matmul(packed_grads[rows, :], w_qkv[:, pl.ds(start, width)])

    by_columns(D, SPREAD, body, looped)


def upstream_rows(into, start, count):
    return jnp.concatenate(
        [into[n * SPREAD + start : n * SPREAD + start + count, :] for n in range(3)], axis=-1
    )


def fold_odd(flat, first, step, pad, blocks):
    for i in range(BLOCKS):
        rows = slice(first + i * step, first + i * step + ODD)
        pad[i * SPAN : i * SPAN + ODD, :] = flat[rows, 0:NARROW]
        pad[i * SPAN + ODD : (i + 1) * SPAN, 0:REST] = flat[rows, NARROW:D]
    blocks[...] = pad[...].reshape(BLOCKS, SPAN, NARROW).astype(HALF16)


def unfold_odd(blocks, pad, flat, first, step):
    pad[...] = wide(blocks[...]).reshape(GROUP, NARROW)
    for i in range(BLOCKS):
        rows = slice(first + i * step, first + i * step + ODD)
        flat[rows, 0:NARROW] = pad[i * SPAN : i * SPAN + ODD, :]
        flat[rows, NARROW:D] = pad[i * SPAN + ODD : (i + 1) * SPAN, 0:REST]


def assemble(tiles, summed, start):
    for core in range(2):
        for k in range(9):
            summed[core, :, start + k * 128 : start + (k + 1) * 128] = tiles[core, k]


def as_blocks(rows):
    return rows.reshape(BLOCKS, SPAN, D).astype(HALF16)


def kernel(
    lengths,
    mod,
    tokens_far,
    cot_far,
    w_spatial_qkv_far,
    w_spatial_out_far,
    w_temporal_qkv_far,
    w_temporal_out_far,
    grad_tokens,
    summed,
    tokens,
    cot,
    w_spatial_qkv,
    w_spatial_out,
    w_temporal_qkv,
    w_temporal_out,
    load_sems,
    cot_blocks,
    cot_place,
    resid_blocks,
    resid_place,
    grad_place,
    cot_odd,
    cot_odd_place,
    resid_odd,
    resid_odd_place,
    grad_odd_place,
    pad,
    flat,
    packed,
    heads,
    mixed_heads,
    mixed,
    normed_time,
    packed_time,
    heads_time,
    scaled,
    grad_inner,
    grad_heads,
    out_heads,
    packed_grads,
    inner_tall,
    tall,
    low,
    high,
    bias,
    grads_time,
    grads_space,
    final_time,
    final_space,
    out_time,
    out_space,
    acc_time,
    acc_space,
    *scratch,
):
    at = Place()
    loads = [
        pltpu.make_async_copy(far, near, load_sems.at[i])
        for i, (far, near) in enumerate(
            (
                (cot_far, cot),
                (tokens_far, tokens),
                (w_spatial_qkv_far, w_spatial_qkv),
                (w_spatial_out_far, w_spatial_out),
                (w_temporal_out_far, w_temporal_out),
                (w_temporal_qkv_far, w_temporal_qkv),
            )
        )
    ]
    for load in loads:
        load.start()
    hail(at.friends())

    taken = 0

    def take(count):
        nonlocal taken
        taken += count
        return scratch[taken - count : taken]

    def trips(source, into, odd, odd_into):
        pairs = [(source.at[g], into.at[g]) for g in range(2)] + [(odd, odd_into)]
        return [Exchange(at, left, right, *take(3)) for left, right in pairs]

    cot_trips = trips(cot_blocks, cot_place, cot_odd, cot_odd_place)
    resid_trips = trips(resid_blocks, resid_place, resid_odd, resid_odd_place)
    grad_trips = trips(cot_blocks, grad_place, cot_odd, grad_odd_place)
    one = Reduction(at, grads_time, [acc_time, *take(3)], take(8))
    two = Reduction(at, grads_space, [acc_space, *take(3)], take(8))
    one_z = Depth(at, final_time, out_time, *take(1), take(6))
    two_z = Depth(at, final_space, out_space, *take(1), take(6))

    pad[...] = jnp.zeros_like(pad)
    loads[0].wait()
    for g in range(2):
        cot_blocks[g] = as_blocks(wide(cot[g * GROUP : (g + 1) * GROUP, :]))
    flat[2 * GROUP : ROWS, :] = wide(cot[2 * GROUP : ROWS, :])
    fold_odd(flat, 2 * GROUP, ODD, pad, cot_odd)
    meet(at.friends())
    for trip in cot_trips:
        trip.start()

    every = slice(0, ROWS)
    normed = cot
    loads[1].wait()

    def norm_rows(start):
        rows = pl.ds(pl.multiple_of(start, ROWS // 2), ROWS // 2)
        normed[rows, :] = modulated(wide(tokens[rows, :]), mod, 0)

    pl.loop(0, ROWS, step=ROWS // 2)(norm_rows)
    loads[2].wait()
    project_rows(normed, every, w_spatial_qkv, packed, every)
    spread_heads(packed, heads, 3 * HEADS, every)
    loads[3].wait()

    def residual(first, last):
        rows = slice(first, last)
        attend_spatial(heads, mixed_heads, rows)
        for h in range(HEADS):
            mixed[rows, h * HEAD_DIM : (h + 1) * HEAD_DIM] = mixed_heads[h, rows]
        for start, width in columns(D):
            cols = slice(start, start + width)
            product = matmul(mixed[rows, :], w_spatial_out[:, cols])
            flat[rows, cols] = wide(tokens[rows, cols]) + mod[2][:, cols] * product

    residual(GROUP, ROWS)
    resid_blocks[1] = as_blocks(flat[GROUP : 2 * GROUP, :])
    resid_trips[1].start()
    fold_odd(flat, 2 * GROUP, ODD, pad, resid_odd)
    resid_trips[2].start()
    residual(0, GROUP)
    resid_blocks[0] = as_blocks(flat[0:GROUP, :])
    resid_trips[0].start()

    limit = lengths[0].astype(jnp.float32)

    def frame_of(index):
        return jnp.floor(index * (1.0 / SPAN))

    keys = lax.broadcasted_iota(jnp.int32, (GROUP, 1), 0).astype(jnp.float32)
    queries = lax.broadcasted_iota(jnp.int32, (1, GROUP), 1).astype(jnp.float32)
    same = (keys - SPAN * frame_of(keys)) == (queries - SPAN * frame_of(queries))
    bias[...] = jnp.where(same & (frame_of(keys) < limit), 0.0, MASKED)

    def frames(place, g):
        return wide(place[g]).reshape(GROUP, D)

    def masked_rows(g):
        return jnp.where(frame_of(keys) < limit, 1.0, 0.0) * frames(cot_place, g)

    def settle_odd(trip, odd_place, place):
        trip.arrive()
        flat[0:GROUP, :] = jnp.zeros((GROUP, D), jnp.float32)
        unfold_odd(odd_place, pad, flat, 0, SPAN)
        place[2] = as_blocks(flat[0:GROUP, :])

    for g in range(2):
        cot_trips[g].arrive()
    settle_odd(cot_trips[2], cot_odd_place, cot_place)
    for g in range(GROUPS):
        scaled[g * GROUP : (g + 1) * GROUP, :] = (mod[5] * masked_rows(g)).astype(HALF16)
    loads[4].wait()
    grad_inner[...] = matmul(scaled[...], w_temporal_out[...], NT).astype(HALF16)
    spread_heads(grad_inner, grad_heads, HEADS, slice(0, SPREAD))
    for trip in cot_trips:
        trip.settle()
    loads[5].wait()

    def temporal(members):
        count = len(members) * GROUP
        here, rows = slice(0, count), slice(members[0] * GROUP, members[0] * GROUP + count)
        for g in members:
            if g == 2:
                settle_odd(resid_trips[g], resid_odd_place, resid_place)
            else:
                resid_trips[g].arrive()
            normed_time[g * GROUP : (g + 1) * GROUP, :] = modulated(frames(resid_place, g), mod, 3)
        project_rows(normed_time, rows, w_temporal_qkv, packed_time, here)
        spread_heads(packed_time, heads_time, 3 * HEADS, here)

        def body(h, _):
            inner = pl.ds(pl.multiple_of(h * HEAD_DIM, 8), HEAD_DIM)
            for i, g in enumerate(members):
                part, whole_rows = slice(i * GROUP, (i + 1) * GROUP), slice(g * GROUP, (g + 1) * GROUP)
                values = heads_time[2 * HEADS + h, part]
                grad_queries, grad_keys, grad_values, soft = head_back(
                    heads_time[h, part],
                    heads_time[HEADS + h, part],
                    values,
                    grad_heads[h, whole_rows],
                    bias[...],
                )
                inner_tall[inner, whole_rows] = matmul(values, soft, TN)
                out_heads[h, part] = grad_queries
                out_heads[HEADS + h, part] = grad_keys
                out_heads[2 * HEADS + h, part] = grad_values
            return 0

        lax.fori_loop(0, HEADS, body, 0, unroll=UNROLL)
        for i in range(3 * HEADS):
            packed_grads[rows, i * HEAD_DIM : (i + 1) * HEAD_DIM] = out_heads[i, here]
        upstream_of(packed_grads, rows, w_temporal_qkv, low, count, False)
        for i, g in enumerate(members):
            total = masked_rows(g) + norm_pullback(
                frames(resid_place, g), upstream_rows(low, i * GROUP, GROUP), 1.0 + mod[4]
            )
            if g == 2:
                flat[0:GROUP, :] = total
                fold_odd(flat, 0, SPAN, pad, cot_odd)
            else:
                cot_blocks[g] = as_blocks(total)
            grad_trips[g].start()

    temporal((1, 2))
    temporal((0,))
    transposed(normed_time, SPREAD, tall)
    qkv_blocks(SPREAD, tall, packed_grads, grads_time, True)
    out_blocks(SPREAD, inner_tall, scaled, low, high, grads_time)
    one.start()

    transposed(normed, ROWS, tall)
    inner_tall[:, every] = wide(mixed[...]).T
    for g in (1, 2, 0):
        grad_trips[g].arrive()
    unfold_odd(grad_odd_place, pad, flat, 2 * GROUP, ODD)
    for g in range(2):
        flat[g * GROUP : (g + 1) * GROUP, :] = frames(grad_place, g)
    scaled[every, :] = (mod[2] * flat[...]).astype(HALF16)
    grad_inner[every, :] = matmul(scaled[every, :], w_spatial_out[...], NT).astype(HALF16)
    spread_heads(grad_inner, grad_heads, HEADS, every)
    one.first()
    one.second()
    out_blocks(ROWS, inner_tall, scaled, low, high, grads_space)

    def attend_back(h, _):
        grad_queries, grad_keys, grad_values, _ = head_back(
            heads[h], heads[HEADS + h], heads[2 * HEADS + h], grad_heads[h, every]
        )
        out_heads[h] = grad_queries
        out_heads[HEADS + h] = grad_keys
        out_heads[2 * HEADS + h] = grad_values
        return 0

    lax.fori_loop(0, HEADS, attend_back, 0, unroll=UNROLL)
    one.third()
    for i in range(3 * HEADS):
        packed_grads[every, i * HEAD_DIM : (i + 1) * HEAD_DIM] = out_heads[i]
    qkv_blocks(ROWS, tall, packed_grads, grads_space, False)
    two.start()
    upstream_of(packed_grads, every, w_spatial_qkv, low, ROWS, True)
    two.first()
    two.second()
    one.fourth()

    def last_rows(start):
        count = ROWS // 2
        rows = pl.ds(pl.multiple_of(start, count), count)
        grad = jnp.concatenate(
            [low[pl.ds(pl.multiple_of(n * SPREAD + start, 32), count), :] for n in range(3)], axis=-1
        )
        grad_tokens[rows, :] = (
            flat[rows, :] + norm_pullback(wide(tokens[rows, :]), grad, 1.0 + mod[1])
        ).astype(HALF16)

    pl.loop(0, ROWS, step=ROWS // 2)(last_rows)
    one.fifth(final_time)
    one_z.start()
    two.third()
    one_z.middle()
    two.fourth()
    one_z.end()
    two.fifth(final_space)
    two_z.start()
    assemble(out_time, summed, 0)
    two_z.middle()
    two_z.end()
    assemble(out_space, summed, HALF)
    for user in resid_trips + grad_trips + [one, two, one_z, two_z]:
        user.settle()


def vmem(shape, dtype=HALF16):
    return pltpu.VMEM(shape, dtype)


def run(lengths, mod, tokens, cotangent, w_spatial_qkv, w_spatial_out, w_temporal_qkv, w_temporal_out):
    full = jnp.float32
    sent, place, odd = vmem((2, BLOCKS, SPAN, D)), vmem((GROUPS, BLOCKS, SPAN, D)), vmem((BLOCKS, SPAN, NARROW))
    scratch = [
        vmem((ROWS, D)),
        vmem((ROWS, D)),
        vmem((QKV, D)),
        vmem((INNER, D)),
        vmem((QKV, D)),
        vmem((INNER, D)),
        pltpu.SemaphoreType.DMA((6,)),
        sent,
        place,
        sent,
        place,
        sent,
        odd,
        odd,
        odd,
        odd,
        odd,
        vmem((GROUP, NARROW), full),
        vmem((ROWS, D), full),
        vmem((ROWS, QKV)),
        vmem((3 * HEADS, ROWS, HEAD_DIM)),
        vmem((HEADS, ROWS, HEAD_DIM)),
        vmem((ROWS, INNER)),
        vmem((SPREAD, D)),
        vmem((2 * GROUP, QKV)),
        vmem((3 * HEADS, 2 * GROUP, HEAD_DIM)),
        vmem((SPREAD, D)),
        vmem((SPREAD, INNER)),
        vmem((HEADS, SPREAD, HEAD_DIM)),
        vmem((3 * HEADS, ROWS, HEAD_DIM)),
        vmem((SPREAD, QKV)),
        vmem((INNER, SPREAD), full),
        vmem((D, SPREAD)),
        vmem((D, SPREAD), full),
        vmem((D, SPREAD), full),
        vmem((GROUP, GROUP), full),
        vmem((BLOCKS, 72, WIDE)),
        vmem((BLOCKS, 72, WIDE)),
        vmem((9, 72, 128)),
        vmem((9, 72, 128)),
        vmem((2, 9, 72, 128)),
        vmem((2, 9, 72, 128)),
        vmem((BLOCKS, 72, HALF)),
        vmem((BLOCKS, 72, HALF)),
    ]
    for _ in range(3 * GROUPS):
        scratch += exchange_sems()
    for _ in range(2):
        scratch += reduction_buffers() + reduction_sems()
    for _ in range(2):
        scratch += [vmem((2, NZ, 72, 128))] + depth_sems()
    return pl.pallas_call(
        kernel,
        out_shape=(
            jax.ShapeDtypeStruct((ROWS, D), HALF16),
            jax.ShapeDtypeStruct((2, 72, WIDE), HALF16),
        ),
        in_specs=[pl.BlockSpec(memory_space=pltpu.SMEM), pl.BlockSpec(memory_space=pltpu.VMEM)]
        + [pl.BlockSpec(memory_space=pl.ANY)] * 6,
        out_specs=(pl.BlockSpec(memory_space=pltpu.VMEM),) * 2,
        scratch_shapes=scratch,
        compiler_params=pltpu.CompilerParams(
            collective_id=0, has_side_effects=True, vmem_limit_bytes=VMEM_LIMIT
        ),
    )(lengths, mod, tokens, cotangent, w_spatial_qkv, w_spatial_out, w_temporal_qkv, w_temporal_out)


def unpack_grads(summed, item):
    left, right = (half[:, item * HALF : (item + 1) * HALF] for half in (summed[0], summed[1]))
    tall = right[:, QKV - HALF :]
    return (
        jnp.concatenate([left, right[:, : QKV - HALF]], axis=-1),
        jnp.concatenate([tall[:36], tall[36:]], axis=-1),
    )


def local(
    tokens,
    cotangent,
    modulation,
    lengths,
    w_spatial_qkv,
    w_spatial_out,
    w_temporal_qkv,
    w_temporal_out,
):
    grad_tokens, summed = run(
        lengths,
        modulation.reshape(6, 1, D),
        tokens.reshape(ROWS, D),
        cotangent.reshape(ROWS, D),
        w_spatial_qkv.T,
        w_spatial_out,
        w_temporal_qkv.T,
        w_temporal_out,
    )
    temporal_qkv, temporal_out = unpack_grads(summed, 0)
    spatial_qkv, spatial_out = unpack_grads(summed, 1)
    return (
        grad_tokens.reshape(tokens.shape),
        spatial_qkv,
        spatial_out,
        temporal_qkv,
        temporal_out,
    )


def solution(mesh):
    placed = (
        P("dp", "seq", None, None),
        P("dp", "seq", None, None),
        P("dp", None, None),
        P("dp"),
        P(),
        P(),
        P(),
        P(),
    )
    return jax.shard_map(
        local,
        mesh=mesh,
        in_specs=placed,
        out_specs=(
            P("dp", "seq", None, None),
            P("seq", None),
            P("seq", None),
            P("seq", None),
            P("seq", None),
        ),
        check_vma=False,
    )
```

```python
import jax
import jax.numpy as jnp
from jax import lax
from jax.experimental import pallas as pl
from jax.experimental.pallas import tpu as pltpu
from jax.sharding import PartitionSpec as P

HEADS = 8
HEAD_DIM = 72
F = 16
SIDE = 4
NZ = 8
BLOCKS = 16
WIDE = 2304
HALF = 1152
VMEM_LIMIT = 63 * 1024 * 1024


def remote(src, dst, send, recv, device):
    return pltpu.make_async_remote_copy(
        src_ref=src,
        dst_ref=dst,
        send_sem=send,
        recv_sem=recv,
        device_id=device,
        device_id_type=pl.DeviceIdType.MESH,
    )


def hail(devices):
    barrier = pltpu.get_barrier_semaphore()
    for device in devices:
        pl.semaphore_signal(barrier, inc=1, device_id=device, device_id_type=pl.DeviceIdType.MESH)


def meet(devices):
    pl.semaphore_wait(pltpu.get_barrier_semaphore(), len(devices))


class Exchange:
    def __init__(self, place, source, into, own_sem, send_sems, recv_sems):
        self.place, self.source, self.into = place, source, into
        self.own_sem, self.send_sems, self.recv_sems = own_sem, send_sems, recv_sems

    def to(self, d):
        return lax.rem(self.place.seq + d, BLOCKS)

    def copy(self, d):
        at = self.place
        return remote(
            self.source.at[self.to(d)],
            self.into.at[at.seq],
            self.send_sems.at[d],
            self.recv_sems.at[d],
            (at.dp, self.to(d)),
        )

    def own(self):
        me = self.place.seq
        return pltpu.make_async_copy(self.source.at[me], self.into.at[me], self.own_sem)

    def start(self):
        self.own().start()
        for d in range(1, BLOCKS):
            self.copy(d).start()

    def arrive(self):
        at = self.place
        for d in range(1, BLOCKS):
            origin = lax.rem(at.seq + BLOCKS - d, BLOCKS)
            remote(
                self.source.at[origin],
                self.into.at[origin],
                self.send_sems.at[d],
                self.recv_sems.at[d],
                (at.dp, origin),
            ).wait_recv()
        self.own().wait()

    def settle(self):
        for d in range(1, BLOCKS):
            self.copy(d).wait_send()


def exchange_sems():
    dma = pltpu.SemaphoreType.DMA
    return [dma, dma((BLOCKS,)), dma((BLOCKS,))]


def plus(*refs):
    total = refs[0].astype(jnp.float32)
    for ref in refs[1:]:
        total = total + ref.astype(jnp.float32)
    return total.astype(jnp.bfloat16)


CUTS = ((0, 640), (640, 512))
DMA_COUNTS = (
    (BLOCKS, 2),
    (2, 2, 2),
    (2, 2, SIDE),
    (2, SIDE),
)


class Place:
    def __init__(self):
        dp, seq = lax.axis_index("dp"), lax.axis_index("seq")
        self.dp, self.seq = dp, seq
        self.z, self.c = lax.div(dp, 2), lax.rem(dp, 2)
        self.y, self.x = lax.div(seq, SIDE), lax.rem(seq, SIDE)
        self.twin = (self.z * 2 + 1 - self.c, seq)

    def neighbour(self, axis, dirn):
        step = 1 if dirn == 0 else SIDE - 1
        if axis == 0:
            return (self.dp, self.y * SIDE + lax.rem(self.x + step, SIDE))
        return (self.dp, lax.rem(self.y + step, SIDE) * SIDE + self.x)

    def along_z(self, d):
        return (lax.rem(self.z + d, NZ) * 2 + self.c, self.seq)

    def line(self):
        return [(self.dp, lax.rem(self.seq + d, BLOCKS)) for d in range(1, BLOCKS)]

    def friends(self):
        return [self.twin] + self.line() + [self.along_z(d) for d in range(1, NZ)]


class Reduction:
    def __init__(self, place, grads, buffers, sems):
        self.place, self.grads = place, grads
        self.acc, self.near, self.far, self.last = buffers
        (
            self.core_send,
            self.core_recv,
            self.near_send,
            self.near_recv,
            self.far_send,
            self.far_recv,
            self.last_send,
            self.last_recv,
        ) = sems

    def lanes(self, part):
        return pl.ds(CUTS[part][0], CUTS[part][1])

    def lanes_of(self, part, core):
        return pl.ds(pl.multiple_of(core * HALF + CUTS[part][0], 128), CUTS[part][1])

    def block(self, part, j, d):
        at = self.place
        if part == 0:
            return j * SIDE + lax.rem(at.x + d, SIDE)
        return lax.rem(at.y + d, SIDE) * SIDE + j

    def core_copy(self, part, b):
        at = self.place
        return remote(
            self.grads.at[b, :, self.lanes_of(part, 1 - at.c)],
            self.acc.at[b, :, self.lanes(part)],
            self.core_send.at[b, part],
            self.core_recv.at[b, part],
            at.twin,
        )

    def near_copy(self, part, dirn, k, b):
        return remote(
            self.acc.at[b, :, self.lanes(part)],
            self.near.at[part, dirn, k, :, pl.ds(0, CUTS[part][1])],
            self.near_send.at[part, dirn, k],
            self.near_recv.at[part, dirn, k],
            self.place.neighbour(part, dirn),
        )

    def far_copy(self, part, dirn, j, b):
        return remote(
            self.acc.at[b, :, self.lanes(part)],
            self.far.at[part, dirn, j, :, pl.ds(0, CUTS[part][1])],
            self.far_send.at[part, dirn, j],
            self.far_recv.at[part, dirn, j],
            self.place.neighbour(part, dirn),
        )

    def last_copy(self, part, d, b):
        at = self.place
        if part == 0:
            to = (at.dp, lax.rem(at.y + d, SIDE) * SIDE + at.x)
        else:
            to = (at.dp, at.y * SIDE + lax.rem(at.x + d, SIDE))
        return remote(
            self.acc.at[b, :, self.lanes(part)],
            self.last.at[part, d, :, pl.ds(0, CUTS[part][1])],
            self.last_send.at[part, d],
            self.last_recv.at[part, d],
            to,
        )

    def gather(self, part, b, *more):
        self.core_copy(part, b).wait_recv()
        lanes = self.lanes(part)
        mine = self.grads[b, :, self.lanes_of(part, self.place.c)]
        self.acc[b, :, lanes] = plus(mine, self.acc[b, :, lanes], *more)

    def start(self):
        for d in (2, 1, 3, 0):

            @pl.loop(0, SIDE)
            def _(j):
                for part in range(2):
                    self.core_copy(part, self.block(part, j, d)).start()

    def first(self):
        for dirn in range(2):

            @pl.loop(0, 2)
            def _(k):
                for part in range(2):
                    b = self.block(part, 2 * dirn + k, 2)
                    self.gather(part, b)
                    self.near_copy(part, dirn, k, b).start()

    def second(self):
        for dirn in range(2):

            @pl.loop(0, 2)
            def _(k):
                for part in range(2):
                    j = 2 * (1 - dirn) + k
                    b = self.block(part, j, 1 + 2 * dirn)
                    self.gather(part, b)
                    self.far_copy(part, dirn, j, b).start()

    def third(self):
        for dirn in range(2):

            @pl.loop(0, 2)
            def _(k):
                for part in range(2):
                    j = 2 * dirn + k
                    b = self.block(part, j, 1 + 2 * dirn)
                    self.near_copy(part, dirn, k, b).wait_recv()
                    self.gather(part, b, self.near[part, dirn, k, :, pl.ds(0, CUTS[part][1])])
                    self.far_copy(part, dirn, j, b).start()

    def finish(self, part, d):
        at = self.place
        b = self.block(1 - part, (at.x, at.y)[part], d)
        j = lax.rem((at.y, at.x)[part] + d, SIDE)
        for dirn in range(2):
            self.far_copy(part, dirn, j, b).wait_recv()
        width = pl.ds(0, CUTS[part][1])
        self.gather(part, b, self.far[part, 0, j, :, width], self.far[part, 1, j, :, width])
        return b

    def fourth(self):
        for d in (2, 1, 3):
            for part in range(2):
                self.last_copy(part, d, self.finish(part, d)).start()

    def fifth(self, final):
        for part in range(2):
            b = self.finish(part, 0)
            total = wide(self.acc[b, :, self.lanes(part)])
            start, width = CUTS[part]
            for d in range(1, SIDE):
                self.last_copy(part, d, b).wait_recv()
                total = total + wide(self.last[part, d, :, pl.ds(0, width)])
            for n in range(0, width, 128):
                final[(start + n) // 128] = total[:, n : n + 128].astype(jnp.bfloat16)

    def settle(self):
        for part in range(2):

            @pl.loop(0, BLOCKS)
            def _(b):
                self.core_copy(part, b).wait_send()

            for dirn in range(2):

                @pl.loop(0, 2)
                def _(k):
                    self.near_copy(part, dirn, k, 0).wait_send()

                @pl.loop(0, SIDE)
                def _(j):
                    self.far_copy(part, dirn, j, 0).wait_send()

            for d in range(1, SIDE):
                self.last_copy(part, d, 0).wait_send()


def reduction_buffers():
    half = jnp.bfloat16
    return [
        pltpu.VMEM((2, 2, 2, 72, 640), half),
        pltpu.VMEM((2, 2, SIDE, 72, 640), half),
        pltpu.VMEM((2, SIDE, 72, 640), half),
    ]


def reduction_sems():
    return [pltpu.SemaphoreType.DMA(counts) for counts in DMA_COUNTS for _ in range(2)]


class Depth:
    def __init__(self, place, final, out, arrived, sems):
        self.place, self.final, self.out = place, final, out
        self.arrived = arrived
        self.up_send, self.up_recv, self.down_send, self.down_recv, self.pair_send, self.pair_recv = sems

    def spot(self, i, core):
        return self.out.at[core, TILES[i][0]]

    def device(self, z):
        return (z * 2 + self.place.c, self.place.seq)

    def up(self, i, z):
        tile, owner, slot = TILES[i]
        return remote(
            self.final.at[tile],
            self.arrived.at[slot, z],
            self.up_send.at[i],
            self.up_recv.at[i, z],
            self.device(owner),
        )

    def down(self, i, z):
        spot = self.spot(i, self.place.c)
        return remote(spot, spot, self.down_send.at[i, z], self.down_recv.at[i], self.device(z))

    def pair(self, i, core):
        spot = self.spot(i, core)
        return remote(spot, spot, self.pair_send.at[i], self.pair_recv.at[i], self.place.twin)

    def owned(self, body):
        for i, (_, owner, _) in enumerate(TILES):
            pl.when(self.place.z == owner)(lambda i=i: body(i))

    def others(self, body):
        for i, (_, owner, _) in enumerate(TILES):
            pl.when(self.place.z != owner)(lambda i=i: body(i))

    def away(self, i):
        return [z for z in range(NZ) if z != TILES[i][1]]

    def start(self):
        self.others(lambda i: self.up(i, self.place.z).start())

    def add(self, i, tile, owner, slot):
        at = self.place
        spot = self.out.at[at.c, tile]
        total = self.final[tile].astype(jnp.float32)
        for d in range(1, NZ):
            z = lax.rem(owner + d, NZ)
            remote(
                self.final.at[tile],
                self.arrived.at[slot, z],
                self.up_send.at[i],
                self.up_recv.at[i, z],
                self.device(owner),
            ).wait_recv()
            total = total + self.arrived[slot, z].astype(jnp.float32)
        spot[...] = total.astype(jnp.bfloat16)
        for d in range(1, NZ):
            z = lax.rem(owner + d, NZ)
            remote(
                spot, spot, self.down_send.at[i, z], self.down_recv.at[i], self.device(z)
            ).start()
        remote(spot, spot, self.pair_send.at[i], self.pair_recv.at[i], at.twin).start()

    def middle(self):
        z = self.place.z
        self.add(z, z, z, 0)
        pl.when(z == 0)(lambda: self.add(NZ, NZ, 0, 1))

    def end(self):
        def forward(i):
            self.down(i, self.place.z).wait_recv()
            self.pair(i, self.place.c).start()

        self.others(forward)
        for i in range(len(TILES)):
            self.pair(i, 1 - self.place.c).wait_recv()

    def settle(self):
        self.others(lambda i: self.up(i, self.place.z).wait_send())

        def left(i):
            for z in self.away(i):
                self.down(i, z).wait_send()

        self.owned(left)
        for i in range(len(TILES)):
            self.pair(i, self.place.c).wait_send()


TILES = tuple((k, k % NZ, k // NZ) for k in range(9))


def depth_sems():
    dma = pltpu.SemaphoreType.DMA
    n = len(TILES)
    return [dma((n,)), dma((n, NZ)), dma((n, NZ)), dma((n,)), dma((n,)), dma((n,))]


NORM_EPS = 1e-06
MASKED = -1e30
ROWS = 320
SPAN = 8
GROUPS = 3
GROUP = SPAN * BLOCKS
SPREAD = GROUPS * GROUP
ODD = 4
D = 1152
INNER = 576
QKV = 1728
UNROLL = 2
NARROW = 640
REST = D - NARROW
SHARP = HEAD_DIM ** (-0.5)
SHARP2 = SHARP * 1.4426950408889634
NN = (((1,), (0,)), ((), ()))
NT = (((1,), (1,)), ((), ()))
TN = (((0,), (0,)), ((), ()))
HALF16 = jnp.bfloat16


def matmul(left, right, dims=NN):
    return lax.dot_general(left, right, dims, preferred_element_type=jnp.float32)


def columns(total, width=256):
    return [(start, min(width, total - start)) for start in range(0, total, width)]


def normalise(source):
    average = jnp.mean(source, axis=-1, keepdims=True)
    centred = source - average
    variance = jnp.mean(centred * centred, axis=-1, keepdims=True)
    spread = lax.rsqrt(variance + NORM_EPS)
    return centred * spread, spread


def modulated(source, mod, first):
    unit, _ = normalise(source)
    return (unit * (1.0 + mod[first + 1]) + mod[first]).astype(HALF16)


def norm_pullback(source, upstream, gain):
    unit, spread = normalise(source)
    grad = upstream * gain
    along = jnp.mean(grad * unit, axis=-1, keepdims=True)
    return spread * (grad - jnp.mean(grad, axis=-1, keepdims=True) - unit * along)


def wide(ref_value):
    return ref_value.astype(jnp.float32)


def by_columns(total, width, body, looped):
    if not looped:
        for start, part in columns(total, width):
            body(start, part)
        return
    even = total // width * width

    @pl.loop(0, even, step=width)
    def _(start):
        body(pl.multiple_of(start, width), width)

    if even < total:
        body(even, total - even)


def project_rows(rows_ref, rows, weight_ref, out_ref, out_rows):
    def body(start, width):
        cols = pl.ds(start, width)
        out_ref[out_rows, cols] = matmul(rows_ref[rows, :], weight_ref[cols, :], NT).astype(HALF16)

    by_columns(weight_ref.shape[0], 256, body, False)


def spread_heads(wide_ref, heads_ref, count, rows):
    for i in range(count):
        heads_ref[i, rows] = wide_ref[rows, i * HEAD_DIM : (i + 1) * HEAD_DIM]


def softmax(scores, axis):
    exponent = jnp.exp2((scores - jnp.max(scores, axis=axis, keepdims=True)) * SHARP2)
    return exponent * (1.0 / jnp.sum(exponent, axis=axis, keepdims=True))


def attend_spatial(heads, mixed_heads, rows):
    def body(h, _):
        scores = matmul(heads[h, rows], heads[HEADS + h], NT)
        soft = softmax(scores, -1).astype(HALF16)
        mixed_heads[h, rows] = matmul(soft, heads[2 * HEADS + h]).astype(HALF16)
        return 0

    lax.fori_loop(0, HEADS, body, 0, unroll=UNROLL)


def head_back(queries, keys, values, upstream, bias=None):
    scores = matmul(keys, queries, NT)
    if bias is not None:
        scores = scores + bias
    soft = softmax(scores, 0)
    soft_rounded = soft.astype(HALF16)
    raw = matmul(values, upstream, NT)
    centred = raw - jnp.sum(raw * soft, axis=0, keepdims=True)
    grad_scores = (soft * centred).astype(HALF16)
    grad_values = matmul(soft_rounded, upstream).astype(HALF16)
    grad_keys = (matmul(grad_scores, queries) * SHARP).astype(HALF16)
    grad_queries = (matmul(grad_scores, keys, TN) * SHARP).astype(HALF16)
    return grad_queries, grad_keys, grad_values, soft_rounded


def qkv_blocks(depth, tall, packed_grads, grads, looped):
    deep = slice(0, depth)

    def body(start, width):
        cols = pl.ds(start, width)
        product = matmul(tall[:, deep], packed_grads[deep, cols])
        grads[:, :, cols] = product.reshape(BLOCKS, 72, width).astype(HALF16)

    by_columns(QKV, 256, body, looped)


def out_blocks(depth, inner_tall, cot, low, high, grads):
    deep = slice(0, depth)
    low[:, deep] = jnp.zeros((D, depth), jnp.float32)
    high[:, deep] = jnp.zeros((D, depth), jnp.float32)
    for s in range(BLOCKS):
        rows = inner_tall[s * 36 : (s + 1) * 36, deep]
        low[s * 72 : s * 72 + 36, deep] = rows
        high[s * 72 + 36 : (s + 1) * 72, deep] = rows
    low_rows, high_rows = low[:, deep].astype(HALF16), high[:, deep].astype(HALF16)
    for start, width in ((0, 192), (192, 192), (384, 192)):
        product = matmul(low_rows, cot[deep, start : start + width]) + matmul(
            high_rows, cot[deep, INNER + start : INNER + start + width]
        )
        grads[:, :, QKV + start : QKV + start + width] = product.reshape(BLOCKS, 72, width).astype(
            HALF16
        )


def transposed(rows_ref, count, tall_ref):
    for start, width in columns(D, 128):
        cols = slice(start, start + width)
        tall_ref[cols, 0:count] = rows_ref[0:count, cols].T


def upstream_of(packed_grads, rows, w_qkv, into, count, looped):
    def body(start, width):
        into[pl.ds(start, count), :] = matmul(packed_grads[rows, :], w_qkv[:, pl.ds(start, width)])

    by_columns(D, SPREAD, body, looped)


def upstream_rows(into, start, count):
    return jnp.concatenate(
        [into[n * SPREAD + start : n * SPREAD + start + count, :] for n in range(3)], axis=-1
    )


def fold_odd(flat, first, step, pad, blocks):
    for i in range(BLOCKS):
        rows = slice(first + i * step, first + i * step + ODD)
        pad[i * SPAN : i * SPAN + ODD, :] = flat[rows, 0:NARROW]
        pad[i * SPAN + ODD : (i + 1) * SPAN, 0:REST] = flat[rows, NARROW:D]
    blocks[...] = pad[...].reshape(BLOCKS, SPAN, NARROW).astype(HALF16)


def unfold_odd(blocks, pad, flat, first, step):
    pad[...] = wide(blocks[...]).reshape(GROUP, NARROW)
    for i in range(BLOCKS):
        rows = slice(first + i * step, first + i * step + ODD)
        flat[rows, 0:NARROW] = pad[i * SPAN : i * SPAN + ODD, :]
        flat[rows, NARROW:D] = pad[i * SPAN + ODD : (i + 1) * SPAN, 0:REST]


def assemble(tiles, summed, start):
    for core in range(2):
        for k in range(9):
            summed[core, :, start + k * 128 : start + (k + 1) * 128] = tiles[core, k]


def as_blocks(rows):
    return rows.reshape(BLOCKS, SPAN, D).astype(HALF16)


def kernel(
    lengths,
    mod,
    tokens_far,
    cot_far,
    w_spatial_qkv_far,
    w_spatial_out_far,
    w_temporal_qkv_far,
    w_temporal_out_far,
    grad_tokens,
    summed,
    tokens,
    cot,
    w_spatial_qkv,
    w_spatial_out,
    w_temporal_qkv,
    w_temporal_out,
    load_sems,
    cot_blocks,
    cot_place,
    resid_blocks,
    resid_place,
    grad_place,
    cot_odd,
    cot_odd_place,
    resid_odd,
    resid_odd_place,
    grad_odd_place,
    pad,
    flat,
    packed,
    heads,
    mixed_heads,
    mixed,
    normed_time,
    packed_time,
    heads_time,
    scaled,
    grad_inner,
    grad_heads,
    out_heads,
    packed_grads,
    inner_tall,
    tall,
    low,
    high,
    bias,
    grads_time,
    grads_space,
    final_time,
    final_space,
    out_time,
    out_space,
    acc_time,
    acc_space,
    *scratch,
):
    at = Place()
    loads = [
        pltpu.make_async_copy(far, near, load_sems.at[i])
        for i, (far, near) in enumerate(
            (
                (cot_far, cot),
                (tokens_far, tokens),
                (w_spatial_qkv_far, w_spatial_qkv),
                (w_spatial_out_far, w_spatial_out),
                (w_temporal_out_far, w_temporal_out),
                (w_temporal_qkv_far, w_temporal_qkv),
            )
        )
    ]
    for load in loads:
        load.start()
    hail(at.friends())

    taken = 0

    def take(count):
        nonlocal taken
        taken += count
        return scratch[taken - count : taken]

    def trips(source, into, odd, odd_into):
        pairs = [(source.at[g], into.at[g]) for g in range(2)] + [(odd, odd_into)]
        return [Exchange(at, left, right, *take(3)) for left, right in pairs]

    cot_trips = trips(cot_blocks, cot_place, cot_odd, cot_odd_place)
    resid_trips = trips(resid_blocks, resid_place, resid_odd, resid_odd_place)
    grad_trips = trips(cot_blocks, grad_place, cot_odd, grad_odd_place)
    one = Reduction(at, grads_time, [acc_time, *take(3)], take(8))
    two = Reduction(at, grads_space, [acc_space, *take(3)], take(8))
    one_z = Depth(at, final_time, out_time, *take(1), take(6))
    two_z = Depth(at, final_space, out_space, *take(1), take(6))

    pad[...] = jnp.zeros_like(pad)
    loads[0].wait()
    for g in range(2):
        cot_blocks[g] = as_blocks(wide(cot[g * GROUP : (g + 1) * GROUP, :]))
    flat[2 * GROUP : ROWS, :] = wide(cot[2 * GROUP : ROWS, :])
    fold_odd(flat, 2 * GROUP, ODD, pad, cot_odd)
    meet(at.friends())
    for trip in cot_trips:
        trip.start()

    every = slice(0, ROWS)
    normed = cot
    loads[1].wait()

    def norm_rows(start):
        rows = pl.ds(pl.multiple_of(start, ROWS // 2), ROWS // 2)
        normed[rows, :] = modulated(wide(tokens[rows, :]), mod, 0)

    pl.loop(0, ROWS, step=ROWS // 2)(norm_rows)
    loads[2].wait()
    project_rows(normed, every, w_spatial_qkv, packed, every)
    spread_heads(packed, heads, 3 * HEADS, every)
    loads[3].wait()

    def residual(first, last):
        rows = slice(first, last)
        attend_spatial(heads, mixed_heads, rows)
        for h in range(HEADS):
            mixed[rows, h * HEAD_DIM : (h + 1) * HEAD_DIM] = mixed_heads[h, rows]
        for start, width in columns(D):
            cols = slice(start, start + width)
            product = matmul(mixed[rows, :], w_spatial_out[:, cols])
            flat[rows, cols] = wide(tokens[rows, cols]) + mod[2][:, cols] * product

    residual(GROUP, ROWS)
    resid_blocks[1] = as_blocks(flat[GROUP : 2 * GROUP, :])
    resid_trips[1].start()
    fold_odd(flat, 2 * GROUP, ODD, pad, resid_odd)
    resid_trips[2].start()
    residual(0, GROUP)
    resid_blocks[0] = as_blocks(flat[0:GROUP, :])
    resid_trips[0].start()

    limit = lengths[0].astype(jnp.float32)

    def frame_of(index):
        return jnp.floor(index * (1.0 / SPAN))

    keys = lax.broadcasted_iota(jnp.int32, (GROUP, 1), 0).astype(jnp.float32)
    queries = lax.broadcasted_iota(jnp.int32, (1, GROUP), 1).astype(jnp.float32)
    same = (keys - SPAN * frame_of(keys)) == (queries - SPAN * frame_of(queries))
    bias[...] = jnp.where(same & (frame_of(keys) < limit), 0.0, MASKED)

    def frames(place, g):
        return wide(place[g]).reshape(GROUP, D)

    def masked_rows(g):
        return jnp.where(frame_of(keys) < limit, 1.0, 0.0) * frames(cot_place, g)

    def settle_odd(trip, odd_place, place):
        trip.arrive()
        flat[0:GROUP, :] = jnp.zeros((GROUP, D), jnp.float32)
        unfold_odd(odd_place, pad, flat, 0, SPAN)
        place[2] = as_blocks(flat[0:GROUP, :])

    for g in range(2):
        cot_trips[g].arrive()
    settle_odd(cot_trips[2], cot_odd_place, cot_place)
    for g in range(GROUPS):
        scaled[g * GROUP : (g + 1) * GROUP, :] = (mod[5] * masked_rows(g)).astype(HALF16)
    loads[4].wait()
    grad_inner[...] = matmul(scaled[...], w_temporal_out[...], NT).astype(HALF16)
    spread_heads(grad_inner, grad_heads, HEADS, slice(0, SPREAD))
    for trip in cot_trips:
        trip.settle()
    loads[5].wait()

    def temporal(members):
        count = len(members) * GROUP
        here, rows = slice(0, count), slice(members[0] * GROUP, members[0] * GROUP + count)
        for g in members:
            if g == 2:
                settle_odd(resid_trips[g], resid_odd_place, resid_place)
            else:
                resid_trips[g].arrive()
            normed_time[g * GROUP : (g + 1) * GROUP, :] = modulated(frames(resid_place, g), mod, 3)
        project_rows(normed_time, rows, w_temporal_qkv, packed_time, here)
        spread_heads(packed_time, heads_time, 3 * HEADS, here)

        def body(h, _):
            inner = pl.ds(pl.multiple_of(h * HEAD_DIM, 8), HEAD_DIM)
            for i, g in enumerate(members):
                part, whole_rows = slice(i * GROUP, (i + 1) * GROUP), slice(g * GROUP, (g + 1) * GROUP)
                values = heads_time[2 * HEADS + h, part]
                grad_queries, grad_keys, grad_values, soft = head_back(
                    heads_time[h, part],
                    heads_time[HEADS + h, part],
                    values,
                    grad_heads[h, whole_rows],
                    bias[...],
                )
                inner_tall[inner, whole_rows] = matmul(values, soft, TN)
                out_heads[h, part] = grad_queries
                out_heads[HEADS + h, part] = grad_keys
                out_heads[2 * HEADS + h, part] = grad_values
            return 0

        lax.fori_loop(0, HEADS, body, 0, unroll=UNROLL)
        for i in range(3 * HEADS):
            packed_grads[rows, i * HEAD_DIM : (i + 1) * HEAD_DIM] = out_heads[i, here]
        upstream_of(packed_grads, rows, w_temporal_qkv, low, count, False)
        for i, g in enumerate(members):
            total = masked_rows(g) + norm_pullback(
                frames(resid_place, g), upstream_rows(low, i * GROUP, GROUP), 1.0 + mod[4]
            )
            if g == 2:
                flat[0:GROUP, :] = total
                fold_odd(flat, 0, SPAN, pad, cot_odd)
            else:
                cot_blocks[g] = as_blocks(total)
            grad_trips[g].start()

    temporal((1, 2))
    temporal((0,))
    transposed(normed_time, SPREAD, tall)
    qkv_blocks(SPREAD, tall, packed_grads, grads_time, True)
    out_blocks(SPREAD, inner_tall, scaled, low, high, grads_time)
    one.start()

    transposed(normed, ROWS, tall)
    inner_tall[:, every] = wide(mixed[...]).T
    for g in (1, 2, 0):
        grad_trips[g].arrive()
    unfold_odd(grad_odd_place, pad, flat, 2 * GROUP, ODD)
    for g in range(2):
        flat[g * GROUP : (g + 1) * GROUP, :] = frames(grad_place, g)
    scaled[every, :] = (mod[2] * flat[...]).astype(HALF16)
    grad_inner[every, :] = matmul(scaled[every, :], w_spatial_out[...], NT).astype(HALF16)
    spread_heads(grad_inner, grad_heads, HEADS, every)
    one.first()
    one.second()
    out_blocks(ROWS, inner_tall, scaled, low, high, grads_space)

    def attend_back(h, _):
        grad_queries, grad_keys, grad_values, _ = head_back(
            heads[h], heads[HEADS + h], heads[2 * HEADS + h], grad_heads[h, every]
        )
        out_heads[h] = grad_queries
        out_heads[HEADS + h] = grad_keys
        out_heads[2 * HEADS + h] = grad_values
        return 0

    lax.fori_loop(0, HEADS, attend_back, 0, unroll=UNROLL)
    one.third()
    for i in range(3 * HEADS):
        packed_grads[every, i * HEAD_DIM : (i + 1) * HEAD_DIM] = out_heads[i]
    qkv_blocks(ROWS, tall, packed_grads, grads_space, False)
    two.start()
    one.fourth()
    upstream_of(packed_grads, every, w_spatial_qkv, low, ROWS, True)
    two.first()
    two.second()

    def last_rows(start):
        count = ROWS // 2
        rows = pl.ds(pl.multiple_of(start, count), count)
        grad = jnp.concatenate(
            [low[pl.ds(pl.multiple_of(n * SPREAD + start, 32), count), :] for n in range(3)], axis=-1
        )
        grad_tokens[rows, :] = (
            flat[rows, :] + norm_pullback(wide(tokens[rows, :]), grad, 1.0 + mod[1])
        ).astype(HALF16)

    pl.loop(0, ROWS, step=ROWS // 2)(last_rows)
    one.fifth(final_time)
    one_z.start()
    two.third()
    one_z.middle()
    two.fourth()
    one_z.end()
    two.fifth(final_space)
    two_z.start()
    assemble(out_time, summed, 0)
    two_z.middle()
    two_z.end()
    assemble(out_space, summed, HALF)
    for user in resid_trips + grad_trips + [one, two, one_z, two_z]:
        user.settle()


def vmem(shape, dtype=HALF16):
    return pltpu.VMEM(shape, dtype)


def run(lengths, mod, tokens, cotangent, w_spatial_qkv, w_spatial_out, w_temporal_qkv, w_temporal_out):
    full = jnp.float32
    sent, place, odd = vmem((2, BLOCKS, SPAN, D)), vmem((GROUPS, BLOCKS, SPAN, D)), vmem((BLOCKS, SPAN, NARROW))
    scratch = [
        vmem((ROWS, D)),
        vmem((ROWS, D)),
        vmem((QKV, D)),
        vmem((INNER, D)),
        vmem((QKV, D)),
        vmem((INNER, D)),
        pltpu.SemaphoreType.DMA((6,)),
        sent,
        place,
        sent,
        place,
        sent,
        odd,
        odd,
        odd,
        odd,
        odd,
        vmem((GROUP, NARROW), full),
        vmem((ROWS, D), full),
        vmem((ROWS, QKV)),
        vmem((3 * HEADS, ROWS, HEAD_DIM)),
        vmem((HEADS, ROWS, HEAD_DIM)),
        vmem((ROWS, INNER)),
        vmem((SPREAD, D)),
        vmem((2 * GROUP, QKV)),
        vmem((3 * HEADS, 2 * GROUP, HEAD_DIM)),
        vmem((SPREAD, D)),
        vmem((SPREAD, INNER)),
        vmem((HEADS, SPREAD, HEAD_DIM)),
        vmem((3 * HEADS, ROWS, HEAD_DIM)),
        vmem((SPREAD, QKV)),
        vmem((INNER, SPREAD), full),
        vmem((D, SPREAD)),
        vmem((D, SPREAD), full),
        vmem((D, SPREAD), full),
        vmem((GROUP, GROUP), full),
        vmem((BLOCKS, 72, WIDE)),
        vmem((BLOCKS, 72, WIDE)),
        vmem((9, 72, 128)),
        vmem((9, 72, 128)),
        vmem((2, 9, 72, 128)),
        vmem((2, 9, 72, 128)),
        vmem((BLOCKS, 72, HALF)),
        vmem((BLOCKS, 72, HALF)),
    ]
    for _ in range(3 * GROUPS):
        scratch += exchange_sems()
    for _ in range(2):
        scratch += reduction_buffers() + reduction_sems()
    for _ in range(2):
        scratch += [vmem((2, NZ, 72, 128))] + depth_sems()
    return pl.pallas_call(
        kernel,
        out_shape=(
            jax.ShapeDtypeStruct((ROWS, D), HALF16),
            jax.ShapeDtypeStruct((2, 72, WIDE), HALF16),
        ),
        in_specs=[pl.BlockSpec(memory_space=pltpu.SMEM), pl.BlockSpec(memory_space=pltpu.VMEM)]
        + [pl.BlockSpec(memory_space=pl.ANY)] * 6,
        out_specs=(pl.BlockSpec(memory_space=pltpu.VMEM),) * 2,
        scratch_shapes=scratch,
        compiler_params=pltpu.CompilerParams(
            collective_id=0, has_side_effects=True, vmem_limit_bytes=VMEM_LIMIT
        ),
    )(lengths, mod, tokens, cotangent, w_spatial_qkv, w_spatial_out, w_temporal_qkv, w_temporal_out)


def unpack_grads(summed, item):
    left, right = (half[:, item * HALF : (item + 1) * HALF] for half in (summed[0], summed[1]))
    tall = right[:, QKV - HALF :]
    return (
        jnp.concatenate([left, right[:, : QKV - HALF]], axis=-1),
        jnp.concatenate([tall[:36], tall[36:]], axis=-1),
    )


def local(
    tokens,
    cotangent,
    modulation,
    lengths,
    w_spatial_qkv,
    w_spatial_out,
    w_temporal_qkv,
    w_temporal_out,
):
    grad_tokens, summed = run(
        lengths,
        modulation.reshape(6, 1, D),
        tokens.reshape(ROWS, D),
        cotangent.reshape(ROWS, D),
        w_spatial_qkv.T,
        w_spatial_out,
        w_temporal_qkv.T,
        w_temporal_out,
    )
    temporal_qkv, temporal_out = unpack_grads(summed, 0)
    spatial_qkv, spatial_out = unpack_grads(summed, 1)
    return (
        grad_tokens.reshape(tokens.shape),
        spatial_qkv,
        spatial_out,
        temporal_qkv,
        temporal_out,
    )


def solution(mesh):
    placed = (
        P("dp", "seq", None, None),
        P("dp", "seq", None, None),
        P("dp", None, None),
        P("dp"),
        P(),
        P(),
        P(),
        P(),
    )
    return jax.shard_map(
        local,
        mesh=mesh,
        in_specs=placed,
        out_specs=(
            P("dp", "seq", None, None),
            P("seq", None),
            P("seq", None),
            P("seq", None),
            P("seq", None),
        ),
        check_vma=False,
    )
```
